32 devices in a mesh: ctx: 2 (over y), exp: 16 (over z, x, core).
Axes of the slice: x: 2, y: 2, z: 4, core: 2. Of those that a mesh axis runs over, the one named last changes fastest.
Arguments:
- hidden_in: bfloat16 [16, 256, 2048], P('exp', 'ctx'), may hold values from -3 to 3
- query: bfloat16 [16, 256, 4096], P('exp', 'ctx'), may hold values from -96 to 96
- keyval: bfloat16 [16, 256, 512], P('exp', 'ctx'), may hold values from -5 to 5
- out_proj: bfloat16 [4096, 2048], P('exp'), may hold values from -0.375 to 0.375
- norm_gain: bfloat16 [2048], replicated, may hold values from 0.099609375 to 1.8984375
- expert_ids: int32 [16, 256, 8], P('exp', 'ctx'), may hold values from 0 to 15, all different within a row; in each aligned block of 128 rows (0 to 127, 128 to 255, ..., all dimensions but the last counted through in order) at most 68 rows name the same one
- gate_weights: float32 [16, 256, 8], P('exp', 'ctx'), may hold values from 0.1 to 0.4
- w_gate: bfloat16 [16, 2048, 768], P('exp'), may hold values from -0.125 to 0.125
- w_up: bfloat16 [16, 2048, 768], P('exp'), may hold values from -0.125 to 0.125
- w_down: bfloat16 [16, 768, 2048], P('exp'), may hold values from -0.21875 to 0.21875
Outputs:
- layer_out: bfloat16 [16, 256, 2048], P('exp', 'ctx')
The draws below stay inside these ranges and needn't reach their ends.
Inputs may be any that keep to these rules, and one draw needn't show every extreme that they name: `expert_ids`: in each aligned block of 128 tokens (the tokens of one device) no expert is named by more than 68 tokens, a bound that some block reaches; a token names 8 different experts.
All inputs are finite; a program needn't handle non-finite values.
Results may differ from the reference program's by a relative error of at most 0.014.
Values may be sent and summed in bfloat16 or wider, within the bound.
No kernel may reach another device: no remote copies, remote signals or barrier semaphores. Data moves between devices by JAX's collectives and lax.ppermute only.
A program may use at most 128 MiB of HBM per device.

```python
import math
import jax
import jax.numpy as jnp
import numpy as np
from jax import lax

D = 2048
QH = 32
KVH = 2
HD = 128
EF = 768
TOP = 8
TOK_DEV = 128
EXPERTS = 16
LENGTH = 256
SEQS = 16
CAP = 68


def shared_keyval(key):
    key_value = jax.random.normal(key, (SEQS, LENGTH, 2 * KVH * HD), jnp.float32)
    return jnp.clip(key_value, -5.0, 5.0)


def draw_keyval(key, part):
    return shared_keyval(key).astype(jnp.bfloat16)


def draw_query(key, part):
    key = jax.random.fold_in(key, 7)
    query_key = jax.random.fold_in(key, 0)
    queries = jnp.clip(2.0 * jax.random.normal(query_key, (SEQS, LENGTH, QH * HD), jnp.float32), -12.0, 12.0)
    return queries.astype(jnp.bfloat16)


def levels(own_key, shape, shards, low, top_value):
    factor_of, own = 1.0, jax.random.fold_in(own_key, 6)
    for position, shards_of in shards:
        draws = jnp.exp(jax.random.uniform(jax.random.fold_in(own, position), (shards_of,), jnp.float32, low / len(shards), top_value / len(shards)))
        factor_of = factor_of * jnp.repeat(draws, shape[position] // shards_of).reshape([-1 if axis == position else 1 for axis in range(len(shape))])
    return factor_of


def assign_block(rng, own, number, rows, amount, top, most, skew):
    order = jax.random.permutation(rng, amount)
    heavy_load, common = load_shares(amount, rows * top, most, skew, True), load_shares(amount, rows * top, most, skew, False)
    places = jnp.arange(amount)

    def named(lengths, rotation):
        used = int((lengths > 0).sum())
        fixed = max(1, used // 4)
        shifted = fixed + (places - fixed + rotation * (used - fixed)) % max(1, amount - fixed)
        return jnp.zeros((amount,), jnp.int32).at[order[jnp.where(places < fixed, places, shifted)]].set(jnp.asarray(lengths, jnp.int32))

    lengths = jnp.where(number % 4 == 0, named(heavy_load, number // 4), named(common, number - number // 4 - 1))
    mixed = jax.random.permutation(jax.random.fold_in(own, 3), amount)
    giver, receiver = mixed[0:amount // 2 * 2:2], mixed[1:amount // 2 * 2:2]
    margin = jnp.minimum(lengths[giver] - 1, most - lengths[receiver]) // 2
    margin = jnp.where((giver == order[0]) | (receiver == order[0]) | (lengths[receiver] == 0), 0, jnp.maximum(margin, 0))
    shifted = jax.random.randint(jax.random.fold_in(own, 4), (amount // 2,), 0, 1 << 20) % (margin + 1)
    lengths = lengths.at[giver].add(-shifted).at[receiver].add(shifted)
    items = jnp.searchsorted(jnp.cumsum(lengths), jnp.arange(rows * top), side="right").astype(jnp.int32)
    grid = items.reshape(top, rows).T
    grid = grid[jax.random.permutation(jax.random.fold_in(own, 1), rows)]
    rotation = jax.random.randint(jax.random.fold_in(own, 2), (rows, 1), 0, top)
    return jnp.take_along_axis(grid, (jnp.arange(top)[None, :] + rotation) % top, axis=1)


def load_shares(number_of, total, limit, slope, full):
    loads = [(1 << 20) // math.isqrt(standing ** slope) + 1 for standing in range(1, number_of + 1)]
    largest = limit if full else min(limit, max(-(-total // number_of), total * loads[0] // sum(loads)))
    least = 1 if total - largest >= number_of - 1 else 0
    given, spare = [largest] + [least] * (number_of - 1), total - largest - least * (number_of - 1)
    while spare > 0:
        candidates = [i for i in range(1, number_of) if given[i] < largest] or [i for i in range(1, number_of) if given[i] < limit]
        mass, left = sum([loads[i] for i in candidates]), spare
        for i in candidates:
            extra = min(limit - given[i], max(1, left * loads[i] // mass), spare)
            given[i] = given[i] + extra
            spare = spare - extra
    return np.array(given)


def bell_draw(own_key, dims, scale, most, cuts=(), kind=jnp.bfloat16):
    values = scale * jax.random.normal(own_key, dims, jnp.float32)
    if cuts:
        values = values * levels(own_key, dims, cuts, -0.22, 0.18)
    return jnp.clip(values, -most, most).astype(kind)


def setup_inputs(seed: int = 0) -> dict:
    seeds = jax.random.split(jax.random.key(seed), 11)
    hidden_in = bell_draw(seeds[0], (SEQS, LENGTH, D), 0.5, 3.0, ((0, 16), (1, 2)))
    query = draw_query(jax.random.fold_in(seeds[10], 71), 0)
    keyval = draw_keyval(jax.random.fold_in(seeds[10], 71), 0)
    out_proj = bell_draw(seeds[3], (QH * HD, D), (QH * HD // 16) ** -0.5, 0.375, ((0, 16),))
    norm_gain = jnp.clip(1.0 + 0.18 * jax.random.normal(seeds[4], (D,), jnp.float32), 0.099609375, 1.8984375).astype(jnp.bfloat16)
    expert_ids_keys = jax.random.split(jax.random.fold_in(seeds[5], 1), SEQS * LENGTH // TOK_DEV)
    expert_ids_turns = jax.random.permutation(jax.random.fold_in(seeds[5], 3), SEQS * LENGTH // TOK_DEV)
    expert_ids = jax.vmap(lambda own, number: assign_block(jax.random.fold_in(seeds[5], 2), own, number, TOK_DEV, EXPERTS, TOP, CAP, 1))(expert_ids_keys, expert_ids_turns).reshape((SEQS, LENGTH, TOP))
    gate_weights = jnp.clip(0.1 + 0.3 * jax.random.uniform(seeds[6], (SEQS, LENGTH, TOP), jnp.float32) ** levels(seeds[6], (SEQS, LENGTH, TOP), ((0, 16), (1, 2)), -0.2, 0.2), 0.1, 0.4)
    w_gate = bell_draw(seeds[7], (EXPERTS, D, EF), D ** -0.5, 0.125, ((0, 16),))
    w_up = bell_draw(seeds[8], (EXPERTS, D, EF), D ** -0.5, 0.125, ((0, 16),))
    w_down = bell_draw(seeds[9], (EXPERTS, EF, D), EF ** -0.5, 0.21875, ((0, 16),))
    return {"hidden_in": hidden_in, "query": query, "keyval": keyval, "out_proj": out_proj, "norm_gain": norm_gain, "expert_ids": expert_ids, "gate_weights": gate_weights, "w_gate": w_gate, "w_up": w_up, "w_down": w_down}


def sequence_attention(query_seq, key_value):
    length = query_seq.shape[0]
    group_size = QH // KVH
    queries = query_seq.astype(jnp.float32).reshape(length, KVH, group_size, HD)
    key_rows = key_value[:, :KVH * HD].astype(jnp.float32).reshape(length, KVH, HD)
    values = key_value[:, KVH * HD:].astype(jnp.float32).reshape(length, KVH, HD)
    scores = jnp.einsum('qhgd,khd->hgqk', queries, key_rows, precision=lax.Precision.HIGHEST) * HD ** (-0.5)
    positions = jnp.arange(length, dtype=jnp.int32)
    visible = positions[:, None] >= positions[None, :]
    scores = jnp.where(visible, scores, -1e+30)
    row_max = lax.optimization_barrier(jnp.max(scores, axis=-1, keepdims=True))
    weights = jnp.where(visible, jnp.exp(scores - row_max), 0.0)
    row_sum = lax.optimization_barrier(jnp.sum(weights, axis=-1))
    weights_b = lax.optimization_barrier(weights.astype(jnp.bfloat16)).astype(jnp.float32)
    mixed = jnp.einsum('hgqk,khd->hgqd', weights_b, values, precision=lax.Precision.HIGHEST) / row_sum[..., None]
    return mixed.transpose(2, 0, 1, 3).reshape(length, QH * HD).astype(jnp.bfloat16)

def reference(hidden_in, query, keyval, out_proj, norm_gain, expert_ids, gate_weights, w_gate, w_up, w_down):
    attended = lax.map(lambda inputs: sequence_attention(inputs[0], inputs[1]), (query, keyval))
    tokens = SEQS * LENGTH
    flat_heads = attended.reshape(tokens, QH * HD)
    projected = jnp.dot(flat_heads, out_proj, preferred_element_type=jnp.float32)
    residual = hidden_in.reshape(tokens, D).astype(jnp.float32) + projected
    scale_inv = lax.rsqrt(lax.optimization_barrier(jnp.mean(residual * residual, axis=-1, keepdims=True)) + 1e-06)
    normed = (residual * scale_inv * norm_gain.astype(jnp.float32)).astype(jnp.bfloat16)
    blocks = tokens // TOK_DEV
    routes = expert_ids.reshape(blocks, TOK_DEV * TOP).astype(jnp.int32)
    onehot = (routes[:, :, None] == jnp.arange(EXPERTS, dtype=jnp.int32)[None, None, :]).astype(jnp.int32)
    slot_rank = lax.optimization_barrier(jnp.sum(onehot * (jnp.cumsum(onehot, axis=1) - 1), axis=2)).astype(jnp.int32)
    block_ids = jnp.broadcast_to(jnp.arange(blocks, dtype=jnp.int32)[:, None], routes.shape)
    pair_ids = jnp.broadcast_to(jnp.arange(TOK_DEV * TOP, dtype=jnp.int32)[None, :], routes.shape)
    slot_table = jnp.full((EXPERTS, blocks, CAP), -1, jnp.int32).at[routes, block_ids, slot_rank].set(pair_ids)
    gate_flat = gate_weights.reshape(tokens * TOP).astype(jnp.float32)

    def one_expert(running, inputs):
        slots, gate_mat, up_mat, down_mat = inputs
        filled = (slots >= 0).reshape(-1)
        pair_idx = jnp.where(slots >= 0, slots, 0).astype(jnp.int32)
        global_pair = (jnp.arange(blocks, dtype=jnp.int32)[:, None] * (TOK_DEV * TOP) + pair_idx).reshape(-1)
        token_idx = (global_pair // TOP).astype(jnp.int32)
        gathered = normed[token_idx]
        gate_pre = jnp.dot(gathered, gate_mat, preferred_element_type=jnp.float32)
        up_pre = jnp.dot(gathered, up_mat, preferred_element_type=jnp.float32)
        activated = (jax.nn.silu(gate_pre) * up_pre).astype(jnp.bfloat16)
        expert_out = jnp.dot(activated, down_mat, preferred_element_type=jnp.float32).astype(jnp.bfloat16)
        expert_out = lax.optimization_barrier(expert_out).astype(jnp.float32)
        weight = jnp.where(filled, gate_flat[global_pair], 0.0)
        return (running.at[token_idx].add(weight[:, None] * expert_out), None)
    expert_sum, _ = lax.scan(one_expert, jnp.zeros((tokens, D), jnp.float32), (slot_table, w_gate, w_up, w_down))
    result = (residual + expert_sum).astype(jnp.bfloat16)
    return result.reshape(SEQS, LENGTH, D)
```

```python
import jax
import jax.numpy as jnp
from jax import lax
from jax.sharding import PartitionSpec as P

D = 2048
QH = 32
KVH = 2
HD = 128
TOP = 8


def shifted(block, axis, distance):
    devices = range(lax.axis_size(axis))
    route = [(i - distance, i) for i in devices if i - distance in devices]
    return lax.ppermute(block, axis, route)


def absorb(state, queries, kv_block, source, position):
    tok_rows = queries.shape[0]
    group_size = QH // KVH

    def compute(running):
        run_max, run_sum, run_out = running
        key_rows = kv_block[:, : KVH * HD].reshape(tok_rows, KVH, HD)
        values = kv_block[:, KVH * HD :].reshape(tok_rows, KVH, HD)
        grouped = queries.reshape(tok_rows, KVH, group_size, HD)
        scores = jnp.einsum(
            "qhgd,khd->hgqk", grouped, key_rows, preferred_element_type=jnp.float32
        ) * HD ** (-0.5)
        offsets = jnp.arange(tok_rows, dtype=jnp.int32)
        visible = (position * tok_rows + offsets)[:, None] >= (source * tok_rows + offsets)[None, :]
        scores = jnp.where(visible, scores, -1e30)
        new_max = jnp.maximum(run_max, jnp.max(scores, axis=-1))
        weights = jnp.where(visible, jnp.exp(scores - new_max[..., None]), 0.0)
        rescale = jnp.exp(run_max - new_max)
        run_sum = run_sum * rescale + jnp.sum(weights, axis=-1)
        mixed = jnp.einsum(
            "hgqk,khd->hgqd",
            weights.astype(jnp.bfloat16),
            values,
            preferred_element_type=jnp.float32,
        )
        run_out = run_out * rescale[..., None] + mixed
        return (new_max, run_sum, run_out)

    return lax.cond(source > position, lambda running: running, compute, state)


def chip_groups(n):
    across = [[i for i in range(n) if i % 2 == core] for core in range(2)]
    pairs = [[2 * chip, 2 * chip + 1] for chip in range(n // 2)]
    return across, pairs


def gather_two_level(block):
    across, pairs = chip_groups(lax.axis_size("exp"))
    over_chips = lax.all_gather(block, "exp", axis_index_groups=across)
    return lax.all_gather(over_chips, "exp", axis_index_groups=pairs)


def scatter_two_level(partial):
    across, pairs = chip_groups(lax.axis_size("exp"))
    own_core = lax.psum_scatter(
        partial, "exp", scatter_dimension=0, axis_index_groups=pairs
    )
    return lax.psum_scatter(own_core, "exp", scatter_dimension=0, axis_index_groups=across)


def body(
    hidden_in, query, keyval, out_proj, norm_gain, expert_ids, gate_weights, w_gate, w_up, w_down
):
    n_ctx = lax.axis_size("ctx")
    n_exp = lax.axis_size("exp")
    n_chip = n_exp // 2
    position = lax.axis_index("ctx")
    tok_rows = hidden_in.shape[1]
    group_size = QH // KVH
    queries = query[0]
    local_kv = keyval[0]
    proj_rows = out_proj.shape[0]
    proj_all = gather_two_level(out_proj).reshape(QH * HD, D)

    local_experts = w_gate.shape[0]
    experts_all = n_exp * local_experts
    experts = jnp.arange(experts_all, dtype=jnp.int32)
    gates = jnp.sum(
        jnp.where(
            expert_ids[0][:, :, None] == experts[None, None, :], gate_weights[0][:, :, None], 0.0
        ),
        axis=1,
    )
    gates_all = lax.all_gather(gates, "exp").reshape(n_chip, 2, tok_rows, n_exp, local_experts)
    gates_own = lax.dynamic_index_in_dim(
        gates_all, lax.axis_index("exp"), axis=3, keepdims=False
    ).transpose(1, 0, 2, 3)

    state = (
        jnp.full((KVH, group_size, tok_rows), -1e30, jnp.float32),
        jnp.zeros((KVH, group_size, tok_rows), jnp.float32),
        jnp.zeros((KVH, group_size, tok_rows, HD), jnp.float32),
    )
    current = local_kv
    for pass_step in range(n_ctx):
        source = (position - pass_step) % n_ctx
        state = absorb(state, queries, current, source, position)
        if pass_step + 1 < n_ctx:
            current = shifted(current, "ctx", 1)
    run_max, run_sum, run_out = state
    attended = (
        (run_out / run_sum[..., None])
        .transpose(2, 0, 1, 3)
        .reshape(tok_rows, n_chip, 2, proj_rows)
        .transpose(0, 2, 1, 3)
        .reshape(tok_rows, QH * HD)
        .astype(jnp.bfloat16)
    )
    projected = jnp.dot(attended, proj_all, preferred_element_type=jnp.float32)
    residual = hidden_in[0].astype(jnp.float32) + projected
    scale_inv = lax.rsqrt(jnp.mean(residual * residual, axis=-1, keepdims=True) + 1e-06)
    normed = (residual * scale_inv * norm_gain.astype(jnp.float32)).astype(jnp.bfloat16)

    tokens = gather_two_level(normed).reshape(n_exp * tok_rows, D)
    gate_pre = jnp.einsum("td,xdf->xtf", tokens, w_gate, preferred_element_type=jnp.float32)
    up_pre = jnp.einsum("td,xdf->xtf", tokens, w_up, preferred_element_type=jnp.float32)
    activated = (jax.nn.silu(gate_pre) * up_pre).astype(jnp.bfloat16)
    expert_out = jnp.einsum(
        "xtf,xfd->xtd", activated, w_down, preferred_element_type=jnp.float32
    )
    weights = gates_own.reshape(n_exp * tok_rows, local_experts).T[..., None]
    partial = jnp.sum(weights * expert_out, axis=0).astype(jnp.bfloat16)
    expert_sum = scatter_two_level(partial.reshape(2, n_chip, tok_rows, D))
    result = (residual + expert_sum.astype(jnp.float32)).astype(jnp.bfloat16)
    return result[None]


def solution(mesh):
    in_specs = (
        P("exp", "ctx", None),
        P("exp", "ctx", None),
        P("exp", "ctx", None),
        P("exp", None),
        P(),
        P("exp", "ctx", None),
        P("exp", "ctx", None),
        P("exp", None, None),
        P("exp", None, None),
        P("exp", None, None),
    )
    out_specs = P("exp", "ctx", None)
    return jax.shard_map(body, mesh=mesh, in_specs=in_specs, out_specs=out_specs, check_vma=False)
```

```python
import jax
import jax.numpy as jnp
from jax import lax
from jax.sharding import PartitionSpec as P

D = 2048
QH = 32
KVH = 2
HD = 128
TOP = 8


def shifted(block, axis, distance):
    devices = range(lax.axis_size(axis))
    route = [(i - distance, i) for i in devices if i - distance in devices]
    return lax.ppermute(block, axis, route)


def absorb(state, queries, kv_block, source, position):
    tok_rows = queries.shape[0]
    group_size = QH // KVH

    def compute(running):
        run_max, run_sum, run_out = running
        key_rows = kv_block[:, : KVH * HD].reshape(tok_rows, KVH, HD)
        values = kv_block[:, KVH * HD :].reshape(tok_rows, KVH, HD)
        grouped = queries.reshape(tok_rows, KVH, group_size, HD)
        scores = jnp.einsum(
            "qhgd,khd->hgqk", grouped, key_rows, preferred_element_type=jnp.float32
        ) * HD ** (-0.5)
        offsets = jnp.arange(tok_rows, dtype=jnp.int32)
        visible = (position * tok_rows + offsets)[:, None] >= (source * tok_rows + offsets)[None, :]
        scores = jnp.where(visible, scores, -1e30)
        new_max = jnp.maximum(run_max, jnp.max(scores, axis=-1))
        weights = jnp.where(visible, jnp.exp(scores - new_max[..., None]), 0.0)
        rescale = jnp.exp(run_max - new_max)
        run_sum = run_sum * rescale + jnp.sum(weights, axis=-1)
        mixed = jnp.einsum(
            "hgqk,khd->hgqd",
            weights.astype(jnp.bfloat16),
            values,
            preferred_element_type=jnp.float32,
        )
        run_out = run_out * rescale[..., None] + mixed
        return (new_max, run_sum, run_out)

    return lax.cond(source > position, lambda running: running, compute, state)


def chip_ring(n):
    chips = n // 2
    return list(range(0, chips, 2)) + list(range(1, chips, 2))[::-1]


def chip_groups(n):
    across = [[2 * chip + core for chip in chip_ring(n)] for core in range(2)]
    pairs = [[2 * chip, 2 * chip + 1] for chip in range(n // 2)]
    return across, pairs


def gather_two_level(block):
    across, pairs = chip_groups(lax.axis_size("exp"))
    over_chips = lax.all_gather(block, "exp", axis_index_groups=across)
    return lax.all_gather(over_chips, "exp", axis_index_groups=pairs)


def scatter_two_level(partial):
    across, pairs = chip_groups(lax.axis_size("exp"))
    own_core = lax.psum_scatter(
        partial, "exp", scatter_dimension=0, axis_index_groups=pairs
    )
    return lax.psum_scatter(own_core, "exp", scatter_dimension=0, axis_index_groups=across)


def body(
    hidden_in, query, keyval, out_proj, norm_gain, expert_ids, gate_weights, w_gate, w_up, w_down
):
    n_ctx = lax.axis_size("ctx")
    n_exp = lax.axis_size("exp")
    n_chip = n_exp // 2
    position = lax.axis_index("ctx")
    tok_rows = hidden_in.shape[1]
    group_size = QH // KVH
    queries = query[0]
    local_kv = keyval[0]
    proj_rows = out_proj.shape[0]
    part = proj_rows // n_ctx
    proj_part = lax.dynamic_slice_in_dim(out_proj, position * part, part, axis=0)
    proj_all = lax.all_gather(proj_part, ("ctx", "exp"), axis=0, tiled=True)

    local_experts = w_gate.shape[0]
    experts_all = n_exp * local_experts
    experts = jnp.arange(experts_all, dtype=jnp.int32)
    gates = jnp.sum(
        jnp.where(
            expert_ids[0][:, :, None] == experts[None, None, :], gate_weights[0][:, :, None], 0.0
        ),
        axis=1,
    )
    gates_all = lax.all_gather(gates, "exp").reshape(n_chip, 2, tok_rows, n_exp, local_experts)
    gates_own = lax.dynamic_index_in_dim(
        gates_all, lax.axis_index("exp"), axis=3, keepdims=False
    ).transpose(1, 0, 2, 3)[:, jnp.array(chip_ring(n_exp))]
    queries, local_kv, gates_own = lax.optimization_barrier((queries, local_kv, gates_own))

    state = (
        jnp.full((KVH, group_size, tok_rows), -1e30, jnp.float32),
        jnp.zeros((KVH, group_size, tok_rows), jnp.float32),
        jnp.zeros((KVH, group_size, tok_rows, HD), jnp.float32),
    )
    current = local_kv
    for pass_step in range(n_ctx):
        source = (position - pass_step) % n_ctx
        state = absorb(state, queries, current, source, position)
        if pass_step + 1 < n_ctx:
            current = shifted(current, "ctx", 1)
    run_max, run_sum, run_out = state
    attended = (
        (run_out / run_sum[..., None])
        .transpose(2, 0, 1, 3)
        .reshape(tok_rows, n_exp, n_ctx, part)
        .transpose(0, 2, 1, 3)
        .reshape(tok_rows, QH * HD)
        .astype(jnp.bfloat16)
    )
    projected = jnp.dot(attended, proj_all, preferred_element_type=jnp.float32)
    residual = hidden_in[0].astype(jnp.float32) + projected
    scale_inv = lax.rsqrt(jnp.mean(residual * residual, axis=-1, keepdims=True) + 1e-06)
    normed = (residual * scale_inv * norm_gain.astype(jnp.float32)).astype(jnp.bfloat16)

    tokens = gather_two_level(normed).reshape(n_exp * tok_rows, D)
    gate_pre = jnp.einsum("td,xdf->xtf", tokens, w_gate, preferred_element_type=jnp.float32)
    up_pre = jnp.einsum("td,xdf->xtf", tokens, w_up, preferred_element_type=jnp.float32)
    activated = (jax.nn.silu(gate_pre) * up_pre).astype(jnp.bfloat16)
    expert_out = jnp.einsum(
        "xtf,xfd->xtd", activated, w_down, preferred_element_type=jnp.float32
    )
    weights = gates_own.reshape(n_exp * tok_rows, local_experts).T[..., None]
    partial = jnp.sum(weights * expert_out, axis=0).astype(jnp.bfloat16)
    expert_sum = scatter_two_level(partial.reshape(2, n_chip, tok_rows, D))
    result = (residual + expert_sum.astype(jnp.float32)).astype(jnp.bfloat16)
    return result[None]


def solution(mesh):
    in_specs = (
        P("exp", "ctx", None),
        P("exp", "ctx", None),
        P("exp", "ctx", None),
        P("exp", None),
        P(),
        P("exp", "ctx", None),
        P("exp", "ctx", None),
        P("exp", None, None),
        P("exp", None, None),
        P("exp", None, None),
    )
    out_specs = P("exp", "ctx", None)
    return jax.shard_map(body, mesh=mesh, in_specs=in_specs, out_specs=out_specs, check_vma=False)
```

```python
import functools

import jax
import jax.numpy as jnp
from jax import lax
from jax.experimental import pallas as pl
from jax.experimental.pallas import tpu as pltpu
from jax.sharding import PartitionSpec as P

D = 2048
QH = 32
KVH = 2
HD = 128
TOP = 8
LANES = 128
TERMS = 3
TILE = 256


def chip_ring(n):
    chips = n // 2
    return list(range(0, chips, 2)) + list(range(1, chips, 2))[::-1]


def device_ring(n):
    return [2 * chip + core for chip in chip_ring(n) for core in range(2)]


def rotate(block, axis, distance):
    n = lax.axis_size(axis)
    return lax.ppermute(block, axis, [(i, (i + distance) % n) for i in range(n)])


def attention_kernel(places, pos_ref, query_ref, *refs):
    *kv_refs, out_ref = refs
    n_ctx = len(kv_refs)
    position = pos_ref[0]
    rows = query_ref.shape[0]
    row = lax.broadcasted_iota(jnp.int32, (rows, rows), 0)
    col = lax.broadcasted_iota(jnp.int32, (rows, rows), 1)
    visible = [row >= col]
    for back in range(1, n_ctx):
        visible.append(jnp.full((rows, rows), position, jnp.int32) >= back)
    visible = jnp.concatenate(visible, axis=1)
    for kv_head in range(KVH):
        k_at = kv_head * HD
        v_at = (KVH + kv_head) * HD
        keys = jnp.concatenate([ref[:, k_at : k_at + HD] for ref in kv_refs], axis=0)
        values = jnp.concatenate([ref[:, v_at : v_at + HD] for ref in kv_refs], axis=0)
        for group in range(QH // KVH):
            head = kv_head * (QH // KVH) + group
            scores = lax.dot_general(
                query_ref[:, head * HD : (head + 1) * HD],
                keys,
                (((1,), (1,)), ((), ())),
                preferred_element_type=jnp.float32,
            ) * HD ** (-0.5)
            scores = jnp.where(visible, scores, -1e30)
            weights = jnp.exp(scores - jnp.max(scores, axis=1, keepdims=True))
            row_sum = jnp.sum(weights, axis=1, keepdims=True)
            mixed = jnp.dot(
                weights.astype(jnp.bfloat16), values, preferred_element_type=jnp.float32
            )
            owner, at = places[head]
            slot = lax.rem(owner - position + n_ctx, n_ctx) if out_ref.shape[0] > 1 else 0
            out_ref[slot, :, at : at + HD] = (mixed / row_sum).astype(jnp.bfloat16)


def norm_kernel(experts_all, hidden_ref, own_ref, *refs):
    *arrived_refs, gain_ref, ids_ref, gates_ref, residual_ref, tokens_ref = refs
    residual = hidden_ref[...].astype(jnp.float32) + own_ref[...]
    for ref in arrived_refs:
        residual = residual + ref[...].astype(jnp.float32)
    residual_ref[...] = residual
    mean_square = jnp.mean(residual * residual, axis=1, keepdims=True)
    normed = residual * lax.rsqrt(mean_square + 1e-06) * gain_ref[...].astype(jnp.float32)
    tokens_ref[:, :D] = normed.astype(jnp.bfloat16)
    shape = (tokens_ref.shape[0], tokens_ref.shape[1] - D)
    column = lax.broadcasted_iota(jnp.int32, shape, 1)
    expert = lax.rem(column, experts_all)
    gates = jnp.zeros(shape, jnp.float32)
    for k in range(TOP):
        gates = gates + jnp.where(ids_ref[:, k : k + 1] == expert, gates_ref[:, k : k + 1], 0.0)
    terms = jnp.zeros(shape, jnp.bfloat16)
    for term in range(TERMS):
        rounded = gates.astype(jnp.bfloat16)
        terms = jnp.where(column // experts_all == term, rounded, terms)
        gates = gates - rounded.astype(jnp.float32)
    tokens_ref[:, D:] = terms


def expert_kernel(experts_all, expert_ref, tokens_ref, gate_ref, up_ref, down_ref, out_ref):
    tokens = tokens_ref[:, :D]
    terms = tokens_ref[:, D:].astype(jnp.float32)
    column = lax.broadcasted_iota(jnp.int32, terms.shape, 1)
    mine = (lax.rem(column, experts_all) == expert_ref[0]) & (column < TERMS * experts_all)
    gates = jnp.sum(jnp.where(mine, terms, 0.0), axis=1, keepdims=True)
    gate_pre = jnp.dot(tokens, gate_ref[...], preferred_element_type=jnp.float32)
    up_pre = jnp.dot(tokens, up_ref[...], preferred_element_type=jnp.float32)
    activated = (gate_pre / (1.0 + jnp.exp(-gate_pre)) * up_pre).astype(jnp.bfloat16)
    expert_out = jnp.dot(activated, down_ref[...], preferred_element_type=jnp.float32)
    out_ref[...] = jnp.where(gates > 0.0, expert_out * gates, 0.0).astype(jnp.bfloat16)


def vmem():
    return pl.BlockSpec(memory_space=pltpu.VMEM)


def smem():
    return pl.BlockSpec(memory_space=pltpu.SMEM)


def attend(position, queries, blocks, n_exp, proj_rows):
    n_ctx = len(blocks)
    rows = queries.shape[0]
    part = proj_rows // n_ctx
    ring = device_ring(n_exp)
    whole_heads = part % HD == 0
    places = {}
    for head in range(QH):
        if whole_heads:
            device, inside = divmod(head * HD, proj_rows)
            owner, rest = divmod(inside, part)
            places[head] = (owner, ring.index(device) * part + rest)
        else:
            places[head] = (0, head * HD)
    slots = n_ctx if whole_heads else 1
    attended = pl.pallas_call(
        functools.partial(attention_kernel, places),
        out_shape=jax.ShapeDtypeStruct((slots, rows, QH * HD // slots), jnp.bfloat16),
        in_specs=[smem()] + [vmem()] * (1 + n_ctx),
        out_specs=vmem(),
        compiler_params=pltpu.CompilerParams(vmem_limit_bytes=32 * 1024 * 1024),
        name="attention",
    )(position.reshape(1), queries, *blocks)
    if whole_heads:
        return [attended[slot] for slot in range(n_ctx)]
    split = attended.reshape(rows, n_exp, n_ctx, part)[:, jnp.array(ring)]
    split = split.transpose(2, 0, 1, 3).reshape(n_ctx, rows, n_exp * part)
    return [
        lax.dynamic_index_in_dim(split, (position + slot) % n_ctx, axis=0, keepdims=False)
        for slot in range(n_ctx)
    ]


def body(
    hidden_in, query, keyval, out_proj, norm_gain, expert_ids, gate_weights, w_gate, w_up, w_down
):
    n_ctx = lax.axis_size("ctx")
    n_exp = lax.axis_size("exp")
    position = lax.axis_index("ctx")
    rows = hidden_in.shape[1]
    proj_rows = out_proj.shape[0]
    ring = [device_ring(n_exp)]

    part = proj_rows // n_ctx
    proj_part = lax.dynamic_slice_in_dim(out_proj, position * part, part, axis=0)
    proj_half = lax.all_gather(proj_part, "exp", axis=0, tiled=True, axis_index_groups=ring)

    blocks = [keyval[0]] + [rotate(keyval[0], "ctx", back) for back in range(1, n_ctx)]
    attended = attend(position, query[0], blocks, n_exp, proj_rows)
    theirs = [rotate(attended[slot], "ctx", slot) for slot in range(1, n_ctx)]
    arrived = []
    for slot in range(1, n_ctx):
        partial = jnp.dot(theirs[slot - 1], proj_half, preferred_element_type=jnp.float32)
        arrived.append(rotate(partial.astype(jnp.bfloat16), "ctx", -slot))
    own = jnp.dot(attended[0], proj_half, preferred_element_type=jnp.float32)

    local_experts = w_gate.shape[0]
    experts_all = n_exp * local_experts
    extra = -(-TERMS * experts_all // LANES) * LANES
    residual, tokens = pl.pallas_call(
        functools.partial(norm_kernel, experts_all),
        out_shape=(
            jax.ShapeDtypeStruct((rows, D), jnp.float32),
            jax.ShapeDtypeStruct((rows, D + extra), jnp.bfloat16),
        ),
        in_specs=[vmem()] * (5 + len(arrived)),
        out_specs=(vmem(), vmem()),
        compiler_params=pltpu.CompilerParams(vmem_limit_bytes=32 * 1024 * 1024),
        name="norm",
    )(hidden_in[0], own, *arrived, norm_gain.reshape(1, D), expert_ids[0], gate_weights[0])

    tokens_all = lax.all_gather(tokens, "exp", axis=0, tiled=True, axis_index_groups=ring)
    total = n_exp * rows
    ef = w_gate.shape[2]
    partial = None
    for local in range(local_experts):
        expert = lax.axis_index("exp") * local_experts + local
        weighted = pl.pallas_call(
            functools.partial(expert_kernel, experts_all),
            grid=(total // TILE,),
            out_shape=jax.ShapeDtypeStruct((total, D), jnp.bfloat16),
            in_specs=[
                smem(),
                pl.BlockSpec((TILE, D + extra), lambda i: (i, 0)),
                pl.BlockSpec((D, ef), lambda i: (0, 0), pipeline_mode=pl.Buffered(1)),
                pl.BlockSpec((D, ef), lambda i: (0, 0), pipeline_mode=pl.Buffered(1)),
                pl.BlockSpec((ef, D), lambda i: (0, 0), pipeline_mode=pl.Buffered(1)),
            ],
            out_specs=pl.BlockSpec((TILE, D), lambda i: (i, 0)),
            compiler_params=pltpu.CompilerParams(vmem_limit_bytes=48 * 1024 * 1024),
            cost_estimate=pl.CostEstimate(
                flops=6 * total * D * ef, bytes_accessed=4 * total * D + 6 * D * ef, transcendentals=0
            ),
            name="experts",
        )(expert.reshape(1), tokens_all, w_gate[local], w_up[local], w_down[local])
        partial = weighted if partial is None else partial + weighted
    expert_sum = lax.psum_scatter(
        partial, "exp", scatter_dimension=0, axis_index_groups=ring, tiled=True
    )
    result = (residual + expert_sum.astype(jnp.float32)).astype(jnp.bfloat16)
    return result[None]


def solution(mesh):
    in_specs = (
        P("exp", "ctx", None),
        P("exp", "ctx", None),
        P("exp", "ctx", None),
        P("exp", None),
        P(),
        P("exp", "ctx", None),
        P("exp", "ctx", None),
        P("exp", None, None),
        P("exp", None, None),
        P("exp", None, None),
    )
    out_specs = P("exp", "ctx", None)
    return jax.shard_map(body, mesh=mesh, in_specs=in_specs, out_specs=out_specs, check_vma=False)
```

```python
import functools

import jax
import jax.numpy as jnp
from jax import lax
from jax.experimental import pallas as pl
from jax.experimental.pallas import tpu as pltpu
from jax.sharding import PartitionSpec as P

D = 2048
QH = 32
KVH = 2
HD = 128
TOP = 8
LANES = 128
TERMS = 3
TILE = 256
PROJ_CHUNKS = 2
TOKEN_CHUNKS = 2


def chip_ring(n):
    chips = n // 2
    return list(range(0, chips, 2)) + list(range(1, chips, 2))[::-1]


def device_ring(n):
    return [2 * chip + core for chip in chip_ring(n) for core in range(2)]


def rotate(block, axis, distance):
    n = lax.axis_size(axis)
    return lax.ppermute(block, axis, [(i, (i + distance) % n) for i in range(n)])


def attention_kernel(places, pos_ref, query_ref, *refs):
    *kv_refs, out_ref = refs
    n_ctx = len(kv_refs)
    position = pos_ref[0]
    rows = query_ref.shape[0]
    row = lax.broadcasted_iota(jnp.int32, (rows, rows), 0)
    col = lax.broadcasted_iota(jnp.int32, (rows, rows), 1)
    visible = [row >= col]
    for back in range(1, n_ctx):
        visible.append(jnp.full((rows, rows), position, jnp.int32) >= back)
    visible = jnp.concatenate(visible, axis=1)
    for kv_head in range(KVH):
        k_at = kv_head * HD
        v_at = (KVH + kv_head) * HD
        keys = jnp.concatenate([ref[:, k_at : k_at + HD] for ref in kv_refs], axis=0)
        values = jnp.concatenate([ref[:, v_at : v_at + HD] for ref in kv_refs], axis=0)
        for group in range(QH // KVH):
            head = kv_head * (QH // KVH) + group
            scores = lax.dot_general(
                query_ref[:, head * HD : (head + 1) * HD],
                keys,
                (((1,), (1,)), ((), ())),
                preferred_element_type=jnp.float32,
            ) * HD ** (-0.5)
            scores = jnp.where(visible, scores, -1e30)
            weights = jnp.exp(scores - jnp.max(scores, axis=1, keepdims=True))
            row_sum = jnp.sum(weights, axis=1, keepdims=True)
            mixed = jnp.dot(
                weights.astype(jnp.bfloat16), values, preferred_element_type=jnp.float32
            )
            owner, at = places[head]
            slot = lax.rem(owner - position + n_ctx, n_ctx) if out_ref.shape[0] > 1 else 0
            out_ref[slot, :, at : at + HD] = (mixed / row_sum).astype(jnp.bfloat16)


def norm_kernel(experts_all, n_own, n_chunks, hidden_ref, *refs):
    own_refs, refs = refs[:n_own], refs[n_own:]
    arrived_refs, refs = refs[: -4 - n_chunks], refs[-4 - n_chunks :]
    gain_ref, ids_ref, gates_ref, residual_ref, *token_refs = refs
    chunks = []
    for c, own_ref in enumerate(own_refs):
        projected = own_ref[...]
        for ref in arrived_refs[c::n_own]:
            projected = projected + ref[...].astype(jnp.float32)
        chunks.append(projected)
    residual = hidden_ref[...].astype(jnp.float32) + jnp.concatenate(chunks, axis=1)
    residual_ref[...] = residual
    mean_square = jnp.mean(residual * residual, axis=1, keepdims=True)
    normed = residual * lax.rsqrt(mean_square + 1e-06) * gain_ref[...].astype(jnp.float32)
    normed = normed.astype(jnp.bfloat16)
    shape = (residual.shape[0], token_refs[0].shape[1] - D)
    column = lax.broadcasted_iota(jnp.int32, shape, 1)
    expert = lax.rem(column, experts_all)
    gates = jnp.zeros(shape, jnp.float32)
    for k in range(TOP):
        gates = gates + jnp.where(ids_ref[:, k : k + 1] == expert, gates_ref[:, k : k + 1], 0.0)
    terms = jnp.zeros(shape, jnp.float32)
    for term in range(TERMS):
        rounded = gates.astype(jnp.bfloat16).astype(jnp.float32)
        terms = jnp.where(column // experts_all == term, rounded, terms)
        gates = gates - rounded
    terms = terms.astype(jnp.bfloat16)
    rows = token_refs[0].shape[0]
    for c, ref in enumerate(token_refs):
        ref[:, :D] = normed[c * rows : (c + 1) * rows]
        ref[:, D:] = terms[c * rows : (c + 1) * rows]


def final_kernel(residual_ref, *refs):
    *sum_refs, out_ref = refs
    rows = sum_refs[0].shape[0]
    for c, ref in enumerate(sum_refs):
        at = pl.ds(c * rows, rows)
        out_ref[0, at, :] = (residual_ref[at, :] + ref[...].astype(jnp.float32)).astype(jnp.bfloat16)


def expert_kernel(experts_all, expert_ref, tokens_ref, gate_ref, up_ref, down_ref, out_ref):
    tokens = tokens_ref[:, :D]
    terms = tokens_ref[:, D:].astype(jnp.float32)
    column = lax.broadcasted_iota(jnp.int32, terms.shape, 1)
    mine = (lax.rem(column, experts_all) == expert_ref[0]) & (column < TERMS * experts_all)
    gates = jnp.sum(jnp.where(mine, terms, 0.0), axis=1, keepdims=True)
    gate_pre = jnp.dot(tokens, gate_ref[...], preferred_element_type=jnp.float32)
    up_pre = jnp.dot(tokens, up_ref[...], preferred_element_type=jnp.float32)
    activated = (gate_pre / (1.0 + jnp.exp(-gate_pre)) * up_pre).astype(jnp.bfloat16)
    expert_out = jnp.dot(activated, down_ref[...], preferred_element_type=jnp.float32)
    out_ref[...] = jnp.where(gates > 0.0, expert_out * gates, 0.0).astype(jnp.bfloat16)


def vmem():
    return pl.BlockSpec(memory_space=pltpu.VMEM)


def smem():
    return pl.BlockSpec(memory_space=pltpu.SMEM)


def attend(position, queries, blocks, n_exp, proj_rows):
    n_ctx = len(blocks)
    rows = queries.shape[0]
    part = proj_rows // n_ctx
    ring = device_ring(n_exp)
    whole_heads = part % HD == 0
    places = {}
    for head in range(QH):
        if whole_heads:
            device, inside = divmod(head * HD, proj_rows)
            owner, rest = divmod(inside, part)
            places[head] = (owner, ring.index(device) * part + rest)
        else:
            places[head] = (0, head * HD)
    slots = n_ctx if whole_heads else 1
    attended = pl.pallas_call(
        functools.partial(attention_kernel, places),
        out_shape=jax.ShapeDtypeStruct((slots, rows, QH * HD // slots), jnp.bfloat16),
        in_specs=[smem()] + [vmem()] * (1 + n_ctx),
        out_specs=vmem(),
        compiler_params=pltpu.CompilerParams(vmem_limit_bytes=32 * 1024 * 1024),
        name="attention",
    )(position.reshape(1), queries, *blocks)
    if whole_heads:
        return [attended[slot] for slot in range(n_ctx)]
    split = attended.reshape(rows, n_exp, n_ctx, part)[:, jnp.array(ring)]
    split = split.transpose(2, 0, 1, 3).reshape(n_ctx, rows, n_exp * part)
    return [
        lax.dynamic_index_in_dim(split, (position + slot) % n_ctx, axis=0, keepdims=False)
        for slot in range(n_ctx)
    ]


def run_expert(experts_all, expert, tokens, w_gate, w_up, w_down):
    total, width = tokens.shape
    ef = w_gate.shape[1]
    return pl.pallas_call(
        functools.partial(expert_kernel, experts_all),
        grid=(total // TILE,),
        out_shape=jax.ShapeDtypeStruct((total, D), jnp.bfloat16),
        in_specs=[
            smem(),
            pl.BlockSpec((TILE, width), lambda i: (i, 0)),
            pl.BlockSpec((D, ef), lambda i: (0, 0), pipeline_mode=pl.Buffered(1)),
            pl.BlockSpec((D, ef), lambda i: (0, 0), pipeline_mode=pl.Buffered(1)),
            pl.BlockSpec((ef, D), lambda i: (0, 0), pipeline_mode=pl.Buffered(1)),
        ],
        out_specs=pl.BlockSpec((TILE, D), lambda i: (i, 0)),
        compiler_params=pltpu.CompilerParams(vmem_limit_bytes=48 * 1024 * 1024),
        cost_estimate=pl.CostEstimate(
            flops=6 * total * D * ef, bytes_accessed=4 * total * D + 6 * D * ef, transcendentals=0
        ),
        name="experts",
    )(expert.reshape(1), tokens, w_gate, w_up, w_down)


def body(
    hidden_in, query, keyval, out_proj, norm_gain, expert_ids, gate_weights, w_gate, w_up, w_down
):
    n_ctx = lax.axis_size("ctx")
    n_exp = lax.axis_size("exp")
    position = lax.axis_index("ctx")
    rows = hidden_in.shape[1]
    proj_rows = out_proj.shape[0]
    ring = [device_ring(n_exp)]

    part = proj_rows // n_ctx
    proj_part = lax.dynamic_slice_in_dim(out_proj, position * part, part, axis=0)
    wide = D // PROJ_CHUNKS
    proj_half = [
        lax.all_gather(
            proj_part[:, c * wide : (c + 1) * wide],
            "exp",
            axis=0,
            tiled=True,
            axis_index_groups=ring,
        )
        for c in range(PROJ_CHUNKS)
    ]

    blocks = [keyval[0]] + [rotate(keyval[0], "ctx", back) for back in range(1, n_ctx)]
    attended = attend(position, query[0], blocks, n_exp, proj_rows)
    theirs = [rotate(attended[slot], "ctx", slot) for slot in range(1, n_ctx)]
    arrived = []
    for slot in range(1, n_ctx):
        for half in proj_half:
            partial = jnp.dot(theirs[slot - 1], half, preferred_element_type=jnp.float32)
            arrived.append(rotate(partial.astype(jnp.bfloat16), "ctx", -slot))
    own = [jnp.dot(attended[0], half, preferred_element_type=jnp.float32) for half in proj_half]

    local_experts = w_gate.shape[0]
    experts_all = n_exp * local_experts
    extra = -(-TERMS * experts_all // LANES) * LANES
    chunk_rows = rows // TOKEN_CHUNKS
    residual, *tokens = pl.pallas_call(
        functools.partial(norm_kernel, experts_all, PROJ_CHUNKS, TOKEN_CHUNKS),
        out_shape=(
            jax.ShapeDtypeStruct((rows, D), jnp.float32),
            *[jax.ShapeDtypeStruct((chunk_rows, D + extra), jnp.bfloat16)] * TOKEN_CHUNKS,
        ),
        in_specs=[vmem()] * (4 + len(own) + len(arrived)),
        out_specs=(vmem(),) * (1 + TOKEN_CHUNKS),
        compiler_params=pltpu.CompilerParams(vmem_limit_bytes=32 * 1024 * 1024),
        name="norm",
    )(hidden_in[0], *own, *arrived, norm_gain.reshape(1, D), expert_ids[0], gate_weights[0])

    gathered = [
        lax.all_gather(chunk, "exp", axis=0, tiled=True, axis_index_groups=ring) for chunk in tokens
    ]
    sums = []
    for chunk in gathered:
        partial = None
        for local in range(local_experts):
            expert = lax.axis_index("exp") * local_experts + local
            weighted = run_expert(
                experts_all, expert, chunk, w_gate[local], w_up[local], w_down[local]
            )
            partial = weighted if partial is None else partial + weighted
        sums.append(
            lax.psum_scatter(
                partial, "exp", scatter_dimension=0, axis_index_groups=ring, tiled=True
            )
        )
    return pl.pallas_call(
        final_kernel,
        out_shape=jax.ShapeDtypeStruct((1, rows, D), jnp.bfloat16),
        in_specs=[vmem()] * (1 + TOKEN_CHUNKS),
        out_specs=vmem(),
        name="final",
    )(residual, *sums)


def solution(mesh):
    in_specs = (
        P("exp", "ctx", None),
        P("exp", "ctx", None),
        P("exp", "ctx", None),
        P("exp", None),
        P(),
        P("exp", "ctx", None),
        P("exp", "ctx", None),
        P("exp", None, None),
        P("exp", None, None),
        P("exp", None, None),
    )
    out_specs = P("exp", "ctx", None)
    return jax.shard_map(body, mesh=mesh, in_specs=in_specs, out_specs=out_specs, check_vma=False)
```

```python
import functools

import jax
import jax.numpy as jnp
from jax import lax
from jax.experimental import pallas as pl
from jax.experimental.pallas import tpu as pltpu
from jax.sharding import PartitionSpec as P

D = 2048
QH = 32
KVH = 2
HD = 128
TOP = 8
LANES = 128
TERMS = 3
TILE = 512
GROUP = 256


def chip_ring(n):
    chips = n // 2
    return list(range(0, chips, 2)) + list(range(1, chips, 2))[::-1]


def device_ring(n):
    return [2 * chip + core for chip in chip_ring(n) for core in range(2)]


def rotate(block, axis, distance):
    n = lax.axis_size(axis)
    return lax.ppermute(block, axis, [(i, (i + distance) % n) for i in range(n)])


def attention_kernel(places, pos_ref, query_ref, *refs):
    *kv_refs, out_ref = refs
    n_ctx = len(kv_refs)
    position = pos_ref[0]
    rows = query_ref.shape[0]
    row = lax.broadcasted_iota(jnp.int32, (rows, rows), 0)
    col = lax.broadcasted_iota(jnp.int32, (rows, rows), 1)
    visible = [row >= col]
    for back in range(1, n_ctx):
        visible.append(jnp.full((rows, rows), position, jnp.int32) >= back)
    visible = jnp.concatenate(visible, axis=1)
    for kv_head in range(KVH):
        k_at = kv_head * HD
        v_at = (KVH + kv_head) * HD
        keys = jnp.concatenate([ref[:, k_at : k_at + HD] for ref in kv_refs], axis=0)
        values = jnp.concatenate([ref[:, v_at : v_at + HD] for ref in kv_refs], axis=0)
        for group in range(QH // KVH):
            head = kv_head * (QH // KVH) + group
            scores = lax.dot_general(
                query_ref[:, head * HD : (head + 1) * HD],
                keys,
                (((1,), (1,)), ((), ())),
                preferred_element_type=jnp.float32,
            ) * HD ** (-0.5)
            scores = jnp.where(visible, scores, -1e30)
            weights = jnp.exp(scores - jnp.max(scores, axis=1, keepdims=True))
            row_sum = jnp.sum(weights, axis=1, keepdims=True)
            mixed = jnp.dot(
                weights.astype(jnp.bfloat16), values, preferred_element_type=jnp.float32
            )
            at = places[head]
            out_ref[:, at : at + HD] = (mixed / row_sum).astype(jnp.bfloat16)


def norm_kernel(experts_all, pos_ref, hidden_ref, *refs):
    *projected_refs, gain_ref, ids_ref, gates_ref, residual_ref, tokens_ref = refs
    n_ctx = len(projected_refs)
    wide = D // n_ctx
    square_sum = None
    for back, ref in enumerate(projected_refs):
        at = pl.ds(pl.multiple_of(lax.rem(pos_ref[0] + back, n_ctx) * wide, wide), wide)
        part = hidden_ref[:, at].astype(jnp.float32) + ref[...].astype(jnp.float32)
        residual_ref[:, at] = part
        squares = jnp.sum(part * part, axis=1, keepdims=True)
        square_sum = squares if square_sum is None else square_sum + squares
    scale_inv = lax.rsqrt(square_sum * (1.0 / D) + 1e-06)
    normed = residual_ref[...] * scale_inv * gain_ref[...].astype(jnp.float32)
    tokens_ref[:, :D] = normed.astype(jnp.bfloat16)
    shape = (tokens_ref.shape[0], tokens_ref.shape[1] - D)
    column = lax.broadcasted_iota(jnp.int32, shape, 1)
    expert = lax.rem(column, experts_all)
    gates = jnp.zeros(shape, jnp.float32)
    for k in range(TOP):
        gates = gates + jnp.where(ids_ref[:, k : k + 1] == expert, gates_ref[:, k : k + 1], 0.0)
    terms = jnp.zeros(shape, jnp.float32)
    for term in range(TERMS):
        rounded = gates.astype(jnp.bfloat16).astype(jnp.float32)
        terms = jnp.where(column // experts_all == term, rounded, terms)
        gates = gates - rounded
    tokens_ref[:, D:] = terms.astype(jnp.bfloat16)


def expert_kernel(
    experts_all, slots, expert_ref, tokens_ref, gate_ref, up_ref, down_ref, out_ref, picked_ref
):
    groups = tokens_ref.shape[0] // GROUP
    row = lax.broadcasted_iota(jnp.int32, (GROUP, GROUP), 0)
    col = lax.broadcasted_iota(jnp.int32, (GROUP, GROUP), 1)
    up_to = (row >= col).astype(jnp.bfloat16)
    slot_row = lax.broadcasted_iota(jnp.int32, (slots, GROUP), 0).astype(jnp.float32)
    slot_col = lax.broadcasted_iota(jnp.int32, (GROUP, slots), 1).astype(jnp.float32)
    weights, places = [], []
    for g in range(groups):
        at = pl.ds(g * GROUP, GROUP)
        terms = tokens_ref[at, D:].astype(jnp.float32)
        column = lax.broadcasted_iota(jnp.int32, terms.shape, 1)
        mine = (lax.rem(column, experts_all) == expert_ref[0]) & (column < TERMS * experts_all)
        gates = jnp.sum(jnp.where(mine, terms, 0.0), axis=1, keepdims=True)
        named = jnp.broadcast_to(gates > 0.0, (GROUP, LANES))
        rank = jnp.dot(
            up_to, named.astype(jnp.bfloat16), preferred_element_type=jnp.float32
        )
        place = jnp.where(named, rank - 1.0, -1.0)
        pick = (slot_row == jnp.transpose(place)[:1]).astype(jnp.bfloat16)
        picked = jnp.dot(pick, tokens_ref[at, :D], preferred_element_type=jnp.float32)
        picked_ref[pl.ds(g * slots, slots), :] = picked.astype(jnp.bfloat16)
        weights.append(gates)
        places.append(place[:, :1])
    picked = picked_ref[...]
    gate_pre = jnp.dot(picked, gate_ref[...], preferred_element_type=jnp.float32)
    up_pre = jnp.dot(picked, up_ref[...], preferred_element_type=jnp.float32)
    activated = (gate_pre / (1.0 + jnp.exp(-gate_pre)) * up_pre).astype(jnp.bfloat16)
    picked_ref[...] = jnp.dot(
        activated, down_ref[...], preferred_element_type=jnp.float32
    ).astype(jnp.bfloat16)
    for g in range(groups):
        put = (slot_col == places[g]).astype(jnp.bfloat16)
        expert_out = jnp.dot(
            put, picked_ref[pl.ds(g * slots, slots), :], preferred_element_type=jnp.float32
        )
        out_ref[pl.ds(g * GROUP, GROUP), :] = (expert_out * weights[g]).astype(jnp.bfloat16)


def vmem():
    return pl.BlockSpec(memory_space=pltpu.VMEM)


def smem():
    return pl.BlockSpec(memory_space=pltpu.SMEM)


def attend(position, queries, blocks, n_exp, proj_rows):
    ring = device_ring(n_exp)
    places = {}
    for head in range(QH):
        device, inside = divmod(head * HD, proj_rows)
        places[head] = ring.index(device) * proj_rows + inside
    return pl.pallas_call(
        functools.partial(attention_kernel, places),
        out_shape=jax.ShapeDtypeStruct(queries.shape, jnp.bfloat16),
        in_specs=[smem()] + [vmem()] * (1 + len(blocks)),
        out_specs=vmem(),
        compiler_params=pltpu.CompilerParams(vmem_limit_bytes=16 * 1024 * 1024),
        name="attention",
    )(position.reshape(1), queries, *blocks)


def run_expert(experts_all, block_rows, expert, tokens, w_gate, w_up, w_down):
    total, width = tokens.shape
    ef = w_gate.shape[1]
    share = block_rows * TOP // experts_all
    capacity = min(block_rows, share + block_rows * TOP // (16 * experts_all))
    slots = min(GROUP, -(-(GROUP // block_rows * capacity) // 16) * 16)
    held = pl.Buffered(1)
    return pl.pallas_call(
        functools.partial(expert_kernel, experts_all, slots),
        grid=(total // TILE,),
        out_shape=jax.ShapeDtypeStruct((total, D), jnp.bfloat16),
        in_specs=[
            smem(),
            pl.BlockSpec((TILE, width), lambda i: (i, 0)),
            pl.BlockSpec((D, ef), lambda i: (0, 0), pipeline_mode=held),
            pl.BlockSpec((D, ef), lambda i: (0, 0), pipeline_mode=held),
            pl.BlockSpec((ef, D), lambda i: (0, 0), pipeline_mode=held),
        ],
        out_specs=pl.BlockSpec((TILE, D), lambda i: (i, 0)),
        scratch_shapes=[pltpu.VMEM((TILE // GROUP * slots, D), jnp.bfloat16)],
        compiler_params=pltpu.CompilerParams(vmem_limit_bytes=36 * 1024 * 1024),
        cost_estimate=pl.CostEstimate(
            flops=4 * total * D * ef, bytes_accessed=4 * total * D + 6 * D * ef, transcendentals=0
        ),
        name="experts",
    )(expert.reshape(1), tokens, w_gate, w_up, w_down)


def body(
    hidden_in, query, keyval, out_proj, norm_gain, expert_ids, gate_weights, w_gate, w_up, w_down
):
    n_ctx = lax.axis_size("ctx")
    n_exp = lax.axis_size("exp")
    position = lax.axis_index("ctx")
    rows = hidden_in.shape[1]
    proj_rows = out_proj.shape[0]
    ring = [device_ring(n_exp)]

    wide = D // n_ctx
    columns = lax.dynamic_slice_in_dim(out_proj, position * wide, wide, axis=1)
    columns = lax.all_gather(columns, "exp", axis=0, tiled=True, axis_index_groups=ring)

    blocks = [keyval[0]] + [rotate(keyval[0], "ctx", back) for back in range(1, n_ctx)]
    attended = attend(position, query[0], blocks, n_exp, proj_rows)
    others = [rotate(attended, "ctx", back) for back in range(1, n_ctx)]
    projected = []
    for back in range(1, n_ctx):
        part = jnp.dot(others[back - 1], columns, preferred_element_type=jnp.float32)
        projected.append(rotate(part.astype(jnp.bfloat16), "ctx", -back))
    projected = [jnp.dot(attended, columns, preferred_element_type=jnp.float32)] + projected

    local_experts = w_gate.shape[0]
    experts_all = n_exp * local_experts
    extra = -(-TERMS * experts_all // LANES) * LANES
    residual, tokens = pl.pallas_call(
        functools.partial(norm_kernel, experts_all),
        out_shape=(
            jax.ShapeDtypeStruct((rows, D), jnp.float32),
            jax.ShapeDtypeStruct((rows, D + extra), jnp.bfloat16),
        ),
        in_specs=[smem()] + [vmem()] * (4 + n_ctx),
        out_specs=(vmem(), vmem()),
        compiler_params=pltpu.CompilerParams(vmem_limit_bytes=16 * 1024 * 1024),
        name="norm",
    )(
        position.reshape(1),
        hidden_in[0],
        *projected,
        norm_gain.reshape(1, D),
        expert_ids[0],
        gate_weights[0],
    )

    tokens_all = lax.all_gather(tokens, "exp", axis=0, tiled=True, axis_index_groups=ring)
    partial = None
    for local in range(local_experts):
        expert = lax.axis_index("exp") * local_experts + local
        weighted = run_expert(
            experts_all, rows, expert, tokens_all, w_gate[local], w_up[local], w_down[local]
        )
        partial = weighted if partial is None else partial + weighted
    expert_sum = lax.psum_scatter(
        partial, "exp", scatter_dimension=0, axis_index_groups=ring, tiled=True
    )
    result = (residual + expert_sum.astype(jnp.float32)).astype(jnp.bfloat16)
    return result[None]


def solution(mesh):
    in_specs = (
        P("exp", "ctx", None),
        P("exp", "ctx", None),
        P("exp", "ctx", None),
        P("exp", None),
        P(),
        P("exp", "ctx", None),
        P("exp", "ctx", None),
        P("exp", None, None),
        P("exp", None, None),
        P("exp", None, None),
    )
    out_specs = P("exp", "ctx", None)
    return jax.shard_map(body, mesh=mesh, in_specs=in_specs, out_specs=out_specs, check_vma=False)
```

```python
import functools

import jax
import jax.numpy as jnp
from jax import lax
from jax.experimental import pallas as pl
from jax.experimental.pallas import tpu as pltpu
from jax.sharding import PartitionSpec as P

D = 2048
QH = 32
KVH = 2
HD = 128
TOP = 8
LANES = 128
TERMS = 3
TILE = 512
GROUP = 256
DEPTH = 1024


def chip_ring(n):
    chips = n // 2
    return list(range(0, chips, 2)) + list(range(1, chips, 2))[::-1]


def device_ring(n):
    return [2 * chip + core for chip in chip_ring(n) for core in range(2)]


def rotate(block, axis, distance):
    n = lax.axis_size(axis)
    return lax.ppermute(block, axis, [(i, (i + distance) % n) for i in range(n)])


def attention_kernel(places, pos_ref, query_ref, *refs):
    *kv_refs, out_ref = refs
    n_ctx = len(kv_refs)
    position = pos_ref[0]
    rows = query_ref.shape[0]
    row = lax.broadcasted_iota(jnp.int32, (rows, rows), 0)
    col = lax.broadcasted_iota(jnp.int32, (rows, rows), 1)
    visible = [row >= col]
    for back in range(1, n_ctx):
        visible.append(jnp.full((rows, rows), position, jnp.int32) >= back)
    visible = jnp.concatenate(visible, axis=1)
    for kv_head in range(KVH):
        k_at = kv_head * HD
        v_at = (KVH + kv_head) * HD
        keys = jnp.concatenate([ref[:, k_at : k_at + HD] for ref in kv_refs], axis=0)
        values = jnp.concatenate([ref[:, v_at : v_at + HD] for ref in kv_refs], axis=0)
        for group in range(QH // KVH):
            head = kv_head * (QH // KVH) + group
            scores = lax.dot_general(
                query_ref[:, head * HD : (head + 1) * HD],
                keys,
                (((1,), (1,)), ((), ())),
                preferred_element_type=jnp.float32,
            ) * HD ** (-0.5)
            scores = jnp.where(visible, scores, -1e30)
            weights = jnp.exp(scores - jnp.max(scores, axis=1, keepdims=True))
            row_sum = jnp.sum(weights, axis=1, keepdims=True)
            mixed = jnp.dot(
                weights.astype(jnp.bfloat16), values, preferred_element_type=jnp.float32
            )
            at = places[head]
            out_ref[:, at : at + HD] = (mixed / row_sum).astype(jnp.bfloat16)


def projection_kernel(n_blocks, *refs):
    block_refs, weight_ref = refs[:n_blocks], refs[n_blocks]
    out_refs, total_ref = refs[n_blocks + 1 : -1], refs[-1]
    step = pl.program_id(0)
    rows, deep = block_refs[0].shape[0], weight_ref.shape[0]
    at = pl.ds(pl.multiple_of(step * deep, deep), deep)
    left = jnp.concatenate([ref[:, at] for ref in block_refs], axis=0)
    part = jnp.dot(left, weight_ref[...], preferred_element_type=jnp.float32)

    @pl.when(step == 0)
    def _():
        total_ref[...] = part

    @pl.when(step > 0)
    def _():
        total_ref[...] += part

    @pl.when(step == pl.num_programs(0) - 1)
    def _():
        for b, ref in enumerate(out_refs):
            ref[...] = total_ref[b * rows : (b + 1) * rows].astype(ref.dtype)


def norm_kernel(experts_all, pos_ref, hidden_ref, *refs):
    *projected_refs, gain_ref, ids_ref, gates_ref, residual_ref, tokens_ref = refs
    n_ctx = len(projected_refs)
    wide = D // n_ctx
    square_sum = None
    for back, ref in enumerate(projected_refs):
        at = pl.ds(pl.multiple_of(lax.rem(pos_ref[0] + back, n_ctx) * wide, wide), wide)
        part = hidden_ref[:, at].astype(jnp.float32) + ref[...].astype(jnp.float32)
        residual_ref[:, at] = part
        squares = jnp.sum(part * part, axis=1, keepdims=True)
        square_sum = squares if square_sum is None else square_sum + squares
    scale_inv = lax.rsqrt(square_sum * (1.0 / D) + 1e-06)
    normed = residual_ref[...] * scale_inv * gain_ref[...].astype(jnp.float32)
    tokens_ref[:, :D] = normed.astype(jnp.bfloat16)
    shape = (tokens_ref.shape[0], tokens_ref.shape[1] - D)
    column = lax.broadcasted_iota(jnp.int32, shape, 1)
    expert = lax.rem(column, experts_all)
    gates = jnp.zeros(shape, jnp.float32)
    for k in range(TOP):
        gates = gates + jnp.where(ids_ref[:, k : k + 1] == expert, gates_ref[:, k : k + 1], 0.0)
    terms = jnp.zeros(shape, jnp.float32)
    for term in range(TERMS):
        rounded = gates.astype(jnp.bfloat16).astype(jnp.float32)
        terms = jnp.where(column // experts_all == term, rounded, terms)
        gates = gates - rounded
    tokens_ref[:, D:] = terms.astype(jnp.bfloat16)


def expert_kernel(
    experts_all,
    slots,
    expert_ref,
    tokens_ref,
    gate_hbm,
    up_hbm,
    down_hbm,
    out_ref,
    picked_ref,
    gate_ref,
    up_ref,
    down_ref,
    sems,
):
    gate_copy = pltpu.make_async_copy(gate_hbm, gate_ref, sems.at[0])
    up_copy = pltpu.make_async_copy(up_hbm, up_ref, sems.at[1])
    down_copy = pltpu.make_async_copy(down_hbm, down_ref, sems.at[2])
    first = pl.program_id(0) == 0

    @pl.when(first)
    def _():
        gate_copy.start()
        up_copy.start()
        down_copy.start()

    groups = tokens_ref.shape[0] // GROUP
    row = lax.broadcasted_iota(jnp.int32, (GROUP, GROUP), 0)
    col = lax.broadcasted_iota(jnp.int32, (GROUP, GROUP), 1)
    up_to = (row >= col).astype(jnp.bfloat16)
    slot_row = lax.broadcasted_iota(jnp.int32, (slots, GROUP), 0).astype(jnp.float32)
    slot_col = lax.broadcasted_iota(jnp.int32, (GROUP, slots), 1).astype(jnp.float32)
    weights, places = [], []
    for g in range(groups):
        at = pl.ds(g * GROUP, GROUP)
        terms = tokens_ref[at, D:].astype(jnp.float32)
        column = lax.broadcasted_iota(jnp.int32, terms.shape, 1)
        mine = (lax.rem(column, experts_all) == expert_ref[0]) & (column < TERMS * experts_all)
        gates = jnp.sum(jnp.where(mine, terms, 0.0), axis=1, keepdims=True)
        named = jnp.broadcast_to(gates > 0.0, (GROUP, LANES))
        rank = jnp.dot(
            up_to, named.astype(jnp.bfloat16), preferred_element_type=jnp.float32
        )
        place = jnp.where(named, rank - 1.0, -1.0)
        pick = (slot_row == jnp.transpose(place)[:1]).astype(jnp.bfloat16)
        picked = jnp.dot(pick, tokens_ref[at, :D], preferred_element_type=jnp.float32)
        picked_ref[pl.ds(g * slots, slots), :] = picked.astype(jnp.bfloat16)
        weights.append(gates)
        places.append(place[:, :1])
    picked = picked_ref[...]
    pl.when(first)(gate_copy.wait)
    gate_pre = jnp.dot(picked, gate_ref[...], preferred_element_type=jnp.float32)
    pl.when(first)(up_copy.wait)
    up_pre = jnp.dot(picked, up_ref[...], preferred_element_type=jnp.float32)
    activated = (gate_pre / (1.0 + jnp.exp(-gate_pre)) * up_pre).astype(jnp.bfloat16)
    pl.when(first)(down_copy.wait)
    picked_ref[...] = jnp.dot(
        activated, down_ref[...], preferred_element_type=jnp.float32
    ).astype(jnp.bfloat16)
    for g in range(groups):
        put = (slot_col == places[g]).astype(jnp.bfloat16)
        expert_out = jnp.dot(
            put, picked_ref[pl.ds(g * slots, slots), :], preferred_element_type=jnp.float32
        )
        out_ref[pl.ds(g * GROUP, GROUP), :] = (expert_out * weights[g]).astype(jnp.bfloat16)


def vmem():
    return pl.BlockSpec(memory_space=pltpu.VMEM)


def smem():
    return pl.BlockSpec(memory_space=pltpu.SMEM)


def attend(position, queries, blocks, n_exp, proj_rows):
    ring = device_ring(n_exp)
    places = {}
    for head in range(QH):
        device, inside = divmod(head * HD, proj_rows)
        places[head] = ring.index(device) * proj_rows + inside
    return pl.pallas_call(
        functools.partial(attention_kernel, places),
        out_shape=jax.ShapeDtypeStruct(queries.shape, jnp.bfloat16),
        in_specs=[smem()] + [vmem()] * (1 + len(blocks)),
        out_specs=vmem(),
        compiler_params=pltpu.CompilerParams(vmem_limit_bytes=16 * 1024 * 1024),
        name="attention",
    )(position.reshape(1), queries, *blocks)


def project(blocks, columns):
    rows, deep = blocks[0].shape
    wide = columns.shape[1]
    types = [jnp.float32] + [jnp.bfloat16] * (len(blocks) - 1)
    return pl.pallas_call(
        functools.partial(projection_kernel, len(blocks)),
        grid=(deep // DEPTH,),
        out_shape=[jax.ShapeDtypeStruct((rows, wide), kind) for kind in types],
        in_specs=[pl.BlockSpec((rows, deep), lambda i: (0, 0))] * len(blocks)
        + [pl.BlockSpec((DEPTH, wide), lambda i: (i, 0))],
        out_specs=[pl.BlockSpec((rows, wide), lambda i: (0, 0))] * len(blocks),
        scratch_shapes=[pltpu.VMEM((len(blocks) * rows, wide), jnp.float32)],
        compiler_params=pltpu.CompilerParams(vmem_limit_bytes=56 * 1024 * 1024),
        name="projection",
    )(*blocks, columns)


def run_expert(experts_all, block_rows, expert, tokens, w_gate, w_up, w_down):
    total, width = tokens.shape
    ef = w_gate.shape[1]
    share = block_rows * TOP // experts_all
    capacity = min(block_rows, share + block_rows * TOP // (16 * experts_all))
    slots = min(GROUP, -(-(GROUP // block_rows * capacity) // 16) * 16)
    return pl.pallas_call(
        functools.partial(expert_kernel, experts_all, slots),
        grid=(total // TILE,),
        out_shape=jax.ShapeDtypeStruct((total, D), jnp.bfloat16),
        in_specs=[
            smem(),
            pl.BlockSpec((TILE, width), lambda i: (i, 0)),
            pl.BlockSpec(memory_space=pl.ANY),
            pl.BlockSpec(memory_space=pl.ANY),
            pl.BlockSpec(memory_space=pl.ANY),
        ],
        out_specs=pl.BlockSpec((TILE, D), lambda i: (i, 0)),
        scratch_shapes=[
            pltpu.VMEM((TILE // GROUP * slots, D), jnp.bfloat16),
            pltpu.VMEM((D, ef), jnp.bfloat16),
            pltpu.VMEM((D, ef), jnp.bfloat16),
            pltpu.VMEM((ef, D), jnp.bfloat16),
            pltpu.SemaphoreType.DMA((3,)),
        ],
        compiler_params=pltpu.CompilerParams(vmem_limit_bytes=56 * 1024 * 1024),
        cost_estimate=pl.CostEstimate(
            flops=4 * total * D * ef, bytes_accessed=4 * total * D + 6 * D * ef, transcendentals=0
        ),
        name="experts",
    )(expert.reshape(1), tokens, w_gate, w_up, w_down)


def body(
    hidden_in, query, keyval, out_proj, norm_gain, expert_ids, gate_weights, w_gate, w_up, w_down
):
    n_ctx = lax.axis_size("ctx")
    n_exp = lax.axis_size("exp")
    position = lax.axis_index("ctx")
    rows = hidden_in.shape[1]
    proj_rows = out_proj.shape[0]
    ring = [device_ring(n_exp)]

    wide = D // n_ctx
    columns = lax.dynamic_slice_in_dim(out_proj, position * wide, wide, axis=1)
    columns = lax.all_gather(columns, "exp", axis=0, tiled=True, axis_index_groups=ring)

    blocks = [keyval[0]] + [rotate(keyval[0], "ctx", back) for back in range(1, n_ctx)]
    attended = attend(position, query[0], blocks, n_exp, proj_rows)
    others = [rotate(attended, "ctx", back) for back in range(1, n_ctx)]
    own, *parts = project([attended] + others, columns)
    projected = [own] + [rotate(part, "ctx", -1 - back) for back, part in enumerate(parts)]

    local_experts = w_gate.shape[0]
    experts_all = n_exp * local_experts
    extra = -(-TERMS * experts_all // LANES) * LANES
    residual, tokens = pl.pallas_call(
        functools.partial(norm_kernel, experts_all),
        out_shape=(
            jax.ShapeDtypeStruct((rows, D), jnp.float32),
            jax.ShapeDtypeStruct((rows, D + extra), jnp.bfloat16),
        ),
        in_specs=[smem()] + [vmem()] * (4 + n_ctx),
        out_specs=(vmem(), vmem()),
        compiler_params=pltpu.CompilerParams(vmem_limit_bytes=16 * 1024 * 1024),
        name="norm",
    )(
        position.reshape(1),
        hidden_in[0],
        *projected,
        norm_gain.reshape(1, D),
        expert_ids[0],
        gate_weights[0],
    )

    tokens_all = lax.all_gather(tokens, "exp", axis=0, tiled=True, axis_index_groups=ring)
    partial = None
    for local in range(local_experts):
        expert = lax.axis_index("exp") * local_experts + local
        weighted = run_expert(
            experts_all, rows, expert, tokens_all, w_gate[local], w_up[local], w_down[local]
        )
        partial = weighted if partial is None else partial + weighted
    expert_sum = lax.psum_scatter(
        partial, "exp", scatter_dimension=0, axis_index_groups=ring, tiled=True
    )
    result = (residual + expert_sum.astype(jnp.float32)).astype(jnp.bfloat16)
    return result[None]


def solution(mesh):
    in_specs = (
        P("exp", "ctx", None),
        P("exp", "ctx", None),
        P("exp", "ctx", None),
        P("exp", None),
        P(),
        P("exp", "ctx", None),
        P("exp", "ctx", None),
        P("exp", None, None),
        P("exp", None, None),
        P("exp", None, None),
    )
    out_specs = P("exp", "ctx", None)
    return jax.shard_map(body, mesh=mesh, in_specs=in_specs, out_specs=out_specs, check_vma=False)
```

```python
import functools

import jax
import jax.numpy as jnp
from jax import lax
from jax.experimental import pallas as pl
from jax.experimental.pallas import tpu as pltpu
from jax.sharding import PartitionSpec as P

D = 2048
QH = 32
KVH = 2
HD = 128
TOP = 8
LANES = 128
TERMS = 3
TILE = 512
GROUP = 256


def chip_ring(n):
    chips = n // 2
    return list(range(0, chips, 2)) + list(range(1, chips, 2))[::-1]


def device_ring(n):
    return [2 * chip + core for chip in chip_ring(n) for core in range(2)]


def rotate(block, axis, distance):
    n = lax.axis_size(axis)
    return lax.ppermute(block, axis, [(i, (i + distance) % n) for i in range(n)])


def attention_kernel(places, pos_ref, query_ref, *refs):
    *kv_refs, out_ref = refs
    n_ctx = len(kv_refs)
    position = pos_ref[0]
    rows = query_ref.shape[0]
    row = lax.broadcasted_iota(jnp.int32, (rows, rows), 0)
    col = lax.broadcasted_iota(jnp.int32, (rows, rows), 1)
    visible = [row >= col]
    for back in range(1, n_ctx):
        visible.append(jnp.full((rows, rows), position, jnp.int32) >= back)
    visible = jnp.concatenate(visible, axis=1)
    for kv_head in range(KVH):
        k_at = kv_head * HD
        v_at = (KVH + kv_head) * HD
        keys = jnp.concatenate([ref[:, k_at : k_at + HD] for ref in kv_refs], axis=0)
        values = jnp.concatenate([ref[:, v_at : v_at + HD] for ref in kv_refs], axis=0)
        for group in range(QH // KVH):
            head = kv_head * (QH // KVH) + group
            scores = lax.dot_general(
                query_ref[:, head * HD : (head + 1) * HD],
                keys,
                (((1,), (1,)), ((), ())),
                preferred_element_type=jnp.float32,
            ) * HD ** (-0.5)
            scores = jnp.where(visible, scores, -1e30)
            weights = jnp.exp(scores - jnp.max(scores, axis=1, keepdims=True))
            row_sum = jnp.sum(weights, axis=1, keepdims=True)
            mixed = jnp.dot(
                weights.astype(jnp.bfloat16), values, preferred_element_type=jnp.float32
            )
            at = places[head]
            out_ref[:, at : at + HD] = (mixed / row_sum).astype(jnp.bfloat16)


def norm_kernel(experts_all, pos_ref, hidden_ref, *refs):
    *projected_refs, gain_ref, ids_ref, gates_ref, residual_ref, tokens_ref = refs
    n_ctx = len(projected_refs)
    wide = D // n_ctx
    square_sum = None
    for back, ref in enumerate(projected_refs):
        at = pl.ds(pl.multiple_of(lax.rem(pos_ref[0] + back, n_ctx) * wide, wide), wide)
        part = hidden_ref[:, at].astype(jnp.float32) + ref[...].astype(jnp.float32)
        residual_ref[:, at] = part
        squares = jnp.sum(part * part, axis=1, keepdims=True)
        square_sum = squares if square_sum is None else square_sum + squares
    scale_inv = lax.rsqrt(square_sum * (1.0 / D) + 1e-06)
    normed = residual_ref[...] * scale_inv * gain_ref[...].astype(jnp.float32)
    tokens_ref[:, :D] = normed.astype(jnp.bfloat16)
    shape = (tokens_ref.shape[0], tokens_ref.shape[1] - D)
    column = lax.broadcasted_iota(jnp.int32, shape, 1)
    expert = lax.rem(column, experts_all)
    gates = jnp.zeros(shape, jnp.float32)
    for k in range(TOP):
        gates = gates + jnp.where(ids_ref[:, k : k + 1] == expert, gates_ref[:, k : k + 1], 0.0)
    terms = jnp.zeros(shape, jnp.float32)
    for term in range(TERMS):
        rounded = gates.astype(jnp.bfloat16).astype(jnp.float32)
        terms = jnp.where(column // experts_all == term, rounded, terms)
        gates = gates - rounded
    tokens_ref[:, D:] = terms.astype(jnp.bfloat16)


def stage_kernel(after_ref, *refs):
    *refs, sems = refs
    half = len(refs) // 2
    copies = [
        pltpu.make_async_copy(refs[i], refs[half + i], sems.at[i]) for i in range(half)
    ]
    for copy in copies:
        copy.start()
    for copy in copies:
        copy.wait()


def expert_kernel(
    experts_all, slots, expert_ref, tokens_hbm, gate_ref, up_ref, down_ref, out_hbm, picked_ref
):
    expert = expert_ref[0]

    def tile(tokens_ref, out_ref):
        expert_tile(
            experts_all, slots, expert, tokens_ref, gate_ref, up_ref, down_ref, out_ref, picked_ref
        )

    total, width = tokens_hbm.shape
    pltpu.emit_pipeline(
        tile,
        grid=(total // TILE,),
        in_specs=[pl.BlockSpec((TILE, width), lambda i: (i, 0))],
        out_specs=[pl.BlockSpec((TILE, D), lambda i: (i, 0))],
    )(tokens_hbm, out_hbm)


def expert_tile(
    experts_all, slots, expert, tokens_ref, gate_ref, up_ref, down_ref, out_ref, picked_ref
):
    groups = tokens_ref.shape[0] // GROUP
    row = lax.broadcasted_iota(jnp.int32, (GROUP, GROUP), 0)
    col = lax.broadcasted_iota(jnp.int32, (GROUP, GROUP), 1)
    up_to = (row >= col).astype(jnp.bfloat16)
    slot_row = lax.broadcasted_iota(jnp.int32, (slots, GROUP), 0).astype(jnp.float32)
    slot_col = lax.broadcasted_iota(jnp.int32, (GROUP, slots), 1).astype(jnp.float32)
    weights, places = [], []
    for g in range(groups):
        at = pl.ds(g * GROUP, GROUP)
        terms = tokens_ref[at, D:].astype(jnp.float32)
        column = lax.broadcasted_iota(jnp.int32, terms.shape, 1)
        mine = (lax.rem(column, experts_all) == expert) & (column < TERMS * experts_all)
        gates = jnp.sum(jnp.where(mine, terms, 0.0), axis=1, keepdims=True)
        named = jnp.broadcast_to(gates > 0.0, (GROUP, LANES))
        rank = jnp.dot(
            up_to, named.astype(jnp.bfloat16), preferred_element_type=jnp.float32
        )
        place = jnp.where(named, rank - 1.0, -1.0)
        pick = (slot_row == jnp.transpose(place)[:1]).astype(jnp.bfloat16)
        picked = jnp.dot(pick, tokens_ref[at, :D], preferred_element_type=jnp.float32)
        picked_ref[pl.ds(g * slots, slots), :] = picked.astype(jnp.bfloat16)
        weights.append(gates)
        places.append(place[:, :1])
    picked = picked_ref[...]
    gate_pre = jnp.dot(picked, gate_ref[...], preferred_element_type=jnp.float32)
    up_pre = jnp.dot(picked, up_ref[...], preferred_element_type=jnp.float32)
    activated = (gate_pre / (1.0 + jnp.exp(-gate_pre)) * up_pre).astype(jnp.bfloat16)
    picked_ref[...] = jnp.dot(
        activated, down_ref[...], preferred_element_type=jnp.float32
    ).astype(jnp.bfloat16)
    for g in range(groups):
        put = (slot_col == places[g]).astype(jnp.bfloat16)
        expert_out = jnp.dot(
            put, picked_ref[pl.ds(g * slots, slots), :], preferred_element_type=jnp.float32
        )
        out_ref[pl.ds(g * GROUP, GROUP), :] = (expert_out * weights[g]).astype(jnp.bfloat16)


def vmem():
    return pl.BlockSpec(memory_space=pltpu.VMEM)


def smem():
    return pl.BlockSpec(memory_space=pltpu.SMEM)


def attend(position, queries, blocks, n_exp, proj_rows):
    ring = device_ring(n_exp)
    places = {}
    for head in range(QH):
        device, inside = divmod(head * HD, proj_rows)
        places[head] = ring.index(device) * proj_rows + inside
    return pl.pallas_call(
        functools.partial(attention_kernel, places),
        out_shape=jax.ShapeDtypeStruct(queries.shape, jnp.bfloat16),
        in_specs=[smem()] + [vmem()] * (1 + len(blocks)),
        out_specs=vmem(),
        compiler_params=pltpu.CompilerParams(vmem_limit_bytes=16 * 1024 * 1024),
        name="attention",
    )(position.reshape(1), queries, *blocks)


def stage(after, arrays):
    return pl.pallas_call(
        stage_kernel,
        out_shape=[jax.ShapeDtypeStruct(array.shape, array.dtype) for array in arrays],
        in_specs=[pl.BlockSpec(memory_space=pl.ANY)] * (1 + len(arrays)),
        out_specs=[vmem()] * len(arrays),
        scratch_shapes=[pltpu.SemaphoreType.DMA((len(arrays),))],
        compiler_params=pltpu.CompilerParams(vmem_limit_bytes=44 * 1024 * 1024),
        cost_estimate=pl.CostEstimate(
            flops=0,
            bytes_accessed=2 * sum(array.size * array.dtype.itemsize for array in arrays),
            transcendentals=0,
        ),
        name="stage",
    )(after, *arrays)


def run_expert(experts_all, block_rows, expert, tokens, w_gate, w_up, w_down):
    total = tokens.shape[0]
    ef = w_gate.shape[1]
    share = block_rows * TOP // experts_all
    capacity = min(block_rows, share + block_rows * TOP // (16 * experts_all))
    slots = min(GROUP, -(-(GROUP // block_rows * capacity) // 16) * 16)
    return pl.pallas_call(
        functools.partial(expert_kernel, experts_all, slots),
        out_shape=jax.ShapeDtypeStruct((total, D), jnp.bfloat16),
        in_specs=[
            smem(),
            pl.BlockSpec(memory_space=pl.ANY),
            vmem(),
            vmem(),
            vmem(),
        ],
        out_specs=pl.BlockSpec(memory_space=pl.ANY),
        scratch_shapes=[pltpu.VMEM((TILE // GROUP * slots, D), jnp.bfloat16)],
        compiler_params=pltpu.CompilerParams(vmem_limit_bytes=44 * 1024 * 1024),
        cost_estimate=pl.CostEstimate(
            flops=4 * total * D * ef, bytes_accessed=4 * total * D + 6 * D * ef, transcendentals=0
        ),
        name="experts",
    )(expert.reshape(1), tokens, w_gate, w_up, w_down)


def body(
    hidden_in, query, keyval, out_proj, norm_gain, expert_ids, gate_weights, w_gate, w_up, w_down
):
    n_ctx = lax.axis_size("ctx")
    n_exp = lax.axis_size("exp")
    position = lax.axis_index("ctx")
    rows = hidden_in.shape[1]
    proj_rows = out_proj.shape[0]
    ring = [device_ring(n_exp)]

    wide = D // n_ctx
    columns = lax.dynamic_slice_in_dim(out_proj, position * wide, wide, axis=1)
    columns = lax.all_gather(columns, "exp", axis=0, tiled=True, axis_index_groups=ring)

    blocks = [keyval[0]] + [rotate(keyval[0], "ctx", back) for back in range(1, n_ctx)]
    attended = attend(position, query[0], blocks, n_exp, proj_rows)
    others = [rotate(attended, "ctx", back) for back in range(1, n_ctx)]
    projected = []
    for back in range(1, n_ctx):
        part = jnp.dot(others[back - 1], columns, preferred_element_type=jnp.float32)
        projected.append(rotate(part.astype(jnp.bfloat16), "ctx", -back))
    projected = [jnp.dot(attended, columns, preferred_element_type=jnp.float32)] + projected

    local_experts = w_gate.shape[0]
    experts_all = n_exp * local_experts
    extra = -(-TERMS * experts_all // LANES) * LANES
    residual, tokens = pl.pallas_call(
        functools.partial(norm_kernel, experts_all),
        out_shape=(
            jax.ShapeDtypeStruct((rows, D), jnp.float32),
            jax.ShapeDtypeStruct((rows, D + extra), jnp.bfloat16),
        ),
        in_specs=[smem()] + [vmem()] * (4 + n_ctx),
        out_specs=(vmem(), vmem()),
        compiler_params=pltpu.CompilerParams(vmem_limit_bytes=16 * 1024 * 1024),
        name="norm",
    )(
        position.reshape(1),
        hidden_in[0],
        *projected,
        norm_gain.reshape(1, D),
        expert_ids[0],
        gate_weights[0],
    )

    tokens_all = lax.all_gather(tokens, "exp", axis=0, tiled=True, axis_index_groups=ring)
    partial = None
    for local in range(local_experts):
        weights = stage(tokens, (w_gate[local], w_up[local], w_down[local]))
        expert = lax.axis_index("exp") * local_experts + local
        weighted = run_expert(
            experts_all, rows, expert, tokens_all, *weights
        )
        partial = weighted if partial is None else partial + weighted
    expert_sum = lax.psum_scatter(
        partial, "exp", scatter_dimension=0, axis_index_groups=ring, tiled=True
    )
    result = (residual + expert_sum.astype(jnp.float32)).astype(jnp.bfloat16)
    return result[None]


def solution(mesh):
    in_specs = (
        P("exp", "ctx", None),
        P("exp", "ctx", None),
        P("exp", "ctx", None),
        P("exp", None),
        P(),
        P("exp", "ctx", None),
        P("exp", "ctx", None),
        P("exp", None, None),
        P("exp", None, None),
        P("exp", None, None),
    )
    out_specs = P("exp", "ctx", None)
    return jax.shard_map(body, mesh=mesh, in_specs=in_specs, out_specs=out_specs, check_vma=False)
```

```python
import functools

import jax
import jax.numpy as jnp
from jax import lax
from jax.experimental import pallas as pl
from jax.experimental.pallas import tpu as pltpu
from jax.sharding import PartitionSpec as P

D = 2048
QH = 32
KVH = 2
HD = 128
TOP = 8
LANES = 128
TERMS = 3
GROUP = 256
BATCHES = 2
PIECES = 2


def chip_ring(n):
    chips = n // 2
    return list(range(0, chips, 2)) + list(range(1, chips, 2))[::-1]


def device_ring(n):
    return [2 * chip + core for chip in chip_ring(n) for core in range(2)]


def rotate(block, axis, distance):
    n = lax.axis_size(axis)
    return lax.ppermute(block, axis, [(i, (i + distance) % n) for i in range(n)])


def attention_kernel(places, pos_ref, query_ref, *refs):
    *kv_refs, out_ref = refs
    n_ctx = len(kv_refs)
    position = pos_ref[0]
    rows = query_ref.shape[0]
    row = lax.broadcasted_iota(jnp.int32, (rows, rows), 0)
    col = lax.broadcasted_iota(jnp.int32, (rows, rows), 1)
    visible = [row >= col]
    for back in range(1, n_ctx):
        visible.append(jnp.full((rows, rows), position, jnp.int32) >= back)
    visible = jnp.concatenate(visible, axis=1)
    for kv_head in range(KVH):
        k_at = kv_head * HD
        v_at = (KVH + kv_head) * HD
        keys = jnp.concatenate([ref[:, k_at : k_at + HD] for ref in kv_refs], axis=0)
        values = jnp.concatenate([ref[:, v_at : v_at + HD] for ref in kv_refs], axis=0)
        for group in range(QH // KVH):
            head = kv_head * (QH // KVH) + group
            scores = lax.dot_general(
                query_ref[:, head * HD : (head + 1) * HD],
                keys,
                (((1,), (1,)), ((), ())),
                preferred_element_type=jnp.float32,
            ) * HD ** (-0.5)
            scores = jnp.where(visible, scores, -1e30)
            weights = jnp.exp(scores - jnp.max(scores, axis=1, keepdims=True))
            row_sum = jnp.sum(weights, axis=1, keepdims=True)
            mixed = jnp.dot(
                weights.astype(jnp.bfloat16), values, preferred_element_type=jnp.float32
            )
            at = places[head]
            out_ref[:, at : at + HD] = (mixed / row_sum).astype(jnp.bfloat16)


def norm_kernel(experts_all, pos_ref, hidden_ref, *refs):
    *projected_refs, gain_ref, ids_ref, gates_ref, residual_ref, tokens_ref = refs
    n_ctx = len(projected_refs)
    wide = D // n_ctx
    square_sum = None
    for back, ref in enumerate(projected_refs):
        at = pl.ds(pl.multiple_of(lax.rem(pos_ref[0] + back, n_ctx) * wide, wide), wide)
        part = hidden_ref[:, at].astype(jnp.float32) + ref[...].astype(jnp.float32)
        residual_ref[:, at] = part
        squares = jnp.sum(part * part, axis=1, keepdims=True)
        square_sum = squares if square_sum is None else square_sum + squares
    scale_inv = lax.rsqrt(square_sum * (1.0 / D) + 1e-06)
    normed = residual_ref[...] * scale_inv * gain_ref[...].astype(jnp.float32)
    tokens_ref[:, :D] = normed.astype(jnp.bfloat16)
    shape = (tokens_ref.shape[0], tokens_ref.shape[1] - D)
    column = lax.broadcasted_iota(jnp.int32, shape, 1)
    expert = lax.rem(column, experts_all)
    gates = jnp.zeros(shape, jnp.float32)
    for k in range(TOP):
        gates = gates + jnp.where(ids_ref[:, k : k + 1] == expert, gates_ref[:, k : k + 1], 0.0)
    terms = jnp.zeros(shape, jnp.float32)
    for term in range(TERMS):
        rounded = gates.astype(jnp.bfloat16).astype(jnp.float32)
        terms = jnp.where(column // experts_all == term, rounded, terms)
        gates = gates - rounded
    tokens_ref[:, D:] = terms.astype(jnp.bfloat16)


def expert_kernel(
    experts_all,
    slots,
    expert_ref,
    tokens_hbm,
    gate_hbm,
    up_hbm,
    down_hbm,
    out_hbm,
    tokens_ref,
    gate_ref,
    up_ref,
    down_ref,
    picked_ref,
    weights_ref,
    places_ref,
    in_sems,
    weight_sems,
    out_sems,
):
    groups = tokens_ref.shape[0]
    batch = groups // BATCHES

    def tokens_in(g):
        at = pl.ds(pl.multiple_of(g * GROUP, GROUP), GROUP)
        return pltpu.make_async_copy(tokens_hbm.at[at], tokens_ref.at[g], in_sems.at[g])

    def result_out(g):
        at = pl.ds(pl.multiple_of(g * GROUP, GROUP), GROUP)
        return pltpu.make_async_copy(
            tokens_ref.at[g, :, pl.ds(0, D)], out_hbm.at[at], out_sems.at[g]
        )

    def weight_in(number, source, target):
        rows = source.shape[0] // PIECES
        return [
            pltpu.make_async_copy(
                source.at[pl.ds(i * rows, rows)],
                target.at[pl.ds(i * rows, rows)],
                weight_sems.at[number * PIECES + i],
            )
            for i in range(PIECES)
        ]

    gate_in = weight_in(0, gate_hbm, gate_ref)
    up_in = weight_in(1, up_hbm, up_ref)
    down_in = weight_in(2, down_hbm, down_ref)
    for g in range(batch):
        tokens_in(g).start()
    for copy in gate_in + up_in + down_in:
        copy.start()
    for g in range(batch, groups):
        tokens_in(g).start()

    row = lax.broadcasted_iota(jnp.int32, (GROUP, GROUP), 0)
    col = lax.broadcasted_iota(jnp.int32, (GROUP, GROUP), 1)
    up_to = (row >= col).astype(jnp.bfloat16)
    slot_row = lax.broadcasted_iota(jnp.int32, (slots, GROUP), 0).astype(jnp.float32)
    slot_col = lax.broadcasted_iota(jnp.int32, (GROUP, slots), 1).astype(jnp.float32)

    def wait_first(number, copies):
        @pl.when(number == 0)
        def _():
            for copy in copies:
                copy.wait()

    def run_batch(number, carry):
        def pick(i, carry):
            g = number * batch + i
            tokens_in(g).wait()
            terms = tokens_ref[g, :, D:].astype(jnp.float32)
            column = lax.broadcasted_iota(jnp.int32, terms.shape, 1)
            mine = lax.rem(column, experts_all) == expert_ref[0]
            mine = mine & (column < TERMS * experts_all)
            gates = jnp.sum(jnp.where(mine, terms, 0.0), axis=1, keepdims=True)
            gates = jnp.broadcast_to(gates, (GROUP, LANES))
            named = gates > 0.0
            rank = jnp.dot(up_to, named.astype(jnp.bfloat16), preferred_element_type=jnp.float32)
            place = jnp.where(named, rank - 1.0, -1.0)
            chosen = (slot_row == jnp.transpose(place)[:1]).astype(jnp.bfloat16)
            picked = jnp.dot(chosen, tokens_ref[g, :, :D], preferred_element_type=jnp.float32)
            at = pl.ds(pl.multiple_of(i * slots, slots), slots)
            picked_ref[at, :] = picked.astype(jnp.bfloat16)
            weights_ref[i] = gates
            places_ref[i] = place
            return carry

        lax.fori_loop(0, batch, pick, 0)
        wait_first(number, gate_in)
        gate_pre = jnp.dot(picked_ref[...], gate_ref[...], preferred_element_type=jnp.float32)
        wait_first(number, up_in)
        up_pre = jnp.dot(picked_ref[...], up_ref[...], preferred_element_type=jnp.float32)
        activated = (gate_pre / (1.0 + jnp.exp(-gate_pre)) * up_pre).astype(jnp.bfloat16)
        wait_first(number, down_in)
        picked_ref[...] = jnp.dot(
            activated, down_ref[...], preferred_element_type=jnp.float32
        ).astype(jnp.bfloat16)

        def put(i, carry):
            g = number * batch + i
            at = pl.ds(pl.multiple_of(i * slots, slots), slots)
            spread = (slot_col == places_ref[i][:, :1]).astype(jnp.bfloat16)
            expert_out = jnp.dot(spread, picked_ref[at, :], preferred_element_type=jnp.float32)
            tokens_ref[g, :, :D] = (expert_out * weights_ref[i][:, :1]).astype(jnp.bfloat16)
            result_out(g).start()
            return carry

        lax.fori_loop(0, batch, put, 0)
        return carry

    lax.fori_loop(0, BATCHES, run_batch, 0)
    for g in range(groups):
        result_out(g).wait()


def vmem():
    return pl.BlockSpec(memory_space=pltpu.VMEM)


def smem():
    return pl.BlockSpec(memory_space=pltpu.SMEM)


def attend(position, queries, blocks, n_exp, proj_rows):
    ring = device_ring(n_exp)
    places = {}
    for head in range(QH):
        device, inside = divmod(head * HD, proj_rows)
        places[head] = ring.index(device) * proj_rows + inside
    return pl.pallas_call(
        functools.partial(attention_kernel, places),
        out_shape=jax.ShapeDtypeStruct(queries.shape, jnp.bfloat16),
        in_specs=[smem()] + [vmem()] * (1 + len(blocks)),
        out_specs=vmem(),
        compiler_params=pltpu.CompilerParams(vmem_limit_bytes=16 * 1024 * 1024),
        name="attention",
    )(position.reshape(1), queries, *blocks)


def run_expert(experts_all, block_rows, expert, tokens, w_gate, w_up, w_down):
    total, width = tokens.shape
    ef = w_gate.shape[1]
    share = block_rows * TOP // experts_all
    capacity = min(block_rows, share + block_rows * TOP // (16 * experts_all))
    slots = min(GROUP, -(-(GROUP // block_rows * capacity) // 16) * 16)
    groups = total // GROUP
    batch = groups // BATCHES
    anywhere = pl.BlockSpec(memory_space=pl.ANY)
    return pl.pallas_call(
        functools.partial(expert_kernel, experts_all, slots),
        out_shape=jax.ShapeDtypeStruct((total, D), jnp.bfloat16),
        in_specs=[smem()] + [anywhere] * 4,
        out_specs=anywhere,
        scratch_shapes=[
            pltpu.VMEM((groups, GROUP, width), jnp.bfloat16),
            pltpu.VMEM((D, ef), jnp.bfloat16),
            pltpu.VMEM((D, ef), jnp.bfloat16),
            pltpu.VMEM((ef, D), jnp.bfloat16),
            pltpu.VMEM((batch * slots, D), jnp.bfloat16),
            pltpu.VMEM((batch, GROUP, LANES), jnp.float32),
            pltpu.VMEM((batch, GROUP, LANES), jnp.float32),
            pltpu.SemaphoreType.DMA((groups,)),
            pltpu.SemaphoreType.DMA((3 * PIECES,)),
            pltpu.SemaphoreType.DMA((groups,)),
        ],
        compiler_params=pltpu.CompilerParams(vmem_limit_bytes=56 * 1024 * 1024),
        cost_estimate=pl.CostEstimate(
            flops=4 * total * D * ef, bytes_accessed=4 * total * D + 6 * D * ef, transcendentals=0
        ),
        name="experts",
    )(expert.reshape(1), tokens, w_gate, w_up, w_down)


def body(
    hidden_in, query, keyval, out_proj, norm_gain, expert_ids, gate_weights, w_gate, w_up, w_down
):
    n_ctx = lax.axis_size("ctx")
    n_exp = lax.axis_size("exp")
    position = lax.axis_index("ctx")
    rows = hidden_in.shape[1]
    proj_rows = out_proj.shape[0]
    ring = [device_ring(n_exp)]

    wide = D // n_ctx
    columns = lax.dynamic_slice_in_dim(out_proj, position * wide, wide, axis=1)
    columns = lax.all_gather(columns, "exp", axis=0, tiled=True, axis_index_groups=ring)

    blocks = [keyval[0]] + [rotate(keyval[0], "ctx", back) for back in range(1, n_ctx)]
    attended = attend(position, query[0], blocks, n_exp, proj_rows)
    others = [rotate(attended, "ctx", back) for back in range(1, n_ctx)]
    projected = []
    for back in range(1, n_ctx):
        part = jnp.dot(others[back - 1], columns, preferred_element_type=jnp.float32)
        projected.append(rotate(part.astype(jnp.bfloat16), "ctx", -back))
    projected = [jnp.dot(attended, columns, preferred_element_type=jnp.float32)] + projected

    local_experts = w_gate.shape[0]
    experts_all = n_exp * local_experts
    extra = -(-TERMS * experts_all // LANES) * LANES
    residual, tokens = pl.pallas_call(
        functools.partial(norm_kernel, experts_all),
        out_shape=(
            jax.ShapeDtypeStruct((rows, D), jnp.float32),
            jax.ShapeDtypeStruct((rows, D + extra), jnp.bfloat16),
        ),
        in_specs=[smem()] + [vmem()] * (4 + n_ctx),
        out_specs=(vmem(), vmem()),
        compiler_params=pltpu.CompilerParams(vmem_limit_bytes=16 * 1024 * 1024),
        name="norm",
    )(
        position.reshape(1),
        hidden_in[0],
        *projected,
        norm_gain.reshape(1, D),
        expert_ids[0],
        gate_weights[0],
    )

    tokens_all = lax.all_gather(tokens, "exp", axis=0, tiled=True, axis_index_groups=ring)
    partial = None
    for local in range(local_experts):
        expert = lax.axis_index("exp") * local_experts + local
        weighted = run_expert(
            experts_all, rows, expert, tokens_all, w_gate[local], w_up[local], w_down[local]
        )
        partial = weighted if partial is None else partial + weighted
    expert_sum = lax.psum_scatter(
        partial, "exp", scatter_dimension=0, axis_index_groups=ring, tiled=True
    )
    result = (residual + expert_sum.astype(jnp.float32)).astype(jnp.bfloat16)
    return result[None]


def solution(mesh):
    in_specs = (
        P("exp", "ctx", None),
        P("exp", "ctx", None),
        P("exp", "ctx", None),
        P("exp", None),
        P(),
        P("exp", "ctx", None),
        P("exp", "ctx", None),
        P("exp", None, None),
        P("exp", None, None),
        P("exp", None, None),
    )
    out_specs = P("exp", "ctx", None)
    return jax.shard_map(body, mesh=mesh, in_specs=in_specs, out_specs=out_specs, check_vma=False)
```

```python
import functools

import jax
import jax.numpy as jnp
from jax import lax
from jax.experimental import pallas as pl
from jax.experimental.pallas import tpu as pltpu
from jax.sharding import PartitionSpec as P

D = 2048
QH = 32
KVH = 2
HD = 128
TOP = 8
LANES = 128
TERMS = 3
GROUP = 256
BATCHES = 4
PIECES = 2


def chip_ring(n):
    chips = n // 2
    return list(range(0, chips, 2)) + list(range(1, chips, 2))[::-1]


def device_ring(n):
    return [2 * chip + core for chip in chip_ring(n) for core in range(2)]


def core_rings(n):
    return [[2 * chip + core for chip in chip_ring(n)] for core in range(2)]


def swap_cores(block):
    n = lax.axis_size("exp")
    return lax.ppermute(block, "exp", [(i, i ^ 1) for i in range(n)])


def rotate(block, axis, distance):
    if distance == 0:
        return block
    n = lax.axis_size(axis)
    return lax.ppermute(block, axis, [(i, (i + distance) % n) for i in range(n)])


def columns_kernel(pos_ref, source, target, sem):
    wide = target.shape[1]
    at = pl.ds(pl.multiple_of(pos_ref[0] * wide, wide), wide)
    copy = pltpu.make_async_copy(source.at[:, at], target, sem)
    copy.start()
    copy.wait()


def attention_kernel(places, pos_ref, query_ref, *refs):
    *kv_refs, out_ref = refs
    n_ctx = len(kv_refs)
    position = pos_ref[0]
    rows = query_ref.shape[0]
    row = lax.broadcasted_iota(jnp.int32, (rows, rows), 0)
    col = lax.broadcasted_iota(jnp.int32, (rows, rows), 1)
    visible = [row >= col]
    for back in range(1, n_ctx):
        visible.append(jnp.full((rows, rows), position, jnp.int32) >= back)
    visible = jnp.concatenate(visible, axis=1)
    for kv_head in range(KVH):
        k_at = kv_head * HD
        v_at = (KVH + kv_head) * HD
        keys = jnp.concatenate([ref[:, k_at : k_at + HD] for ref in kv_refs], axis=0)
        values = jnp.concatenate([ref[:, v_at : v_at + HD] for ref in kv_refs], axis=0)
        for group in range(QH // KVH):
            head = kv_head * (QH // KVH) + group
            scores = lax.dot_general(
                query_ref[:, head * HD : (head + 1) * HD],
                keys,
                (((1,), (1,)), ((), ())),
                preferred_element_type=jnp.float32,
            ) * HD ** (-0.5)
            scores = jnp.where(visible, scores, -1e30)
            weights = jnp.exp(scores - jnp.max(scores, axis=1, keepdims=True))
            row_sum = jnp.sum(weights, axis=1, keepdims=True)
            mixed = jnp.dot(
                weights.astype(jnp.bfloat16), values, preferred_element_type=jnp.float32
            )
            core, at = places[head]
            slot = lax.rem(core + pos_ref[1], 2)
            out_ref[slot, :, at : at + HD] = (mixed / row_sum).astype(jnp.bfloat16)


def norm_kernel(experts_all, pos_ref, hidden_ref, *refs):
    *projected_refs, gain_ref, ids_ref, gates_ref, residual_ref, tokens_ref = refs
    n_ctx = len(projected_refs)
    wide = D // n_ctx
    square_sum = None
    for back, ref in enumerate(projected_refs):
        at = pl.ds(pl.multiple_of(lax.rem(pos_ref[0] + back, n_ctx) * wide, wide), wide)
        part = hidden_ref[:, at].astype(jnp.float32) + ref[...].astype(jnp.float32)
        residual_ref[:, at] = part
        squares = jnp.sum(part * part, axis=1, keepdims=True)
        square_sum = squares if square_sum is None else square_sum + squares
    scale_inv = lax.rsqrt(square_sum * (1.0 / D) + 1e-06)
    normed = residual_ref[...] * scale_inv * gain_ref[...].astype(jnp.float32)
    tokens_ref[:, :D] = normed.astype(jnp.bfloat16)
    shape = (tokens_ref.shape[0], tokens_ref.shape[1] - D)
    column = lax.broadcasted_iota(jnp.int32, shape, 1)
    expert = lax.rem(column, experts_all)
    gates = jnp.zeros(shape, jnp.float32)
    for k in range(TOP):
        gates = gates + jnp.where(ids_ref[:, k : k + 1] == expert, gates_ref[:, k : k + 1], 0.0)
    terms = jnp.zeros(shape, jnp.float32)
    for term in range(TERMS):
        rounded = gates.astype(jnp.bfloat16).astype(jnp.float32)
        terms = jnp.where(column // experts_all == term, rounded, terms)
        gates = gates - rounded
    tokens_ref[:, D:] = terms.astype(jnp.bfloat16)


def expert_kernel(
    experts_all,
    slots,
    expert_ref,
    tokens_hbm,
    gate_hbm,
    up_hbm,
    down_hbm,
    out_hbm,
    tokens_ref,
    gate_ref,
    up_ref,
    down_ref,
    picked_ref,
    weights_ref,
    places_ref,
    in_sems,
    weight_sems,
    out_sems,
):
    groups = tokens_ref.shape[0]
    batch = groups // BATCHES

    def tokens_in(g):
        at = pl.ds(pl.multiple_of(g * GROUP, GROUP), GROUP)
        return pltpu.make_async_copy(tokens_hbm.at[at], tokens_ref.at[g], in_sems.at[g])

    def result_out(g):
        at = pl.ds(pl.multiple_of(g * GROUP, GROUP), GROUP)
        return pltpu.make_async_copy(
            tokens_ref.at[g, :, pl.ds(0, D)], out_hbm.at[at], out_sems.at[g]
        )

    def weight_in(number, source, target):
        rows = source.shape[0] // PIECES
        return [
            pltpu.make_async_copy(
                source.at[pl.ds(i * rows, rows)],
                target.at[pl.ds(i * rows, rows)],
                weight_sems.at[number * PIECES + i],
            )
            for i in range(PIECES)
        ]

    gate_in = weight_in(0, gate_hbm, gate_ref)
    up_in = weight_in(1, up_hbm, up_ref)
    down_in = weight_in(2, down_hbm, down_ref)
    for g in range(batch):
        tokens_in(g).start()
    for copy in gate_in:
        copy.start()

    row = lax.broadcasted_iota(jnp.int32, (GROUP, GROUP), 0)
    col = lax.broadcasted_iota(jnp.int32, (GROUP, GROUP), 1)
    up_to = (row >= col).astype(jnp.bfloat16)
    slot_row = lax.broadcasted_iota(jnp.int32, (slots, GROUP), 0).astype(jnp.float32)
    slot_col = lax.broadcasted_iota(jnp.int32, (GROUP, slots), 1).astype(jnp.float32)

    def at_first(number, arrived, following):
        @pl.when(number == 0)
        def _():
            for copy in arrived:
                copy.wait()
            for copy in following:
                copy.start()

    def run_batch(number, carry):
        def pick(i, carry):
            g = number * batch + i
            tokens_in(g).wait()
            terms = tokens_ref[g, :, D:].astype(jnp.float32)
            column = lax.broadcasted_iota(jnp.int32, terms.shape, 1)
            mine = lax.rem(column, experts_all) == expert_ref[0]
            mine = mine & (column < TERMS * experts_all)
            gates = jnp.sum(jnp.where(mine, terms, 0.0), axis=1, keepdims=True)
            gates = jnp.broadcast_to(gates, (GROUP, LANES))
            named = gates > 0.0
            rank = jnp.dot(up_to, named.astype(jnp.bfloat16), preferred_element_type=jnp.float32)
            place = jnp.where(named, rank - 1.0, -1.0)
            chosen = (slot_row == jnp.transpose(place)[:1]).astype(jnp.bfloat16)
            picked = jnp.dot(chosen, tokens_ref[g, :, :D], preferred_element_type=jnp.float32)
            at = pl.ds(pl.multiple_of(i * slots, slots), slots)
            picked_ref[at, :] = picked.astype(jnp.bfloat16)
            weights_ref[i] = gates
            places_ref[i] = place
            return carry

        lax.fori_loop(0, batch, pick, 0)
        at_first(number, [], up_in)
        at_first(number, gate_in, down_in)
        gate_pre = jnp.dot(picked_ref[...], gate_ref[...], preferred_element_type=jnp.float32)
        at_first(number, up_in, [tokens_in(g) for g in range(batch, 2 * batch)])
        up_pre = jnp.dot(picked_ref[...], up_ref[...], preferred_element_type=jnp.float32)
        activated = (gate_pre / (1.0 + jnp.exp(-gate_pre)) * up_pre).astype(jnp.bfloat16)
        at_first(number, down_in, [tokens_in(g) for g in range(2 * batch, groups)])
        picked_ref[...] = jnp.dot(
            activated, down_ref[...], preferred_element_type=jnp.float32
        ).astype(jnp.bfloat16)

        def put(i, carry):
            g = number * batch + i
            at = pl.ds(pl.multiple_of(i * slots, slots), slots)
            spread = (slot_col == places_ref[i][:, :1]).astype(jnp.bfloat16)
            expert_out = jnp.dot(spread, picked_ref[at, :], preferred_element_type=jnp.float32)
            tokens_ref[g, :, :D] = (expert_out * weights_ref[i][:, :1]).astype(jnp.bfloat16)
            result_out(g).start()
            return carry

        lax.fori_loop(0, batch, put, 0)
        return carry

    lax.fori_loop(0, BATCHES, run_batch, 0)
    for g in range(groups):
        result_out(g).wait()


def vmem():
    return pl.BlockSpec(memory_space=pltpu.VMEM)


def smem():
    return pl.BlockSpec(memory_space=pltpu.SMEM)


def own_columns(position, matrix, n_parts):
    rows, width = matrix.shape
    return pl.pallas_call(
        columns_kernel,
        out_shape=jax.ShapeDtypeStruct((rows, width // n_parts), matrix.dtype),
        in_specs=[smem(), pl.BlockSpec(memory_space=pl.ANY)],
        out_specs=pl.BlockSpec(memory_space=pl.ANY),
        scratch_shapes=[pltpu.SemaphoreType.DMA(())],
        compiler_params=pltpu.CompilerParams(vmem_limit_bytes=60 * 1024 * 1024),
        name="columns",
    )(position.reshape(1), matrix)


def attend(position, core, queries, blocks, n_exp, proj_rows):
    rows = queries.shape[0]
    rings = core_rings(n_exp)
    places = {}
    for head in range(QH):
        device, inside = divmod(head * HD, proj_rows)
        places[head] = (device % 2, rings[device % 2].index(device) * proj_rows + inside)
    return pl.pallas_call(
        functools.partial(attention_kernel, places),
        out_shape=jax.ShapeDtypeStruct((2, rows, QH * HD // 2), jnp.bfloat16),
        in_specs=[smem()] + [vmem()] * (1 + len(blocks)),
        out_specs=vmem(),
        compiler_params=pltpu.CompilerParams(vmem_limit_bytes=16 * 1024 * 1024),
        name="attention",
    )(jnp.stack([position, core]), queries, *blocks)


def run_expert(experts_all, block_rows, expert, tokens, w_gate, w_up, w_down):
    total, width = tokens.shape
    ef = w_gate.shape[1]
    share = block_rows * TOP // experts_all
    capacity = min(block_rows, share + block_rows * TOP // (16 * experts_all))
    slots = min(GROUP, -(-(GROUP // block_rows * capacity) // 16) * 16)
    groups = total // GROUP
    batch = groups // BATCHES
    anywhere = pl.BlockSpec(memory_space=pl.ANY)
    return pl.pallas_call(
        functools.partial(expert_kernel, experts_all, slots),
        out_shape=jax.ShapeDtypeStruct((total, D), jnp.bfloat16),
        in_specs=[smem()] + [anywhere] * 4,
        out_specs=anywhere,
        scratch_shapes=[
            pltpu.VMEM((groups, GROUP, width), jnp.bfloat16),
            pltpu.VMEM((D, ef), jnp.bfloat16),
            pltpu.VMEM((D, ef), jnp.bfloat16),
            pltpu.VMEM((ef, D), jnp.bfloat16),
            pltpu.VMEM((batch * slots, D), jnp.bfloat16),
            pltpu.VMEM((batch, GROUP, LANES), jnp.float32),
            pltpu.VMEM((batch, GROUP, LANES), jnp.float32),
            pltpu.SemaphoreType.DMA((groups,)),
            pltpu.SemaphoreType.DMA((3 * PIECES,)),
            pltpu.SemaphoreType.DMA((groups,)),
        ],
        compiler_params=pltpu.CompilerParams(vmem_limit_bytes=56 * 1024 * 1024),
        cost_estimate=pl.CostEstimate(
            flops=4 * total * D * ef, bytes_accessed=4 * total * D + 6 * D * ef, transcendentals=0
        ),
        name="experts",
    )(expert.reshape(1), tokens, w_gate, w_up, w_down)


def body(
    hidden_in, query, keyval, out_proj, norm_gain, expert_ids, gate_weights, w_gate, w_up, w_down
):
    n_ctx = lax.axis_size("ctx")
    n_exp = lax.axis_size("exp")
    position = lax.axis_index("ctx")
    rows = hidden_in.shape[1]
    proj_rows = out_proj.shape[0]
    ring = [device_ring(n_exp)]

    columns = lax.all_gather(
        own_columns(position, out_proj, n_ctx),
        "exp",
        axis=0,
        tiled=True,
        axis_index_groups=core_rings(n_exp),
    )

    def times_columns(block):
        return jnp.dot(block, columns, preferred_element_type=jnp.float32)

    core = lax.axis_index("exp") % 2
    blocks = [keyval[0]] + [rotate(keyval[0], "ctx", back) for back in range(1, n_ctx)]
    attended = attend(position, core, query[0], blocks, n_exp, proj_rows)
    own_heads, other_heads = attended[0], attended[1]
    sibling_heads = swap_cores(other_heads)
    projected = []
    for back in range(n_ctx):
        heads = [rotate(own_heads, "ctx", back), rotate(sibling_heads, "ctx", back)]
        from_sibling = swap_cores(times_columns(heads[1]).astype(jnp.bfloat16))
        part = times_columns(heads[0]) + from_sibling.astype(jnp.float32)
        if back:
            part = rotate(part.astype(jnp.bfloat16), "ctx", -back)
        projected.append(part)

    local_experts = w_gate.shape[0]
    experts_all = n_exp * local_experts
    extra = -(-TERMS * experts_all // LANES) * LANES
    residual, tokens = pl.pallas_call(
        functools.partial(norm_kernel, experts_all),
        out_shape=(
            jax.ShapeDtypeStruct((rows, D), jnp.float32),
            jax.ShapeDtypeStruct((rows, D + extra), jnp.bfloat16),
        ),
        in_specs=[smem()] + [vmem()] * (4 + n_ctx),
        out_specs=(vmem(), vmem()),
        compiler_params=pltpu.CompilerParams(vmem_limit_bytes=16 * 1024 * 1024),
        name="norm",
    )(
        position.reshape(1),
        hidden_in[0],
        *projected,
        norm_gain.reshape(1, D),
        expert_ids[0],
        gate_weights[0],
    )

    tokens_all = lax.all_gather(tokens, "exp", axis=0, tiled=True, axis_index_groups=ring)
    partial = None
    for local in range(local_experts):
        expert = lax.axis_index("exp") * local_experts + local
        weighted = run_expert(
            experts_all, rows, expert, tokens_all, w_gate[local], w_up[local], w_down[local]
        )
        partial = weighted if partial is None else partial + weighted
    expert_sum = lax.psum_scatter(
        partial, "exp", scatter_dimension=0, axis_index_groups=ring, tiled=True
    )
    result = (residual + expert_sum.astype(jnp.float32)).astype(jnp.bfloat16)
    return result[None]


def solution(mesh):
    in_specs = (
        P("exp", "ctx", None),
        P("exp", "ctx", None),
        P("exp", "ctx", None),
        P("exp", None),
        P(),
        P("exp", "ctx", None),
        P("exp", "ctx", None),
        P("exp", None, None),
        P("exp", None, None),
        P("exp", None, None),
    )
    out_specs = P("exp", "ctx", None)
    return jax.shard_map(body, mesh=mesh, in_specs=in_specs, out_specs=out_specs, check_vma=False)
```

```python
import functools

import jax
import jax.numpy as jnp
from jax import lax
from jax.experimental import pallas as pl
from jax.experimental.pallas import tpu as pltpu
from jax.sharding import PartitionSpec as P

D = 2048
QH = 32
KVH = 2
HD = 128
TOP = 8
LANES = 128
TERMS = 3


def chip_ring(n):
    chips = n // 2
    return list(range(0, chips, 2)) + list(range(1, chips, 2))[::-1]


def device_ring(n):
    return [2 * chip + core for chip in chip_ring(n) for core in range(2)]


def core_rings(n):
    return [[2 * chip + core for chip in chip_ring(n)] for core in range(2)]


def swap_cores(block):
    n = lax.axis_size("exp")
    return lax.ppermute(block, "exp", [(i, i ^ 1) for i in range(n)])


def round_ring(block, direction):
    n = lax.axis_size("exp")
    route = []
    for ring in core_rings(n):
        route += [(ring[i], ring[(i + direction) % len(ring)]) for i in range(len(ring))]
    return lax.ppermute(block, "exp", route)


def rotate(block, axis, distance):
    if distance == 0:
        return block
    n = lax.axis_size(axis)
    return lax.ppermute(block, axis, [(i, (i + distance) % n) for i in range(n)])


def attention_kernel(places, pos_ref, query_ref, *refs):
    *kv_refs, out_ref = refs
    n_ctx = len(kv_refs)
    position = pos_ref[0]
    rows = query_ref.shape[0]
    row = lax.broadcasted_iota(jnp.int32, (rows, rows), 0)
    col = lax.broadcasted_iota(jnp.int32, (rows, rows), 1)
    visible = [row >= col]
    for back in range(1, n_ctx):
        visible.append(jnp.full((rows, rows), position, jnp.int32) >= back)
    visible = jnp.concatenate(visible, axis=1)
    for kv_head in range(KVH):
        k_at = kv_head * HD
        v_at = (KVH + kv_head) * HD
        keys = jnp.concatenate([ref[:, k_at : k_at + HD] for ref in kv_refs], axis=0)
        values = jnp.concatenate([ref[:, v_at : v_at + HD] for ref in kv_refs], axis=0)
        for group in range(QH // KVH):
            head = kv_head * (QH // KVH) + group
            scores = lax.dot_general(
                query_ref[:, head * HD : (head + 1) * HD],
                keys,
                (((1,), (1,)), ((), ())),
                preferred_element_type=jnp.float32,
            ) * HD ** (-0.5)
            scores = jnp.where(visible, scores, -1e30)
            weights = jnp.exp(scores - jnp.max(scores, axis=1, keepdims=True))
            row_sum = jnp.sum(weights, axis=1, keepdims=True)
            mixed = jnp.dot(
                weights.astype(jnp.bfloat16), values, preferred_element_type=jnp.float32
            )
            core, at = places[head]
            slot = lax.rem(core + pos_ref[1], 2)
            out_ref[slot, :, at : at + HD] = (mixed / row_sum).astype(jnp.bfloat16)


def norm_kernel(experts_all, pos_ref, hidden_ref, *refs):
    *projected_refs, gain_ref, ids_ref, gates_ref, residual_ref, tokens_ref = refs
    n_ctx = len(projected_refs)
    wide = D // n_ctx
    square_sum = None
    for back, ref in enumerate(projected_refs):
        at = pl.ds(pl.multiple_of(lax.rem(pos_ref[0] + back, n_ctx) * wide, wide), wide)
        part = hidden_ref[:, at].astype(jnp.float32) + ref[...].astype(jnp.float32)
        residual_ref[:, at] = part
        squares = jnp.sum(part * part, axis=1, keepdims=True)
        square_sum = squares if square_sum is None else square_sum + squares
    scale_inv = lax.rsqrt(square_sum * (1.0 / D) + 1e-06)
    normed = residual_ref[...] * scale_inv * gain_ref[...].astype(jnp.float32)
    tokens_ref[:, :D] = normed.astype(jnp.bfloat16)
    shape = (tokens_ref.shape[0], tokens_ref.shape[1] - D)
    column = lax.broadcasted_iota(jnp.int32, shape, 1)
    expert = lax.rem(column, experts_all)
    gates = jnp.zeros(shape, jnp.float32)
    for k in range(TOP):
        gates = gates + jnp.where(ids_ref[:, k : k + 1] == expert, gates_ref[:, k : k + 1], 0.0)
    terms = jnp.zeros(shape, jnp.float32)
    for term in range(TERMS):
        rounded = gates.astype(jnp.bfloat16).astype(jnp.float32)
        terms = jnp.where(column // experts_all == term, rounded, terms)
        gates = gates - rounded
    tokens_ref[:, D:] = terms.astype(jnp.bfloat16)


def expert_kernel(experts_all, n_chip, offsets, parts, chained, where_ref, *refs):
    groups = len(offsets)
    gate_ref, up_ref, down_ref, *refs = refs
    block_refs, refs = refs[: 2 * groups * parts], refs[2 * groups * parts + chained :]
    out_hbm, result_ref, sems = refs
    blocks = jnp.concatenate([ref[...] for ref in block_refs], axis=0)
    terms = blocks[:, D:].astype(jnp.float32)
    column = lax.broadcasted_iota(jnp.int32, terms.shape, 1)
    mine = (lax.rem(column, experts_all) == where_ref[0]) & (column < TERMS * experts_all)
    gates = jnp.sum(jnp.where(mine, terms, 0.0), axis=1, keepdims=True)
    tokens = blocks[:, :D]
    gate_pre = jnp.dot(tokens, gate_ref[...], preferred_element_type=jnp.float32)
    up_pre = jnp.dot(tokens, up_ref[...], preferred_element_type=jnp.float32)
    activated = (gate_pre / (1.0 + jnp.exp(-gate_pre)) * up_pre).astype(jnp.bfloat16)
    expert_out = jnp.dot(activated, down_ref[...], preferred_element_type=jnp.float32)
    weighted = jnp.where(gates > 0.0, expert_out * gates, 0.0).astype(jnp.bfloat16)
    rows = blocks.shape[0] // (2 * groups)
    copies = []
    for g in range(groups):
        for other in range(2):
            core = lax.rem(where_ref[1] + other, 2)
            at = pl.ds(pl.multiple_of(core * rows, rows), rows)
            start = (2 * g + other) * rows
            result_ref[g, at, :] = weighted[start : start + rows]
        place = lax.rem(where_ref[2] + offsets[g], n_chip)
        at = pl.ds(pl.multiple_of(place * (2 * rows), 2 * rows), 2 * rows)
        copies.append(pltpu.make_async_copy(result_ref.at[g], out_hbm.at[at], sems.at[g]))
        copies[-1].start()
    for copy in copies:
        copy.wait()


def vmem():
    return pl.BlockSpec(memory_space=pltpu.VMEM)


def smem():
    return pl.BlockSpec(memory_space=pltpu.SMEM)


def attend(position, core, queries, blocks, n_exp, proj_rows):
    rows = queries.shape[0]
    rings = core_rings(n_exp)
    places = {}
    for head in range(QH):
        device, inside = divmod(head * HD, proj_rows)
        places[head] = (device % 2, rings[device % 2].index(device) * proj_rows + inside)
    return pl.pallas_call(
        functools.partial(attention_kernel, places),
        out_shape=jax.ShapeDtypeStruct((2, rows, QH * HD // 2), jnp.bfloat16),
        in_specs=[smem()] + [vmem()] * (1 + len(blocks)),
        out_specs=vmem(),
        compiler_params=pltpu.CompilerParams(vmem_limit_bytes=16 * 1024 * 1024),
        name="attention",
    )(jnp.stack([position, core]), queries, *blocks)


def run_expert(experts_all, n_chip, where, chips, earlier, weights):
    groups, parts = len(chips), len(chips[0][1])
    blocks = [block for _, own, other in chips for block in own + other]
    rows = sum(block.shape[0] for block in blocks) // (2 * groups)
    offsets = [offset for offset, _, _ in chips]
    anywhere = pl.BlockSpec(memory_space=pl.ANY)
    chained = [] if earlier is None else [earlier]
    ef = weights[0].shape[1]
    return pl.pallas_call(
        functools.partial(expert_kernel, experts_all, n_chip, offsets, parts, len(chained)),
        out_shape=jax.ShapeDtypeStruct((n_chip * 2 * rows, D), jnp.bfloat16),
        in_specs=[smem()] + [vmem()] * (3 + len(blocks)) + [anywhere] * len(chained),
        out_specs=anywhere,
        scratch_shapes=[
            pltpu.VMEM((groups, 2 * rows, D), jnp.bfloat16),
            pltpu.SemaphoreType.DMA((groups,)),
        ],
        input_output_aliases={4 + len(blocks): 0} if chained else {},
        compiler_params=pltpu.CompilerParams(vmem_limit_bytes=38 * 1024 * 1024),
        cost_estimate=pl.CostEstimate(
            flops=12 * groups * rows * D * ef,
            bytes_accessed=8 * groups * rows * D + 6 * D * ef,
            transcendentals=0,
        ),
        name="experts",
    )(where, *weights, *blocks, *chained)


def body(
    hidden_in, query, keyval, out_proj, norm_gain, expert_ids, gate_weights, w_gate, w_up, w_down
):
    n_ctx = lax.axis_size("ctx")
    n_exp = lax.axis_size("exp")
    position = lax.axis_index("ctx")
    rows = hidden_in.shape[1]
    proj_rows = out_proj.shape[0]
    wide = D // n_ctx
    columns = lax.all_gather(
        lax.dynamic_slice_in_dim(out_proj, position * wide, wide, axis=1),
        "exp",
        axis=0,
        tiled=True,
        axis_index_groups=core_rings(n_exp),
    )

    def times_columns(block):
        return jnp.dot(block, columns, preferred_element_type=jnp.float32)

    core = lax.axis_index("exp") % 2
    blocks = [keyval[0]] + [rotate(keyval[0], "ctx", back) for back in range(1, n_ctx)]
    attended = attend(position, core, query[0], blocks, n_exp, proj_rows)
    own_heads, other_heads = attended[0], attended[1]
    sibling_heads = swap_cores(other_heads)
    projected = []
    for back in range(n_ctx):
        heads = [rotate(own_heads, "ctx", back), rotate(sibling_heads, "ctx", back)]
        from_sibling = swap_cores(times_columns(heads[1]).astype(jnp.bfloat16))
        part = times_columns(heads[0]) + from_sibling.astype(jnp.float32)
        if back:
            part = rotate(part.astype(jnp.bfloat16), "ctx", -back)
        projected.append(part)

    local_experts = w_gate.shape[0]
    experts_all = n_exp * local_experts
    extra = -(-TERMS * experts_all // LANES) * LANES
    residual, tokens = pl.pallas_call(
        functools.partial(norm_kernel, experts_all),
        out_shape=(
            jax.ShapeDtypeStruct((rows, D), jnp.float32),
            jax.ShapeDtypeStruct((rows, D + extra), jnp.bfloat16),
        ),
        in_specs=[smem()] + [vmem()] * (4 + n_ctx),
        out_specs=(vmem(), vmem()),
        compiler_params=pltpu.CompilerParams(vmem_limit_bytes=16 * 1024 * 1024),
        name="norm",
    )(
        position.reshape(1),
        hidden_in[0],
        *projected,
        norm_gain.reshape(1, D),
        expert_ids[0],
        gate_weights[0],
    )

    n_chip = n_exp // 2
    chip = lax.axis_index("exp") // 2
    place = jnp.where(chip % 2 == 0, chip // 2, n_chip - 1 - chip // 2)
    arrived = [[(0, [tokens], [swap_cores(tokens)])]]
    forward, backward = tokens, tokens
    for step in range(1, n_chip // 2):
        forward, backward = round_ring(forward, 1), round_ring(backward, -1)
        arrived.append(
            [
                (n_chip - step, [forward], [swap_cores(forward)]),
                (step, [backward], [swap_cores(backward)]),
            ]
        )
    halves = [round_ring(forward[: rows // 2], 1), round_ring(backward[rows // 2 :], -1)]
    arrived.append([(n_chip // 2, halves, [swap_cores(half) for half in halves])])

    partial = None
    for local in range(local_experts):
        expert = lax.axis_index("exp") * local_experts + local
        where = jnp.stack([expert, core, place])
        weights = (w_gate[local], w_up[local], w_down[local])
        weighted = None
        for chips in arrived:
            weighted = run_expert(experts_all, n_chip, where, chips, weighted, weights)
        partial = weighted if partial is None else partial + weighted
    expert_sum = lax.psum_scatter(
        partial,
        "exp",
        scatter_dimension=0,
        axis_index_groups=[device_ring(n_exp)],
        tiled=True,
    )
    result = (residual + expert_sum.astype(jnp.float32)).astype(jnp.bfloat16)
    return result[None]


def solution(mesh):
    in_specs = (
        P("exp", "ctx", None),
        P("exp", "ctx", None),
        P("exp", "ctx", None),
        P("exp", None),
        P(),
        P("exp", "ctx", None),
        P("exp", "ctx", None),
        P("exp", None, None),
        P("exp", None, None),
        P("exp", None, None),
    )
    out_specs = P("exp", "ctx", None)
    return jax.shard_map(body, mesh=mesh, in_specs=in_specs, out_specs=out_specs, check_vma=False)
```

```python
import functools

import jax
import jax.numpy as jnp
from jax import lax
from jax.experimental import pallas as pl
from jax.experimental.pallas import tpu as pltpu
from jax.sharding import PartitionSpec as P

D = 2048
QH = 32
KVH = 2
HD = 128
TOP = 8
LANES = 128
TERMS = 3


def chip_ring(n):
    chips = n // 2
    return list(range(0, chips, 2)) + list(range(1, chips, 2))[::-1]


def device_ring(n):
    return [2 * chip + core for chip in chip_ring(n) for core in range(2)]


def core_rings(n):
    return [[2 * chip + core for chip in chip_ring(n)] for core in range(2)]


def swap_cores(block):
    n = lax.axis_size("exp")
    return lax.ppermute(block, "exp", [(i, i ^ 1) for i in range(n)])


def round_ring(block, direction):
    n = lax.axis_size("exp")
    route = []
    for ring in core_rings(n):
        route += [(ring[i], ring[(i + direction) % len(ring)]) for i in range(len(ring))]
    return lax.ppermute(block, "exp", route)


def rotate(block, axis, distance):
    if distance == 0:
        return block
    n = lax.axis_size(axis)
    return lax.ppermute(block, axis, [(i, (i + distance) % n) for i in range(n)])


def attention_kernel(places, pos_ref, query_ref, *refs):
    *kv_refs, out_ref = refs
    n_ctx = len(kv_refs)
    position = pos_ref[0]
    rows = query_ref.shape[0]
    row = lax.broadcasted_iota(jnp.int32, (rows, rows), 0)
    col = lax.broadcasted_iota(jnp.int32, (rows, rows), 1)
    visible = [row >= col]
    for back in range(1, n_ctx):
        visible.append(jnp.full((rows, rows), position, jnp.int32) >= back)
    visible = jnp.concatenate(visible, axis=1)
    for kv_head in range(KVH):
        k_at = kv_head * HD
        v_at = (KVH + kv_head) * HD
        keys = jnp.concatenate([ref[:, k_at : k_at + HD] for ref in kv_refs], axis=0)
        values = jnp.concatenate([ref[:, v_at : v_at + HD] for ref in kv_refs], axis=0)
        for group in range(QH // KVH):
            head = kv_head * (QH // KVH) + group
            scores = lax.dot_general(
                query_ref[:, head * HD : (head + 1) * HD],
                keys,
                (((1,), (1,)), ((), ())),
                preferred_element_type=jnp.float32,
            ) * HD ** (-0.5)
            scores = jnp.where(visible, scores, -1e30)
            weights = jnp.exp(scores - jnp.max(scores, axis=1, keepdims=True))
            row_sum = jnp.sum(weights, axis=1, keepdims=True)
            mixed = jnp.dot(
                weights.astype(jnp.bfloat16), values, preferred_element_type=jnp.float32
            )
            core, at = places[head]
            slot = lax.rem(core + pos_ref[1], 2)
            out_ref[slot, :, at : at + HD] = (mixed / row_sum).astype(jnp.bfloat16)


def norm_kernel(experts_all, pos_ref, hidden_ref, *refs):
    *projected_refs, gain_ref, ids_ref, gates_ref, residual_ref, tokens_ref = refs
    n_ctx = len(projected_refs)
    wide = D // n_ctx
    square_sum = None
    for back, ref in enumerate(projected_refs):
        at = pl.ds(pl.multiple_of(lax.rem(pos_ref[0] + back, n_ctx) * wide, wide), wide)
        part = hidden_ref[:, at].astype(jnp.float32) + ref[...].astype(jnp.float32)
        residual_ref[:, at] = part
        squares = jnp.sum(part * part, axis=1, keepdims=True)
        square_sum = squares if square_sum is None else square_sum + squares
    scale_inv = lax.rsqrt(square_sum * (1.0 / D) + 1e-06)
    normed = residual_ref[...] * scale_inv * gain_ref[...].astype(jnp.float32)
    tokens_ref[:, :D] = normed.astype(jnp.bfloat16)
    shape = (tokens_ref.shape[0], tokens_ref.shape[1] - D)
    column = lax.broadcasted_iota(jnp.int32, shape, 1)
    expert = lax.rem(column, experts_all)
    gates = jnp.zeros(shape, jnp.float32)
    for k in range(TOP):
        gates = gates + jnp.where(ids_ref[:, k : k + 1] == expert, gates_ref[:, k : k + 1], 0.0)
    terms = jnp.zeros(shape, jnp.float32)
    for term in range(TERMS):
        rounded = gates.astype(jnp.bfloat16).astype(jnp.float32)
        terms = jnp.where(column // experts_all == term, rounded, terms)
        gates = gates - rounded
    tokens_ref[:, D:] = terms.astype(jnp.bfloat16)


def expert_kernel(experts_all, n_chip, offsets, parts, chained, where_ref, *refs):
    groups = len(offsets)
    gate_ref, up_ref, down_ref, *refs = refs
    block_refs, refs = refs[: 2 * groups * parts], refs[2 * groups * parts + chained :]
    out_hbm, result_ref, sems = refs
    blocks = jnp.concatenate([ref[...] for ref in block_refs], axis=0)
    terms = blocks[:, D:].astype(jnp.float32)
    column = lax.broadcasted_iota(jnp.int32, terms.shape, 1)
    mine = (lax.rem(column, experts_all) == where_ref[0]) & (column < TERMS * experts_all)
    gates = jnp.sum(jnp.where(mine, terms, 0.0), axis=1, keepdims=True)
    tokens = blocks[:, :D]
    gate_pre = jnp.dot(tokens, gate_ref[...], preferred_element_type=jnp.float32)
    up_pre = jnp.dot(tokens, up_ref[...], preferred_element_type=jnp.float32)
    activated = (gate_pre / (1.0 + jnp.exp(-gate_pre)) * up_pre).astype(jnp.bfloat16)
    expert_out = jnp.dot(activated, down_ref[...], preferred_element_type=jnp.float32)
    weighted = jnp.where(gates > 0.0, expert_out * gates, 0.0).astype(jnp.bfloat16)
    rows = blocks.shape[0] // (2 * groups)
    copies = []
    for g in range(groups):
        for other in range(2):
            core = lax.rem(where_ref[1] + other, 2)
            at = pl.ds(pl.multiple_of(core * rows, rows), rows)
            start = (2 * g + other) * rows
            result_ref[g, at, :] = weighted[start : start + rows]
        place = lax.rem(where_ref[2] + offsets[g], n_chip)
        at = pl.ds(pl.multiple_of(place * (2 * rows), 2 * rows), 2 * rows)
        copies.append(pltpu.make_async_copy(result_ref.at[g], out_hbm.at[at], sems.at[g]))
        copies[-1].start()
    for copy in copies:
        copy.wait()


def vmem():
    return pl.BlockSpec(memory_space=pltpu.VMEM)


def smem():
    return pl.BlockSpec(memory_space=pltpu.SMEM)


def attend(position, core, queries, blocks, n_exp, proj_rows):
    rows = queries.shape[0]
    rings = core_rings(n_exp)
    places = {}
    for head in range(QH):
        device, inside = divmod(head * HD, proj_rows)
        places[head] = (device % 2, rings[device % 2].index(device) * proj_rows + inside)
    return pl.pallas_call(
        functools.partial(attention_kernel, places),
        out_shape=jax.ShapeDtypeStruct((2, rows, QH * HD // 2), jnp.bfloat16),
        in_specs=[smem()] + [vmem()] * (1 + len(blocks)),
        out_specs=vmem(),
        compiler_params=pltpu.CompilerParams(vmem_limit_bytes=16 * 1024 * 1024),
        name="attention",
    )(jnp.stack([position, core]), queries, *blocks)


def run_expert(experts_all, n_chip, where, chips, earlier, weights):
    groups, parts = len(chips), len(chips[0][1])
    blocks = [block for _, own, other in chips for block in own + other]
    rows = sum(block.shape[0] for block in blocks) // (2 * groups)
    offsets = [offset for offset, _, _ in chips]
    anywhere = pl.BlockSpec(memory_space=pl.ANY)
    chained = [] if earlier is None else [earlier]
    ef = weights[0].shape[1]
    return pl.pallas_call(
        functools.partial(expert_kernel, experts_all, n_chip, offsets, parts, len(chained)),
        out_shape=jax.ShapeDtypeStruct((n_chip * 2 * rows, D), jnp.bfloat16),
        in_specs=[smem()] + [vmem()] * (3 + len(blocks)) + [anywhere] * len(chained),
        out_specs=anywhere,
        scratch_shapes=[
            pltpu.VMEM((groups, 2 * rows, D), jnp.bfloat16),
            pltpu.SemaphoreType.DMA((groups,)),
        ],
        input_output_aliases={4 + len(blocks): 0} if chained else {},
        compiler_params=pltpu.CompilerParams(vmem_limit_bytes=38 * 1024 * 1024),
        cost_estimate=pl.CostEstimate(
            flops=12 * groups * rows * D * ef,
            bytes_accessed=8 * groups * rows * D + 6 * D * ef,
            transcendentals=0,
        ),
        name="experts",
    )(where, *weights, *blocks, *chained)


def body(
    hidden_in, query, keyval, out_proj, norm_gain, expert_ids, gate_weights, w_gate, w_up, w_down
):
    n_ctx = lax.axis_size("ctx")
    n_exp = lax.axis_size("exp")
    position = lax.axis_index("ctx")
    rows = hidden_in.shape[1]
    proj_rows = out_proj.shape[0]
    wide = D // n_ctx
    columns = lax.all_gather(
        lax.dynamic_slice_in_dim(out_proj, position * wide, wide, axis=1),
        "exp",
        axis=0,
        tiled=True,
        axis_index_groups=core_rings(n_exp),
    )

    def times_columns(block):
        return jnp.dot(block, columns, preferred_element_type=jnp.float32)

    core = lax.axis_index("exp") % 2
    blocks = [keyval[0]] + [rotate(keyval[0], "ctx", back) for back in range(1, n_ctx)]
    attended = attend(position, core, query[0], blocks, n_exp, proj_rows)
    own_heads, other_heads = attended[0], attended[1]
    sibling_heads = swap_cores(other_heads)
    projected = []
    for back in range(n_ctx):
        heads = [rotate(own_heads, "ctx", back), rotate(sibling_heads, "ctx", back)]
        from_sibling = swap_cores(times_columns(heads[1]).astype(jnp.bfloat16))
        part = times_columns(heads[0]) + from_sibling.astype(jnp.float32)
        if back:
            part = rotate(part.astype(jnp.bfloat16), "ctx", -back)
        projected.append(part)

    local_experts = w_gate.shape[0]
    experts_all = n_exp * local_experts
    extra = -(-TERMS * experts_all // LANES) * LANES
    residual, tokens = pl.pallas_call(
        functools.partial(norm_kernel, experts_all),
        out_shape=(
            jax.ShapeDtypeStruct((rows, D), jnp.float32),
            jax.ShapeDtypeStruct((rows, D + extra), jnp.bfloat16),
        ),
        in_specs=[smem()] + [vmem()] * (4 + n_ctx),
        out_specs=(vmem(), vmem()),
        compiler_params=pltpu.CompilerParams(vmem_limit_bytes=16 * 1024 * 1024),
        name="norm",
    )(
        position.reshape(1),
        hidden_in[0],
        *projected,
        norm_gain.reshape(1, D),
        expert_ids[0],
        gate_weights[0],
    )

    n_chip = n_exp // 2
    chip = lax.axis_index("exp") // 2
    place = jnp.where(chip % 2 == 0, chip // 2, n_chip - 1 - chip // 2)

    def experts_on(chips, earlier):
        results = []
        for local in range(local_experts):
            where = jnp.stack([lax.axis_index("exp") * local_experts + local, core, place])
            weights = (w_gate[local], w_up[local], w_down[local])
            before = None if earlier is None else earlier[local]
            results.append(run_expert(experts_all, n_chip, where, chips, before, weights))
        return results

    def send_on(forward, backward, step):
        if step < n_chip // 2:
            return round_ring(forward, 1), round_ring(backward, -1)
        return round_ring(forward[: rows // 2], 1), round_ring(backward[rows // 2 :], -1)

    forward, backward = send_on(tokens, tokens, 1)
    weighted = experts_on([(0, [tokens], [swap_cores(tokens)])], None)
    forward, backward, weighted = lax.optimization_barrier((forward, backward, weighted))
    for step in range(1, n_chip // 2):
        chips = [
            (n_chip - step, [forward], [swap_cores(forward)]),
            (step, [backward], [swap_cores(backward)]),
        ]
        forward, backward = send_on(forward, backward, step + 1)
        weighted = experts_on(chips, weighted)
        forward, backward, weighted = lax.optimization_barrier((forward, backward, weighted))
    halves = [forward, backward]
    swapped = [swap_cores(half) for half in halves]
    weighted = experts_on([(n_chip // 2, halves, swapped)], weighted)
    partial = functools.reduce(jnp.add, weighted)
    expert_sum = lax.psum_scatter(
        partial,
        "exp",
        scatter_dimension=0,
        axis_index_groups=[device_ring(n_exp)],
        tiled=True,
    )
    result = (residual + expert_sum.astype(jnp.float32)).astype(jnp.bfloat16)
    return result[None]


def solution(mesh):
    in_specs = (
        P("exp", "ctx", None),
        P("exp", "ctx", None),
        P("exp", "ctx", None),
        P("exp", None),
        P(),
        P("exp", "ctx", None),
        P("exp", "ctx", None),
        P("exp", None, None),
        P("exp", None, None),
        P("exp", None, None),
    )
    out_specs = P("exp", "ctx", None)
    return jax.shard_map(body, mesh=mesh, in_specs=in_specs, out_specs=out_specs, check_vma=False)
```

```python
import functools

import jax
import jax.numpy as jnp
from jax import lax
from jax.experimental import pallas as pl
from jax.experimental.pallas import tpu as pltpu
from jax.sharding import PartitionSpec as P

D = 2048
QH = 32
KVH = 2
HD = 128
TOP = 8
LANES = 128
TERMS = 3


def chip_ring(n):
    chips = n // 2
    return list(range(0, chips, 2)) + list(range(1, chips, 2))[::-1]


def device_ring(n):
    return [2 * chip + core for chip in chip_ring(n) for core in range(2)]


def core_rings(n):
    return [[2 * chip + core for chip in chip_ring(n)] for core in range(2)]


def swap_cores(block):
    n = lax.axis_size("exp")
    return lax.ppermute(block, "exp", [(i, i ^ 1) for i in range(n)])


def round_ring(block, direction):
    n = lax.axis_size("exp")
    route = []
    for ring in core_rings(n):
        route += [(ring[i], ring[(i + direction) % len(ring)]) for i in range(len(ring))]
    return lax.ppermute(block, "exp", route)


def rotate(block, axis, distance):
    if distance == 0:
        return block
    n = lax.axis_size(axis)
    return lax.ppermute(block, axis, [(i, (i + distance) % n) for i in range(n)])


def attention_kernel(places, pos_ref, query_ref, *refs):
    *kv_refs, out_ref = refs
    n_ctx = len(kv_refs)
    position = pos_ref[0]
    rows = query_ref.shape[0]
    row = lax.broadcasted_iota(jnp.int32, (rows, rows), 0)
    col = lax.broadcasted_iota(jnp.int32, (rows, rows), 1)
    visible = [row >= col]
    for back in range(1, n_ctx):
        visible.append(jnp.full((rows, rows), position, jnp.int32) >= back)
    visible = jnp.concatenate(visible, axis=1)
    for kv_head in range(KVH):
        k_at = kv_head * HD
        v_at = (KVH + kv_head) * HD
        keys = jnp.concatenate([ref[:, k_at : k_at + HD] for ref in kv_refs], axis=0)
        values = jnp.concatenate([ref[:, v_at : v_at + HD] for ref in kv_refs], axis=0)
        for group in range(QH // KVH):
            head = kv_head * (QH // KVH) + group
            scores = lax.dot_general(
                query_ref[:, head * HD : (head + 1) * HD],
                keys,
                (((1,), (1,)), ((), ())),
                preferred_element_type=jnp.float32,
            ) * HD ** (-0.5)
            scores = jnp.where(visible, scores, -1e30)
            weights = jnp.exp(scores - jnp.max(scores, axis=1, keepdims=True))
            row_sum = jnp.sum(weights, axis=1, keepdims=True)
            mixed = jnp.dot(
                weights.astype(jnp.bfloat16), values, preferred_element_type=jnp.float32
            )
            core, at = places[head]
            slot = lax.rem(core + pos_ref[1], 2)
            out_ref[slot, :, at : at + HD] = (mixed / row_sum).astype(jnp.bfloat16)


def norm_kernel(experts_all, pos_ref, hidden_ref, *refs):
    *projected_refs, gain_ref, ids_ref, gates_ref, residual_ref, tokens_ref = refs
    n_ctx = len(projected_refs)
    wide = D // n_ctx
    square_sum = None
    for back, ref in enumerate(projected_refs):
        at = pl.ds(pl.multiple_of(lax.rem(pos_ref[0] + back, n_ctx) * wide, wide), wide)
        part = hidden_ref[:, at].astype(jnp.float32) + ref[...].astype(jnp.float32)
        residual_ref[:, at] = part
        squares = jnp.sum(part * part, axis=1, keepdims=True)
        square_sum = squares if square_sum is None else square_sum + squares
    scale_inv = lax.rsqrt(square_sum * (1.0 / D) + 1e-06)
    normed = residual_ref[...] * scale_inv * gain_ref[...].astype(jnp.float32)
    tokens_ref[:, :D] = normed.astype(jnp.bfloat16)
    shape = (tokens_ref.shape[0], tokens_ref.shape[1] - D)
    column = lax.broadcasted_iota(jnp.int32, shape, 1)
    expert = lax.rem(column, experts_all)
    gates = jnp.zeros(shape, jnp.float32)
    for k in range(TOP):
        gates = gates + jnp.where(ids_ref[:, k : k + 1] == expert, gates_ref[:, k : k + 1], 0.0)
    terms = jnp.zeros(shape, jnp.float32)
    for term in range(TERMS):
        rounded = gates.astype(jnp.bfloat16).astype(jnp.float32)
        terms = jnp.where(column // experts_all == term, rounded, terms)
        gates = gates - rounded
    tokens_ref[:, D:] = terms.astype(jnp.bfloat16)


def expert_kernel(experts_all, groups, parts, expert_ref, *refs):
    gate_ref, up_ref, down_ref, *refs = refs
    block_refs, out_refs = refs[: 2 * groups * parts], refs[2 * groups * parts :]
    blocks = jnp.concatenate([ref[...] for ref in block_refs], axis=0)
    terms = blocks[:, D:].astype(jnp.float32)
    column = lax.broadcasted_iota(jnp.int32, terms.shape, 1)
    mine = (lax.rem(column, experts_all) == expert_ref[0]) & (column < TERMS * experts_all)
    gates = jnp.sum(jnp.where(mine, terms, 0.0), axis=1, keepdims=True)
    tokens = blocks[:, :D]
    gate_pre = jnp.dot(tokens, gate_ref[...], preferred_element_type=jnp.float32)
    up_pre = jnp.dot(tokens, up_ref[...], preferred_element_type=jnp.float32)
    activated = (gate_pre / (1.0 + jnp.exp(-gate_pre)) * up_pre).astype(jnp.bfloat16)
    expert_out = jnp.dot(activated, down_ref[...], preferred_element_type=jnp.float32)
    weighted = jnp.where(gates > 0.0, expert_out * gates, 0.0).astype(jnp.bfloat16)
    rows = out_refs[0].shape[0]
    for i, ref in enumerate(out_refs):
        ref[...] = weighted[i * rows : (i + 1) * rows]


def vmem():
    return pl.BlockSpec(memory_space=pltpu.VMEM)


def smem():
    return pl.BlockSpec(memory_space=pltpu.SMEM)


def attend(position, core, queries, blocks, n_exp, proj_rows):
    rows = queries.shape[0]
    rings = core_rings(n_exp)
    places = {}
    for head in range(QH):
        device, inside = divmod(head * HD, proj_rows)
        places[head] = (device % 2, rings[device % 2].index(device) * proj_rows + inside)
    return pl.pallas_call(
        functools.partial(attention_kernel, places),
        out_shape=jax.ShapeDtypeStruct((2, rows, QH * HD // 2), jnp.bfloat16),
        in_specs=[smem()] + [vmem()] * (1 + len(blocks)),
        out_specs=vmem(),
        compiler_params=pltpu.CompilerParams(vmem_limit_bytes=16 * 1024 * 1024),
        name="attention",
    )(jnp.stack([position, core]), queries, *blocks)


def run_expert(experts_all, expert, chips, weights):
    groups, parts = len(chips), len(chips[0][0])
    blocks = [block for own, other in chips for block in own + other]
    rows = sum(block.shape[0] for block in blocks) // (2 * groups)
    ef = weights[0].shape[1]
    results = pl.pallas_call(
        functools.partial(expert_kernel, experts_all, groups, parts),
        out_shape=[jax.ShapeDtypeStruct((rows, D), jnp.bfloat16)] * (2 * groups),
        in_specs=[smem()] + [vmem()] * (3 + len(blocks)),
        out_specs=[vmem()] * (2 * groups),
        compiler_params=pltpu.CompilerParams(vmem_limit_bytes=38 * 1024 * 1024),
        cost_estimate=pl.CostEstimate(
            flops=12 * groups * rows * D * ef,
            bytes_accessed=8 * groups * rows * D + 6 * D * ef,
            transcendentals=0,
        ),
        name="experts",
    )(expert.reshape(1), *weights, *blocks)
    return [(results[2 * g], results[2 * g + 1]) for g in range(groups)]


def body(
    hidden_in, query, keyval, out_proj, norm_gain, expert_ids, gate_weights, w_gate, w_up, w_down
):
    n_ctx = lax.axis_size("ctx")
    n_exp = lax.axis_size("exp")
    position = lax.axis_index("ctx")
    rows = hidden_in.shape[1]
    proj_rows = out_proj.shape[0]
    wide = D // n_ctx
    columns = lax.all_gather(
        lax.dynamic_slice_in_dim(out_proj, position * wide, wide, axis=1),
        "exp",
        axis=0,
        tiled=True,
        axis_index_groups=core_rings(n_exp),
    )

    def times_columns(block):
        return jnp.dot(block, columns, preferred_element_type=jnp.float32)

    core = lax.axis_index("exp") % 2
    blocks = [keyval[0]] + [rotate(keyval[0], "ctx", back) for back in range(1, n_ctx)]
    attended = attend(position, core, query[0], blocks, n_exp, proj_rows)
    own_heads, other_heads = attended[0], attended[1]
    sibling_heads = swap_cores(other_heads)
    projected = []
    for back in range(n_ctx):
        heads = [rotate(own_heads, "ctx", back), rotate(sibling_heads, "ctx", back)]
        from_sibling = swap_cores(times_columns(heads[1]).astype(jnp.bfloat16))
        part = times_columns(heads[0]) + from_sibling.astype(jnp.float32)
        if back:
            part = rotate(part.astype(jnp.bfloat16), "ctx", -back)
        projected.append(part)

    local_experts = w_gate.shape[0]
    experts_all = n_exp * local_experts
    extra = -(-TERMS * experts_all // LANES) * LANES
    residual, tokens = pl.pallas_call(
        functools.partial(norm_kernel, experts_all),
        out_shape=(
            jax.ShapeDtypeStruct((rows, D), jnp.float32),
            jax.ShapeDtypeStruct((rows, D + extra), jnp.bfloat16),
        ),
        in_specs=[smem()] + [vmem()] * (4 + n_ctx),
        out_specs=(vmem(), vmem()),
        compiler_params=pltpu.CompilerParams(vmem_limit_bytes=16 * 1024 * 1024),
        name="norm",
    )(
        position.reshape(1),
        hidden_in[0],
        *projected,
        norm_gain.reshape(1, D),
        expert_ids[0],
        gate_weights[0],
    )

    n_chip = n_exp // 2
    far = n_chip // 2
    half_rows = rows // 2
    sums = {}

    def experts_on(chips):
        offsets = [offset for offset, _, _ in chips]
        total = None
        for local in range(local_experts):
            expert = lax.axis_index("exp") * local_experts + local
            weights = (w_gate[local], w_up[local], w_down[local])
            pairs = run_expert(
                experts_all, expert, [(own, other) for _, own, other in chips], weights
            )
            total = pairs if total is None else jax.tree.map(jnp.add, total, pairs)
        for offset, (own, other) in zip(offsets, total):
            sums[offset] = [own, swap_cores(other)]
        return total

    def send_on(forward, backward, step):
        if step < far:
            return round_ring(forward, 1), round_ring(backward, -1)
        return round_ring(forward[:half_rows], 1), round_ring(backward[half_rows:], -1)

    def total_of(terms, half):
        at = slice(half * half_rows, (half + 1) * half_rows)
        terms = [term if term.shape[0] == half_rows else term[at] for term in terms]
        return functools.reduce(jnp.add, [term.astype(jnp.float32) for term in terms])

    def after(blocks, results):
        return lax.optimization_barrier((blocks, results))[0]

    forward, backward = send_on(tokens, tokens, 1)
    results = experts_on([(0, [tokens], [swap_cores(tokens)])])
    forward, backward = after((forward, backward), results)
    for step in range(1, far):
        earlier = list(sums.values())
        chips = [
            (n_chip - step, [forward], [swap_cores(forward)]),
            (step, [backward], [swap_cores(backward)]),
        ]
        forward, backward = send_on(forward, backward, step + 1)
        results = experts_on(chips)
        forward, backward = after((forward, backward), (results, earlier))

    def total_at(direction, half, hop, carried):
        offset = hop if direction > 0 else n_chip - hop
        return total_of(sums[offset] + carried, half).astype(jnp.bfloat16)

    halves = [forward, backward]
    swapped = [swap_cores(half) for half in halves]
    ahead = [total_at(1, 1, far - 1, []), total_at(-1, 0, far - 1, [])]
    halves, swapped, ahead = lax.optimization_barrier((halves, swapped, ahead))
    ahead = [round_ring(ahead[0], 1), round_ring(ahead[1], -1)]
    experts_on([(far, halves, swapped)])

    def running_sum(direction, half, hops, carried):
        for hop in range(hops, 0, -1):
            carried = [round_ring(total_at(direction, half, hop, carried), direction)]
        return carried

    arrived = [
        running_sum(1, 0, far, []) + running_sum(-1, 0, far - 2, ahead[1:]),
        running_sum(1, 1, far - 2, ahead[:1]) + running_sum(-1, 1, far, []),
    ]
    result = [
        total_of([residual] + sums[0] + arrived[half], half).astype(jnp.bfloat16)
        for half in range(2)
    ]
    return jnp.concatenate(result, axis=0)[None]


def solution(mesh):
    in_specs = (
        P("exp", "ctx", None),
        P("exp", "ctx", None),
        P("exp", "ctx", None),
        P("exp", None),
        P(),
        P("exp", "ctx", None),
        P("exp", "ctx", None),
        P("exp", None, None),
        P("exp", None, None),
        P("exp", None, None),
    )
    out_specs = P("exp", "ctx", None)
    return jax.shard_map(body, mesh=mesh, in_specs=in_specs, out_specs=out_specs, check_vma=False)
```

```python
import functools

import jax
import jax.numpy as jnp
from jax import lax
from jax.experimental import pallas as pl
from jax.experimental.pallas import tpu as pltpu
from jax.sharding import PartitionSpec as P

D = 2048
QH = 32
KVH = 2
HD = 128
TOP = 8
LANES = 128
TERMS = 3


def chip_ring(n):
    chips = n // 2
    return list(range(0, chips, 2)) + list(range(1, chips, 2))[::-1]


def device_ring(n):
    return [2 * chip + core for chip in chip_ring(n) for core in range(2)]


def core_rings(n):
    return [[2 * chip + core for chip in chip_ring(n)] for core in range(2)]


def swap_cores(block):
    n = lax.axis_size("exp")
    return lax.ppermute(block, "exp", [(i, i ^ 1) for i in range(n)])


def round_ring(block, direction):
    n = lax.axis_size("exp")
    route = []
    for ring in core_rings(n):
        route += [(ring[i], ring[(i + direction) % len(ring)]) for i in range(len(ring))]
    return lax.ppermute(block, "exp", route)


def rotate(block, axis, distance):
    if distance == 0:
        return block
    n = lax.axis_size(axis)
    return lax.ppermute(block, axis, [(i, (i + distance) % n) for i in range(n)])


def attention_kernel(places, pos_ref, query_ref, *refs):
    *kv_refs, out_ref = refs
    n_ctx = len(kv_refs)
    position = pos_ref[0]
    rows = query_ref.shape[0]
    row = lax.broadcasted_iota(jnp.int32, (rows, rows), 0)
    col = lax.broadcasted_iota(jnp.int32, (rows, rows), 1)
    visible = [row >= col]
    for back in range(1, n_ctx):
        visible.append(jnp.full((rows, rows), position, jnp.int32) >= back)
    visible = jnp.concatenate(visible, axis=1)
    for kv_head in range(KVH):
        k_at = kv_head * HD
        v_at = (KVH + kv_head) * HD
        keys = jnp.concatenate([ref[:, k_at : k_at + HD] for ref in kv_refs], axis=0)
        values = jnp.concatenate([ref[:, v_at : v_at + HD] for ref in kv_refs], axis=0)
        for group in range(QH // KVH):
            head = kv_head * (QH // KVH) + group
            scores = lax.dot_general(
                query_ref[:, head * HD : (head + 1) * HD],
                keys,
                (((1,), (1,)), ((), ())),
                preferred_element_type=jnp.float32,
            ) * HD ** (-0.5)
            scores = jnp.where(visible, scores, -1e30)
            weights = jnp.exp(scores - jnp.max(scores, axis=1, keepdims=True))
            row_sum = jnp.sum(weights, axis=1, keepdims=True)
            mixed = jnp.dot(
                weights.astype(jnp.bfloat16), values, preferred_element_type=jnp.float32
            )
            core, at = places[head]
            slot = lax.rem(core + pos_ref[1], 2)
            out_ref[slot, :, at : at + HD] = (mixed / row_sum).astype(jnp.bfloat16)


def norm_kernel(experts_all, pos_ref, hidden_ref, *refs):
    *projected_refs, gain_ref, ids_ref, gates_ref, residual_ref, tokens_ref = refs
    n_ctx = len(projected_refs)
    wide = D // n_ctx
    square_sum = None
    for back, ref in enumerate(projected_refs):
        at = pl.ds(pl.multiple_of(lax.rem(pos_ref[0] + back, n_ctx) * wide, wide), wide)
        part = hidden_ref[:, at].astype(jnp.float32) + ref[...].astype(jnp.float32)
        residual_ref[:, at] = part
        squares = jnp.sum(part * part, axis=1, keepdims=True)
        square_sum = squares if square_sum is None else square_sum + squares
    scale_inv = lax.rsqrt(square_sum * (1.0 / D) + 1e-06)
    normed = residual_ref[...] * scale_inv * gain_ref[...].astype(jnp.float32)
    tokens_ref[:, :D] = normed.astype(jnp.bfloat16)
    shape = (tokens_ref.shape[0], tokens_ref.shape[1] - D)
    column = lax.broadcasted_iota(jnp.int32, shape, 1)
    expert = lax.rem(column, experts_all)
    gates = jnp.zeros(shape, jnp.float32)
    for k in range(TOP):
        gates = gates + jnp.where(ids_ref[:, k : k + 1] == expert, gates_ref[:, k : k + 1], 0.0)
    terms = jnp.zeros(shape, jnp.float32)
    for term in range(TERMS):
        rounded = gates.astype(jnp.bfloat16).astype(jnp.float32)
        terms = jnp.where(column // experts_all == term, rounded, terms)
        gates = gates - rounded
    tokens_ref[:, D:] = terms.astype(jnp.bfloat16)


def expert_kernel(experts_all, groups, parts, expert_ref, *refs):
    gate_ref, up_ref, down_ref, *refs = refs
    block_refs, out_refs = refs[: 2 * groups * parts], refs[2 * groups * parts :]
    blocks = jnp.concatenate([ref[...] for ref in block_refs], axis=0)
    terms = blocks[:, D:].astype(jnp.float32)
    column = lax.broadcasted_iota(jnp.int32, terms.shape, 1)
    mine = (lax.rem(column, experts_all) == expert_ref[0]) & (column < TERMS * experts_all)
    gates = jnp.sum(jnp.where(mine, terms, 0.0), axis=1, keepdims=True)
    tokens = blocks[:, :D]
    gate_pre = jnp.dot(tokens, gate_ref[...], preferred_element_type=jnp.float32)
    up_pre = jnp.dot(tokens, up_ref[...], preferred_element_type=jnp.float32)
    activated = (gate_pre / (1.0 + jnp.exp(-gate_pre)) * up_pre).astype(jnp.bfloat16)
    expert_out = jnp.dot(activated, down_ref[...], preferred_element_type=jnp.float32)
    weighted = jnp.where(gates > 0.0, expert_out * gates, 0.0).astype(jnp.bfloat16)
    rows = out_refs[0].shape[0]
    for i, ref in enumerate(out_refs):
        ref[...] = weighted[i * rows : (i + 1) * rows]


def vmem():
    return pl.BlockSpec(memory_space=pltpu.VMEM)


def smem():
    return pl.BlockSpec(memory_space=pltpu.SMEM)


def attend(position, core, queries, blocks, n_exp, proj_rows):
    rows = queries.shape[0]
    rings = core_rings(n_exp)
    places = {}
    for head in range(QH):
        device, inside = divmod(head * HD, proj_rows)
        places[head] = (device % 2, rings[device % 2].index(device) * proj_rows + inside)
    return pl.pallas_call(
        functools.partial(attention_kernel, places),
        out_shape=jax.ShapeDtypeStruct((2, rows, QH * HD // 2), jnp.bfloat16),
        in_specs=[smem()] + [vmem()] * (1 + len(blocks)),
        out_specs=vmem(),
        compiler_params=pltpu.CompilerParams(vmem_limit_bytes=16 * 1024 * 1024),
        name="attention",
    )(jnp.stack([position, core]), queries, *blocks)


def run_expert(experts_all, expert, chips, weights):
    groups, parts = len(chips), len(chips[0][0])
    blocks = [block for own, other in chips for block in own + other]
    rows = sum(block.shape[0] for block in blocks) // (2 * groups)
    ef = weights[0].shape[1]
    results = pl.pallas_call(
        functools.partial(expert_kernel, experts_all, groups, parts),
        out_shape=[jax.ShapeDtypeStruct((rows, D), jnp.bfloat16)] * (2 * groups),
        in_specs=[smem()] + [vmem()] * (3 + len(blocks)),
        out_specs=[vmem()] * (2 * groups),
        compiler_params=pltpu.CompilerParams(vmem_limit_bytes=38 * 1024 * 1024),
        cost_estimate=pl.CostEstimate(
            flops=12 * groups * rows * D * ef,
            bytes_accessed=8 * groups * rows * D + 6 * D * ef,
            transcendentals=0,
        ),
        name="experts",
    )(expert.reshape(1), *weights, *blocks)
    return [(results[2 * g], results[2 * g + 1]) for g in range(groups)]


def body(
    hidden_in, query, keyval, out_proj, norm_gain, expert_ids, gate_weights, w_gate, w_up, w_down
):
    n_ctx = lax.axis_size("ctx")
    n_exp = lax.axis_size("exp")
    position = lax.axis_index("ctx")
    rows = hidden_in.shape[1]
    proj_rows = out_proj.shape[0]
    wide = D // n_ctx
    columns = lax.all_gather(
        lax.dynamic_slice_in_dim(out_proj, position * wide, wide, axis=1),
        "exp",
        axis=0,
        tiled=True,
        axis_index_groups=core_rings(n_exp),
    )

    def times_columns(block):
        return jnp.dot(block, columns, preferred_element_type=jnp.float32)

    core = lax.axis_index("exp") % 2
    blocks = [keyval[0]] + [rotate(keyval[0], "ctx", back) for back in range(1, n_ctx)]
    attended = attend(position, core, query[0], blocks, n_exp, proj_rows)
    own_heads, other_heads = attended[0], attended[1]
    sibling_heads = swap_cores(other_heads)
    projected = []
    for back in range(n_ctx):
        heads = [rotate(own_heads, "ctx", back), rotate(sibling_heads, "ctx", back)]
        from_sibling = swap_cores(times_columns(heads[1]).astype(jnp.bfloat16))
        part = times_columns(heads[0]) + from_sibling.astype(jnp.float32)
        if back:
            part = rotate(part.astype(jnp.bfloat16), "ctx", -back)
        projected.append(part)

    local_experts = w_gate.shape[0]
    experts_all = n_exp * local_experts
    extra = -(-TERMS * experts_all // LANES) * LANES
    residual, tokens = pl.pallas_call(
        functools.partial(norm_kernel, experts_all),
        out_shape=(
            jax.ShapeDtypeStruct((rows, D), jnp.float32),
            jax.ShapeDtypeStruct((rows, D + extra), jnp.bfloat16),
        ),
        in_specs=[smem()] + [vmem()] * (4 + n_ctx),
        out_specs=(vmem(), vmem()),
        compiler_params=pltpu.CompilerParams(vmem_limit_bytes=16 * 1024 * 1024),
        name="norm",
    )(
        position.reshape(1),
        hidden_in[0],
        *projected,
        norm_gain.reshape(1, D),
        expert_ids[0],
        gate_weights[0],
    )

    n_chip = n_exp // 2
    far = n_chip // 2
    half_rows = rows // 2
    sums = {}

    def experts_on(chips):
        offsets = [offset for offset, _, _ in chips]
        total = None
        for local in range(local_experts):
            expert = lax.axis_index("exp") * local_experts + local
            weights = (w_gate[local], w_up[local], w_down[local])
            pairs = run_expert(
                experts_all, expert, [(own, other) for _, own, other in chips], weights
            )
            total = pairs if total is None else jax.tree.map(jnp.add, total, pairs)
        return dict(zip(offsets, total))

    def swap_results(results):
        return {offset: [own, swap_cores(other)] for offset, (own, other) in results.items()}

    def send_on(forward, backward, step):
        if step < far:
            return round_ring(forward, 1), round_ring(backward, -1)
        return round_ring(forward[:half_rows], 1), round_ring(backward[half_rows:], -1)

    def total_of(terms, half):
        at = slice(half * half_rows, (half + 1) * half_rows)
        terms = [term if term.shape[0] == half_rows else term[at] for term in terms]
        return functools.reduce(jnp.add, [term.astype(jnp.float32) for term in terms])

    barrier = lax.optimization_barrier
    forward, backward = send_on(tokens, tokens, 1)
    results = experts_on([(0, [tokens], [swap_cores(tokens)])])
    forward, backward, results = barrier((forward, backward, results))
    for step in range(1, far):
        chips = [
            (n_chip - step, [forward], [swap_cores(forward)]),
            (step, [backward], [swap_cores(backward)]),
        ]
        forward, backward = send_on(forward, backward, step + 1)
        sums |= swap_results(results)
        results = experts_on(chips)
        forward, backward, results, sums = barrier((forward, backward, results, sums))
    halves = [forward, backward]
    swapped = [swap_cores(half) for half in halves]
    sums |= swap_results(results)
    halves, swapped, sums = barrier((halves, swapped, sums))
    sums |= swap_results(experts_on([(far, halves, swapped)]))

    def total_at(direction, half, hop, carried):
        offset = hop if direction > 0 else n_chip - hop
        return total_of(sums[offset] + carried, half).astype(jnp.bfloat16)

    def running_sum(direction, half, hops):
        carried = []
        for hop in range(hops, 0, -1):
            carried = [round_ring(total_at(direction, half, hop, carried), direction)]
        return carried

    arrived = [
        running_sum(1, 0, far) + running_sum(-1, 0, far - 1),
        running_sum(1, 1, far - 1) + running_sum(-1, 1, far),
    ]
    result = [
        total_of([residual] + sums[0] + arrived[half], half).astype(jnp.bfloat16)
        for half in range(2)
    ]
    return jnp.concatenate(result, axis=0)[None]


def solution(mesh):
    in_specs = (
        P("exp", "ctx", None),
        P("exp", "ctx", None),
        P("exp", "ctx", None),
        P("exp", None),
        P(),
        P("exp", "ctx", None),
        P("exp", "ctx", None),
        P("exp", None, None),
        P("exp", None, None),
        P("exp", None, None),
    )
    out_specs = P("exp", "ctx", None)
    return jax.shard_map(body, mesh=mesh, in_specs=in_specs, out_specs=out_specs, check_vma=False)
```

```python
import functools

import jax
import jax.numpy as jnp
from jax import lax
from jax.experimental import pallas as pl
from jax.experimental.pallas import tpu as pltpu
from jax.sharding import PartitionSpec as P

D = 2048
QH = 32
KVH = 2
HD = 128
TOP = 8


def chip_ring(n):
    chips = n // 2
    return list(range(0, chips, 2)) + list(range(1, chips, 2))[::-1]


def device_ring(n):
    return [2 * chip + core for chip in chip_ring(n) for core in range(2)]


def core_rings(n):
    return [[2 * chip + core for chip in chip_ring(n)] for core in range(2)]


def swap_cores(block):
    n = lax.axis_size("exp")
    return lax.ppermute(block, "exp", [(i, i ^ 1) for i in range(n)])


def round_ring(block, direction):
    n = lax.axis_size("exp")
    route = []
    for ring in core_rings(n):
        route += [(ring[i], ring[(i + direction) % len(ring)]) for i in range(len(ring))]
    return lax.ppermute(block, "exp", route)


def rotate(block, axis, distance):
    if distance == 0:
        return block
    n = lax.axis_size(axis)
    return lax.ppermute(block, axis, [(i, (i + distance) % n) for i in range(n)])


def attention_kernel(places, pos_ref, query_ref, *refs):
    *kv_refs, out_ref = refs
    n_ctx = len(kv_refs)
    position = pos_ref[0]
    rows = query_ref.shape[0]
    row = lax.broadcasted_iota(jnp.int32, (rows, rows), 0)
    col = lax.broadcasted_iota(jnp.int32, (rows, rows), 1)
    visible = [row >= col]
    for back in range(1, n_ctx):
        visible.append(jnp.full((rows, rows), position, jnp.int32) >= back)
    visible = jnp.concatenate(visible, axis=1)
    for kv_head in range(KVH):
        k_at = kv_head * HD
        v_at = (KVH + kv_head) * HD
        keys = jnp.concatenate([ref[:, k_at : k_at + HD] for ref in kv_refs], axis=0)
        values = jnp.concatenate([ref[:, v_at : v_at + HD] for ref in kv_refs], axis=0)
        for group in range(QH // KVH):
            head = kv_head * (QH // KVH) + group
            scores = lax.dot_general(
                query_ref[:, head * HD : (head + 1) * HD],
                keys,
                (((1,), (1,)), ((), ())),
                preferred_element_type=jnp.float32,
            ) * HD ** (-0.5)
            scores = jnp.where(visible, scores, -1e30)
            weights = jnp.exp(scores - jnp.max(scores, axis=1, keepdims=True))
            row_sum = jnp.sum(weights, axis=1, keepdims=True)
            mixed = jnp.dot(
                weights.astype(jnp.bfloat16), values, preferred_element_type=jnp.float32
            )
            core, at = places[head]
            slot = lax.rem(core + pos_ref[1], 2)
            out_ref[slot, :, at : at + HD] = (mixed / row_sum).astype(jnp.bfloat16)


def columns_kernel(pos_ref, source_ref, target_ref):
    target_ref[...] = source_ref[...]


def norm_kernel(pos_ref, hidden_ref, *refs):
    *projected_refs, gain_ref, residual_ref, tokens_ref = refs
    n_ctx = len(projected_refs)
    wide = D // n_ctx
    square_sum = None
    for back, ref in enumerate(projected_refs):
        at = pl.ds(pl.multiple_of(lax.rem(pos_ref[0] + back, n_ctx) * wide, wide), wide)
        part = hidden_ref[:, at].astype(jnp.float32) + ref[...].astype(jnp.float32)
        residual_ref[:, at] = part
        squares = jnp.sum(part * part, axis=1, keepdims=True)
        square_sum = squares if square_sum is None else square_sum + squares
    scale_inv = lax.rsqrt(square_sum * (1.0 / D) + 1e-06)
    normed = residual_ref[...] * scale_inv * gain_ref[...].astype(jnp.float32)
    tokens_ref[...] = normed.astype(jnp.bfloat16)


def final_kernel(residual_ref, own_ref, sibling_ref, *refs):
    *arrived_refs, out_ref = refs
    rows = arrived_refs[0].shape[0]
    for half in range(2):
        at = pl.ds(half * rows, rows)
        total = residual_ref[at, :]
        for ref in (own_ref.at[at], sibling_ref.at[at], *arrived_refs[2 * half : 2 * half + 2]):
            total = total + ref[...].astype(jnp.float32)
        out_ref[0, at, :] = total.astype(jnp.bfloat16)


def expert_kernel(groups, parts, expert_ref, *refs):
    gate_ref, up_ref, down_ref, *refs = refs
    blocks, refs = refs[: 2 * groups * parts], refs[2 * groups * parts :]
    gate_refs, out_refs = refs[: 2 * groups], refs[2 * groups :]
    tokens = jnp.concatenate([ref[...] for ref in blocks], axis=0)
    gates = jnp.concatenate([ref[...] for ref in gate_refs], axis=0)
    column = lax.broadcasted_iota(jnp.int32, gates.shape, 1)
    gates = jnp.sum(jnp.where(column == expert_ref[0], gates, 0.0), axis=1, keepdims=True)
    gate_pre = jnp.dot(tokens, gate_ref[...], preferred_element_type=jnp.float32)
    up_pre = jnp.dot(tokens, up_ref[...], preferred_element_type=jnp.float32)
    activated = (gate_pre / (1.0 + jnp.exp(-gate_pre)) * up_pre).astype(jnp.bfloat16)
    expert_out = jnp.dot(activated, down_ref[...], preferred_element_type=jnp.float32)
    weighted = jnp.where(gates > 0.0, expert_out * gates, 0.0).astype(jnp.bfloat16)
    rows = out_refs[0].shape[0]
    for i, ref in enumerate(out_refs):
        ref[...] = weighted[i * rows : (i + 1) * rows]


def vmem():
    return pl.BlockSpec(memory_space=pltpu.VMEM)


def smem():
    return pl.BlockSpec(memory_space=pltpu.SMEM)


def attend(position, core, queries, blocks, n_exp, proj_rows):
    rows = queries.shape[0]
    rings = core_rings(n_exp)
    places = {}
    for head in range(QH):
        device, inside = divmod(head * HD, proj_rows)
        places[head] = (device % 2, rings[device % 2].index(device) * proj_rows + inside)
    return pl.pallas_call(
        functools.partial(attention_kernel, places),
        out_shape=jax.ShapeDtypeStruct((2, rows, QH * HD // 2), jnp.bfloat16),
        in_specs=[smem()] + [vmem()] * (1 + len(blocks)),
        out_specs=vmem(),
        compiler_params=pltpu.CompilerParams(vmem_limit_bytes=16 * 1024 * 1024),
        name="attention",
    )(jnp.stack([position, core]), queries, *blocks)


def own_columns(position, matrix, n_parts):
    rows, width = matrix.shape
    wide = width // n_parts
    return pl.pallas_call(
        columns_kernel,
        grid_spec=pltpu.PrefetchScalarGridSpec(
            num_scalar_prefetch=1,
            grid=(1,),
            in_specs=[pl.BlockSpec((rows, wide), lambda i, pos: (0, pos[0]))],
            out_specs=pl.BlockSpec((rows, wide), lambda i, pos: (0, 0)),
        ),
        out_shape=jax.ShapeDtypeStruct((rows, wide), matrix.dtype),
        compiler_params=pltpu.CompilerParams(vmem_limit_bytes=60 * 1024 * 1024),
        name="columns",
    )(position.reshape(1), matrix)


def run_expert(expert, chips, gates, weights):
    groups, parts = len(chips), len(chips[0][0])
    blocks = [block for own, other in chips for block in own + other]
    gates = [block for pair in gates for block in pair]
    rows = gates[0].shape[0]
    ef = weights[0].shape[1]
    results = pl.pallas_call(
        functools.partial(expert_kernel, groups, parts),
        out_shape=[jax.ShapeDtypeStruct((rows, D), jnp.bfloat16)] * (2 * groups),
        in_specs=[smem()] + [vmem()] * (3 + len(blocks) + len(gates)),
        out_specs=[vmem()] * (2 * groups),
        compiler_params=pltpu.CompilerParams(vmem_limit_bytes=38 * 1024 * 1024),
        cost_estimate=pl.CostEstimate(
            flops=12 * groups * rows * D * ef,
            bytes_accessed=8 * groups * rows * D + 6 * D * ef,
            transcendentals=0,
        ),
        name="experts",
    )(expert.reshape(1), *weights, *blocks, *gates)
    return [(results[2 * g], results[2 * g + 1]) for g in range(groups)]


def body(
    hidden_in, query, keyval, out_proj, norm_gain, expert_ids, gate_weights, w_gate, w_up, w_down
):
    n_ctx = lax.axis_size("ctx")
    n_exp = lax.axis_size("exp")
    position = lax.axis_index("ctx")
    rows = hidden_in.shape[1]
    proj_rows = out_proj.shape[0]
    columns = lax.all_gather(
        own_columns(position, out_proj, n_ctx),
        "exp",
        axis=0,
        tiled=True,
        axis_index_groups=core_rings(n_exp),
    )

    def times_columns(block):
        return jnp.dot(block, columns, preferred_element_type=jnp.float32)

    core = lax.axis_index("exp") % 2
    blocks = [keyval[0]] + [rotate(keyval[0], "ctx", back) for back in range(1, n_ctx)]
    attended = attend(position, core, query[0], blocks, n_exp, proj_rows)
    own_heads, other_heads = attended[0], attended[1]

    local_experts = w_gate.shape[0]
    experts = jnp.arange(n_exp * local_experts, dtype=jnp.int32)
    named = expert_ids[0][:, :, None] == experts[None, None, :]
    gates = jnp.sum(jnp.where(named, gate_weights[0][:, :, None], 0.0), axis=1)
    n_chip = n_exp // 2
    far = n_chip // 2
    gates_at = {0: gates}
    forward, backward = gates, gates
    for step in range(1, far + 1):
        forward, backward = round_ring(forward, 1), round_ring(backward, -1)
        gates_at |= {n_chip - step: forward} if step == far else {n_chip - step: forward, step: backward}
    gates_at = {offset: (block, swap_cores(block)) for offset, block in gates_at.items()}
    own_heads, other_heads, gates_at = lax.optimization_barrier((own_heads, other_heads, gates_at))

    sibling_heads = swap_cores(other_heads)
    projected = []
    for back in range(n_ctx):
        heads = [rotate(own_heads, "ctx", back), rotate(sibling_heads, "ctx", back)]
        from_sibling = swap_cores(times_columns(heads[1]).astype(jnp.bfloat16))
        part = times_columns(heads[0]) + from_sibling.astype(jnp.float32)
        if back:
            part = rotate(part.astype(jnp.bfloat16), "ctx", -back)
        projected.append(part)

    residual, tokens = pl.pallas_call(
        norm_kernel,
        out_shape=(
            jax.ShapeDtypeStruct((rows, D), jnp.float32),
            jax.ShapeDtypeStruct((rows, D), jnp.bfloat16),
        ),
        in_specs=[smem()] + [vmem()] * (2 + n_ctx),
        out_specs=(vmem(), vmem()),
        compiler_params=pltpu.CompilerParams(vmem_limit_bytes=16 * 1024 * 1024),
        name="norm",
    )(position.reshape(1), hidden_in[0], *projected, norm_gain.reshape(1, D))

    half_rows = rows // 2
    sums = {}

    def experts_on(chips):
        offsets = [offset for offset, _, _ in chips]
        total = None
        for local in range(local_experts):
            expert = lax.axis_index("exp") * local_experts + local
            weights = (w_gate[local], w_up[local], w_down[local])
            pairs = run_expert(
                expert,
                [(own, other) for _, own, other in chips],
                [gates_at[offset] for offset in offsets],
                weights,
            )
            total = pairs if total is None else jax.tree.map(jnp.add, total, pairs)
        return dict(zip(offsets, total))

    def swap_results(results):
        return {offset: [own, swap_cores(other)] for offset, (own, other) in results.items()}

    def send_on(forward, backward, step):
        if step < far:
            return round_ring(forward, 1), round_ring(backward, -1)
        return round_ring(forward[:half_rows], 1), round_ring(backward[half_rows:], -1)

    def total_of(terms, half):
        at = slice(half * half_rows, (half + 1) * half_rows)
        terms = [term if term.shape[0] == half_rows else term[at] for term in terms]
        return functools.reduce(jnp.add, [term.astype(jnp.float32) for term in terms])

    barrier = lax.optimization_barrier
    forward, backward = send_on(tokens, tokens, 1)
    results = experts_on([(0, [tokens], [swap_cores(tokens)])])
    forward, backward, results = barrier((forward, backward, results))
    for step in range(1, far):
        ours = forward, backward
        swapped = swap_cores(forward), swap_cores(backward)
        forward, backward = send_on(forward, backward, step + 1)
        if step + 1 < far:
            swapped, results = barrier((swapped, results))
        sums |= swap_results(results)
        results = experts_on(
            [(n_chip - step, [ours[0]], [swapped[0]]), (step, [ours[1]], [swapped[1]])]
        )
        forward, backward, results, sums = barrier((forward, backward, results, sums))
    swapped = [swap_cores(forward), swap_cores(backward)]
    swapped, results = barrier((swapped, results))
    sums |= swap_results(results)
    results = experts_on([(far, [forward, backward], swapped)])
    results, sums = barrier((results, sums))
    sums |= swap_results(results)

    def total_at(direction, half, hop, carried):
        offset = hop if direction > 0 else n_chip - hop
        return total_of(sums[offset] + carried, half).astype(jnp.bfloat16)

    def running_sum(direction, half, hops):
        carried = []
        for hop in range(hops, 0, -1):
            carried = [round_ring(total_at(direction, half, hop, carried), direction)]
        return carried

    arrived = [
        running_sum(1, 0, far) + running_sum(-1, 0, far - 1),
        running_sum(1, 1, far - 1) + running_sum(-1, 1, far),
    ]
    return pl.pallas_call(
        final_kernel,
        out_shape=jax.ShapeDtypeStruct((1, rows, D), jnp.bfloat16),
        in_specs=[vmem()] * 7,
        out_specs=vmem(),
        compiler_params=pltpu.CompilerParams(vmem_limit_bytes=16 * 1024 * 1024),
        name="final",
    )(residual, *sums[0], *arrived[0], *arrived[1])


def solution(mesh):
    in_specs = (
        P("exp", "ctx", None),
        P("exp", "ctx", None),
        P("exp", "ctx", None),
        P("exp", None),
        P(),
        P("exp", "ctx", None),
        P("exp", "ctx", None),
        P("exp", None, None),
        P("exp", None, None),
        P("exp", None, None),
    )
    out_specs = P("exp", "ctx", None)
    return jax.shard_map(body, mesh=mesh, in_specs=in_specs, out_specs=out_specs, check_vma=False)
```

```python
import functools

import jax
import jax.numpy as jnp
from jax import lax
from jax.experimental import pallas as pl
from jax.experimental.pallas import tpu as pltpu
from jax.sharding import PartitionSpec as P

D = 2048
QH = 32
KVH = 2
HD = 128
TOP = 8
LANES = 128
TERMS = 3


def chip_ring(n):
    chips = n // 2
    return list(range(0, chips, 2)) + list(range(1, chips, 2))[::-1]


def device_ring(n):
    return [2 * chip + core for chip in chip_ring(n) for core in range(2)]


def core_rings(n):
    return [[2 * chip + core for chip in chip_ring(n)] for core in range(2)]


def swap_cores(block):
    n = lax.axis_size("exp")
    return lax.ppermute(block, "exp", [(i, i ^ 1) for i in range(n)])


def round_ring(block, direction):
    n = lax.axis_size("exp")
    route = []
    for ring in core_rings(n):
        route += [(ring[i], ring[(i + direction) % len(ring)]) for i in range(len(ring))]
    return lax.ppermute(block, "exp", route)


def rotate(block, axis, distance):
    if distance == 0:
        return block
    n = lax.axis_size(axis)
    return lax.ppermute(block, axis, [(i, (i + distance) % n) for i in range(n)])


def attention_kernel(places, pos_ref, query_ref, *refs):
    *kv_refs, out_ref = refs
    n_ctx = len(kv_refs)
    position = pos_ref[0]
    rows = query_ref.shape[0]
    row = lax.broadcasted_iota(jnp.int32, (rows, rows), 0)
    col = lax.broadcasted_iota(jnp.int32, (rows, rows), 1)
    visible = [row >= col]
    for back in range(1, n_ctx):
        visible.append(jnp.full((rows, rows), position, jnp.int32) >= back)
    visible = jnp.concatenate(visible, axis=1)
    for kv_head in range(KVH):
        k_at = kv_head * HD
        v_at = (KVH + kv_head) * HD
        keys = jnp.concatenate([ref[:, k_at : k_at + HD] for ref in kv_refs], axis=0)
        values = jnp.concatenate([ref[:, v_at : v_at + HD] for ref in kv_refs], axis=0)
        for group in range(QH // KVH):
            head = kv_head * (QH // KVH) + group
            scores = lax.dot_general(
                query_ref[:, head * HD : (head + 1) * HD],
                keys,
                (((1,), (1,)), ((), ())),
                preferred_element_type=jnp.float32,
            ) * HD ** (-0.5)
            scores = jnp.where(visible, scores, -1e30)
            weights = jnp.exp(scores - jnp.max(scores, axis=1, keepdims=True))
            row_sum = jnp.sum(weights, axis=1, keepdims=True)
            mixed = jnp.dot(
                weights.astype(jnp.bfloat16), values, preferred_element_type=jnp.float32
            )
            core, at = places[head]
            slot = lax.rem(core + pos_ref[1], 2)
            out_ref[slot, :, at : at + HD] = (mixed / row_sum).astype(jnp.bfloat16)


def norm_kernel(experts_all, pos_ref, hidden_ref, *refs):
    *projected_refs, gain_ref, ids_ref, gates_ref, residual_ref, tokens_ref = refs
    n_ctx = len(projected_refs)
    wide = D // n_ctx
    square_sum = None
    for back, ref in enumerate(projected_refs):
        at = pl.ds(pl.multiple_of(lax.rem(pos_ref[0] + back, n_ctx) * wide, wide), wide)
        part = hidden_ref[:, at].astype(jnp.float32) + ref[...].astype(jnp.float32)
        residual_ref[:, at] = part
        squares = jnp.sum(part * part, axis=1, keepdims=True)
        square_sum = squares if square_sum is None else square_sum + squares
    scale_inv = lax.rsqrt(square_sum * (1.0 / D) + 1e-06)
    normed = residual_ref[...] * scale_inv * gain_ref[...].astype(jnp.float32)
    tokens_ref[:, :D] = normed.astype(jnp.bfloat16)
    shape = (tokens_ref.shape[0], tokens_ref.shape[1] - D)
    column = lax.broadcasted_iota(jnp.int32, shape, 1)
    expert = lax.rem(column, experts_all)
    gates = jnp.zeros(shape, jnp.float32)
    for k in range(TOP):
        gates = gates + jnp.where(ids_ref[:, k : k + 1] == expert, gates_ref[:, k : k + 1], 0.0)
    terms = jnp.zeros(shape, jnp.float32)
    for term in range(TERMS):
        rounded = gates.astype(jnp.bfloat16).astype(jnp.float32)
        terms = jnp.where(column // experts_all == term, rounded, terms)
        gates = gates - rounded
    tokens_ref[:, D:] = terms.astype(jnp.bfloat16)


def final_kernel(residual_ref, own_ref, sibling_ref, *refs):
    *arrived_refs, out_ref = refs
    rows = arrived_refs[0].shape[0]
    for half in range(2):
        at = pl.ds(half * rows, rows)
        total = residual_ref[at, :]
        for ref in (own_ref.at[at], sibling_ref.at[at], *arrived_refs[2 * half : 2 * half + 2]):
            total = total + ref[...].astype(jnp.float32)
        out_ref[0, at, :] = total.astype(jnp.bfloat16)


def expert_kernel(experts_all, groups, parts, expert_ref, *refs):
    gate_ref, up_ref, down_ref, *refs = refs
    block_refs, out_refs = refs[: 2 * groups * parts], refs[2 * groups * parts :]
    blocks = jnp.concatenate([ref[...] for ref in block_refs], axis=0)
    terms = blocks[:, D:].astype(jnp.float32)
    column = lax.broadcasted_iota(jnp.int32, terms.shape, 1)
    mine = (lax.rem(column, experts_all) == expert_ref[0]) & (column < TERMS * experts_all)
    gates = jnp.sum(jnp.where(mine, terms, 0.0), axis=1, keepdims=True)
    tokens = blocks[:, :D]
    gate_pre = jnp.dot(tokens, gate_ref[...], preferred_element_type=jnp.float32)
    up_pre = jnp.dot(tokens, up_ref[...], preferred_element_type=jnp.float32)
    activated = (gate_pre / (1.0 + jnp.exp(-gate_pre)) * up_pre).astype(jnp.bfloat16)
    expert_out = jnp.dot(activated, down_ref[...], preferred_element_type=jnp.float32)
    weighted = jnp.where(gates > 0.0, expert_out * gates, 0.0).astype(jnp.bfloat16)
    rows = out_refs[0].shape[0]
    for i, ref in enumerate(out_refs):
        ref[...] = weighted[i * rows : (i + 1) * rows]


def vmem():
    return pl.BlockSpec(memory_space=pltpu.VMEM)


def smem():
    return pl.BlockSpec(memory_space=pltpu.SMEM)


def attend(position, core, queries, blocks, n_exp, proj_rows):
    rows = queries.shape[0]
    rings = core_rings(n_exp)
    places = {}
    for head in range(QH):
        device, inside = divmod(head * HD, proj_rows)
        places[head] = (device % 2, rings[device % 2].index(device) * proj_rows + inside)
    return pl.pallas_call(
        functools.partial(attention_kernel, places),
        out_shape=jax.ShapeDtypeStruct((2, rows, QH * HD // 2), jnp.bfloat16),
        in_specs=[smem()] + [vmem()] * (1 + len(blocks)),
        out_specs=vmem(),
        compiler_params=pltpu.CompilerParams(vmem_limit_bytes=16 * 1024 * 1024),
        name="attention",
    )(jnp.stack([position, core]), queries, *blocks)


def run_expert(experts_all, expert, chips, weights):
    groups, parts = len(chips), len(chips[0][0])
    blocks = [block for own, other in chips for block in own + other]
    rows = sum(block.shape[0] for block in blocks) // (2 * groups)
    ef = weights[0].shape[1]
    results = pl.pallas_call(
        functools.partial(expert_kernel, experts_all, groups, parts),
        out_shape=[jax.ShapeDtypeStruct((rows, D), jnp.bfloat16)] * (2 * groups),
        in_specs=[smem()] + [vmem()] * (3 + len(blocks)),
        out_specs=[vmem()] * (2 * groups),
        compiler_params=pltpu.CompilerParams(vmem_limit_bytes=38 * 1024 * 1024),
        cost_estimate=pl.CostEstimate(
            flops=12 * groups * rows * D * ef,
            bytes_accessed=8 * groups * rows * D + 6 * D * ef,
            transcendentals=0,
        ),
        name="experts",
    )(expert.reshape(1), *weights, *blocks)
    return [(results[2 * g], results[2 * g + 1]) for g in range(groups)]


def body(
    hidden_in, query, keyval, out_proj, norm_gain, expert_ids, gate_weights, w_gate, w_up, w_down
):
    n_ctx = lax.axis_size("ctx")
    n_exp = lax.axis_size("exp")
    position = lax.axis_index("ctx")
    rows = hidden_in.shape[1]
    proj_rows = out_proj.shape[0]
    wide = D // n_ctx
    columns = lax.all_gather(
        lax.dynamic_slice_in_dim(out_proj, position * wide, wide, axis=1),
        "exp",
        axis=0,
        tiled=True,
        axis_index_groups=core_rings(n_exp),
    )

    def times_columns(block):
        return jnp.dot(block, columns, preferred_element_type=jnp.float32)

    core = lax.axis_index("exp") % 2
    blocks = [keyval[0]] + [rotate(keyval[0], "ctx", back) for back in range(1, n_ctx)]
    attended = attend(position, core, query[0], blocks, n_exp, proj_rows)
    own_heads, other_heads = attended[0], attended[1]
    sibling_heads = swap_cores(other_heads)
    projected = []
    for back in list(range(1, n_ctx)) + [0]:
        heads = [rotate(own_heads, "ctx", back), rotate(sibling_heads, "ctx", back)]
        from_sibling = swap_cores(times_columns(heads[1]).astype(jnp.bfloat16))
        part = lax.optimization_barrier(times_columns(heads[0]))
        part = part + from_sibling.astype(jnp.float32)
        if back:
            part = rotate(part.astype(jnp.bfloat16), "ctx", -back)
        projected.append(part)
    projected = projected[-1:] + projected[:-1]

    local_experts = w_gate.shape[0]
    experts_all = n_exp * local_experts
    extra = -(-TERMS * experts_all // LANES) * LANES
    residual, tokens = pl.pallas_call(
        functools.partial(norm_kernel, experts_all),
        out_shape=(
            jax.ShapeDtypeStruct((rows, D), jnp.float32),
            jax.ShapeDtypeStruct((rows, D + extra), jnp.bfloat16),
        ),
        in_specs=[smem()] + [vmem()] * (4 + n_ctx),
        out_specs=(vmem(), vmem()),
        compiler_params=pltpu.CompilerParams(vmem_limit_bytes=16 * 1024 * 1024),
        name="norm",
    )(
        position.reshape(1),
        hidden_in[0],
        *projected,
        norm_gain.reshape(1, D),
        expert_ids[0],
        gate_weights[0],
    )

    n_chip = n_exp // 2
    far = n_chip // 2
    half_rows = rows // 2
    sums = {}

    def experts_on(chips):
        offsets = [offset for offset, _, _ in chips]
        total = None
        for local in range(local_experts):
            expert = lax.axis_index("exp") * local_experts + local
            weights = (w_gate[local], w_up[local], w_down[local])
            pairs = run_expert(
                experts_all, expert, [(own, other) for _, own, other in chips], weights
            )
            total = pairs if total is None else jax.tree.map(jnp.add, total, pairs)
        return dict(zip(offsets, total))

    def swap_results(results):
        return {offset: [own, swap_cores(other)] for offset, (own, other) in results.items()}

    def send_on(forward, backward, step):
        if step < far:
            return round_ring(forward, 1), round_ring(backward, -1)
        return round_ring(forward[:half_rows], 1), round_ring(backward[half_rows:], -1)

    def total_of(terms, half):
        at = slice(half * half_rows, (half + 1) * half_rows)
        terms = [term if term.shape[0] == half_rows else term[at] for term in terms]
        return functools.reduce(jnp.add, [term.astype(jnp.float32) for term in terms])

    barrier = lax.optimization_barrier
    forward, backward = send_on(tokens, tokens, 1)
    results = experts_on([(0, [tokens], [swap_cores(tokens)])])
    forward, backward, results = barrier((forward, backward, results))
    for step in range(1, far):
        ours = forward, backward
        swapped = swap_cores(forward), swap_cores(backward)
        forward, backward = send_on(forward, backward, step + 1)
        if step + 1 < far:
            swapped, results = barrier((swapped, results))
        sums |= swap_results(results)
        results = experts_on(
            [(n_chip - step, [ours[0]], [swapped[0]]), (step, [ours[1]], [swapped[1]])]
        )
        forward, backward, results, sums = barrier((forward, backward, results, sums))
    swapped = [swap_cores(forward), swap_cores(backward)]
    swapped, results = barrier((swapped, results))
    sums |= swap_results(results)
    results = experts_on([(far, [forward, backward], swapped)])
    results, sums = barrier((results, sums))
    sums |= swap_results(results)

    def total_at(direction, half, hop, carried):
        offset = hop if direction > 0 else n_chip - hop
        return total_of(sums[offset] + carried, half).astype(jnp.bfloat16)

    def running_sum(direction, half, hops):
        carried = []
        for hop in range(hops, 0, -1):
            carried = [round_ring(total_at(direction, half, hop, carried), direction)]
        return carried

    arrived = [
        running_sum(1, 0, far) + running_sum(-1, 0, far - 1),
        running_sum(1, 1, far - 1) + running_sum(-1, 1, far),
    ]
    return pl.pallas_call(
        final_kernel,
        out_shape=jax.ShapeDtypeStruct((1, rows, D), jnp.bfloat16),
        in_specs=[vmem()] * 7,
        out_specs=vmem(),
        compiler_params=pltpu.CompilerParams(vmem_limit_bytes=16 * 1024 * 1024),
        name="final",
    )(residual, *sums[0], *arrived[0], *arrived[1])


def solution(mesh):
    in_specs = (
        P("exp", "ctx", None),
        P("exp", "ctx", None),
        P("exp", "ctx", None),
        P("exp", None),
        P(),
        P("exp", "ctx", None),
        P("exp", "ctx", None),
        P("exp", None, None),
        P("exp", None, None),
        P("exp", None, None),
    )
    out_specs = P("exp", "ctx", None)
    return jax.shard_map(body, mesh=mesh, in_specs=in_specs, out_specs=out_specs, check_vma=False)
```

```python
import functools

import jax
import jax.numpy as jnp
from jax import lax
from jax.experimental import pallas as pl
from jax.experimental.pallas import tpu as pltpu
from jax.sharding import PartitionSpec as P

D = 2048
QH = 32
KVH = 2
HD = 128
TOP = 8
LANES = 128
TERMS = 3


def chip_ring(n):
    chips = n // 2
    return list(range(0, chips, 2)) + list(range(1, chips, 2))[::-1]


def device_ring(n):
    return [2 * chip + core for chip in chip_ring(n) for core in range(2)]


def core_rings(n):
    return [[2 * chip + core for chip in chip_ring(n)] for core in range(2)]


def swap_cores(block):
    n = lax.axis_size("exp")
    return lax.ppermute(block, "exp", [(i, i ^ 1) for i in range(n)])


def round_ring(block, direction):
    n = lax.axis_size("exp")
    route = []
    for ring in core_rings(n):
        route += [(ring[i], ring[(i + direction) % len(ring)]) for i in range(len(ring))]
    return lax.ppermute(block, "exp", route)


def rotate(block, axis, distance):
    if distance == 0:
        return block
    n = lax.axis_size(axis)
    return lax.ppermute(block, axis, [(i, (i + distance) % n) for i in range(n)])


def attention_kernel(places, pos_ref, query_ref, *refs):
    *kv_refs, out_ref = refs
    n_ctx = len(kv_refs)
    position = pos_ref[0]
    rows = query_ref.shape[0]
    row = lax.broadcasted_iota(jnp.int32, (rows, rows), 0)
    col = lax.broadcasted_iota(jnp.int32, (rows, rows), 1)
    visible = [row >= col]
    for back in range(1, n_ctx):
        visible.append(jnp.full((rows, rows), position, jnp.int32) >= back)
    visible = jnp.concatenate(visible, axis=1)
    for kv_head in range(KVH):
        k_at = kv_head * HD
        v_at = (KVH + kv_head) * HD
        keys = jnp.concatenate([ref[:, k_at : k_at + HD] for ref in kv_refs], axis=0)
        values = jnp.concatenate([ref[:, v_at : v_at + HD] for ref in kv_refs], axis=0)
        for group in range(QH // KVH):
            head = kv_head * (QH // KVH) + group
            scores = lax.dot_general(
                query_ref[:, head * HD : (head + 1) * HD],
                keys,
                (((1,), (1,)), ((), ())),
                preferred_element_type=jnp.float32,
            ) * HD ** (-0.5)
            scores = jnp.where(visible, scores, -1e30)
            weights = jnp.exp(scores - jnp.max(scores, axis=1, keepdims=True))
            row_sum = jnp.sum(weights, axis=1, keepdims=True)
            mixed = jnp.dot(
                weights.astype(jnp.bfloat16), values, preferred_element_type=jnp.float32
            )
            core, at = places[head]
            slot = lax.rem(core + pos_ref[1], 2)
            out_ref[slot, :, at : at + HD] = (mixed / row_sum).astype(jnp.bfloat16)


def columns_kernel(pos_ref, source_ref, target_ref):
    target_ref[...] = source_ref[...]


def norm_kernel(experts_all, pos_ref, hidden_ref, *refs):
    *projected_refs, gain_ref, ids_ref, gates_ref, residual_ref, tokens_ref = refs
    n_ctx = len(projected_refs)
    wide = D // n_ctx
    square_sum = None
    for back, ref in enumerate(projected_refs):
        at = pl.ds(pl.multiple_of(lax.rem(pos_ref[0] + back, n_ctx) * wide, wide), wide)
        part = hidden_ref[:, at].astype(jnp.float32) + ref[...].astype(jnp.float32)
        residual_ref[:, at] = part
        squares = jnp.sum(part * part, axis=1, keepdims=True)
        square_sum = squares if square_sum is None else square_sum + squares
    scale_inv = lax.rsqrt(square_sum * (1.0 / D) + 1e-06)
    normed = residual_ref[...] * scale_inv * gain_ref[...].astype(jnp.float32)
    tokens_ref[:, :D] = normed.astype(jnp.bfloat16)
    shape = (tokens_ref.shape[0], tokens_ref.shape[1] - D)
    column = lax.broadcasted_iota(jnp.int32, shape, 1)
    expert = lax.rem(column, experts_all)
    gates = jnp.zeros(shape, jnp.float32)
    for k in range(TOP):
        gates = gates + jnp.where(ids_ref[:, k : k + 1] == expert, gates_ref[:, k : k + 1], 0.0)
    terms = jnp.zeros(shape, jnp.float32)
    for term in range(TERMS):
        rounded = gates.astype(jnp.bfloat16).astype(jnp.float32)
        terms = jnp.where(column // experts_all == term, rounded, terms)
        gates = gates - rounded
    tokens_ref[:, D:] = terms.astype(jnp.bfloat16)


def final_kernel(residual_ref, own_ref, sibling_ref, *refs):
    *arrived_refs, out_ref = refs
    rows = arrived_refs[0].shape[0]
    for half in range(2):
        at = pl.ds(half * rows, rows)
        total = residual_ref[at, :]
        for ref in (own_ref.at[at], sibling_ref.at[at], *arrived_refs[2 * half : 2 * half + 2]):
            total = total + ref[...].astype(jnp.float32)
        out_ref[0, at, :] = total.astype(jnp.bfloat16)


def expert_kernel(experts_all, groups, parts, expert_ref, *refs):
    gate_ref, up_ref, down_ref, *refs = refs
    block_refs, out_refs = refs[: 2 * groups * parts], refs[2 * groups * parts :]
    blocks = jnp.concatenate([ref[...] for ref in block_refs], axis=0)
    terms = blocks[:, D:].astype(jnp.float32)
    column = lax.broadcasted_iota(jnp.int32, terms.shape, 1)
    mine = (lax.rem(column, experts_all) == expert_ref[0]) & (column < TERMS * experts_all)
    gates = jnp.sum(jnp.where(mine, terms, 0.0), axis=1, keepdims=True)
    tokens = blocks[:, :D]
    gate_pre = jnp.dot(tokens, gate_ref[...], preferred_element_type=jnp.float32)
    up_pre = jnp.dot(tokens, up_ref[...], preferred_element_type=jnp.float32)
    activated = (gate_pre / (1.0 + jnp.exp(-gate_pre)) * up_pre).astype(jnp.bfloat16)
    expert_out = jnp.dot(activated, down_ref[...], preferred_element_type=jnp.float32)
    weighted = jnp.where(gates > 0.0, expert_out * gates, 0.0).astype(jnp.bfloat16)
    rows = out_refs[0].shape[0]
    for i, ref in enumerate(out_refs):
        ref[...] = weighted[i * rows : (i + 1) * rows]


def vmem():
    return pl.BlockSpec(memory_space=pltpu.VMEM)


def smem():
    return pl.BlockSpec(memory_space=pltpu.SMEM)


def attend(position, core, queries, blocks, n_exp, proj_rows):
    rows = queries.shape[0]
    rings = core_rings(n_exp)
    places = {}
    for head in range(QH):
        device, inside = divmod(head * HD, proj_rows)
        places[head] = (device % 2, rings[device % 2].index(device) * proj_rows + inside)
    return pl.pallas_call(
        functools.partial(attention_kernel, places),
        out_shape=jax.ShapeDtypeStruct((2, rows, QH * HD // 2), jnp.bfloat16),
        in_specs=[smem()] + [vmem()] * (1 + len(blocks)),
        out_specs=vmem(),
        compiler_params=pltpu.CompilerParams(vmem_limit_bytes=16 * 1024 * 1024),
        name="attention",
    )(jnp.stack([position, core]), queries, *blocks)


def own_columns(position, matrix, n_parts):
    rows, width = matrix.shape
    wide, step = width // n_parts, rows // 4
    return pl.pallas_call(
        columns_kernel,
        grid_spec=pltpu.PrefetchScalarGridSpec(
            num_scalar_prefetch=1,
            grid=(4,),
            in_specs=[pl.BlockSpec((step, wide), lambda i, pos: (i, pos[0]))],
            out_specs=pl.BlockSpec((step, wide), lambda i, pos: (i, 0)),
        ),
        out_shape=jax.ShapeDtypeStruct((rows, wide), matrix.dtype),
        compiler_params=pltpu.CompilerParams(vmem_limit_bytes=60 * 1024 * 1024),
        name="columns",
    )(position.reshape(1), matrix)


def run_expert(experts_all, expert, chips, weights):
    groups, parts = len(chips), len(chips[0][0])
    blocks = [block for own, other in chips for block in own + other]
    rows = sum(block.shape[0] for block in blocks) // (2 * groups)
    ef = weights[0].shape[1]
    results = pl.pallas_call(
        functools.partial(expert_kernel, experts_all, groups, parts),
        out_shape=[jax.ShapeDtypeStruct((rows, D), jnp.bfloat16)] * (2 * groups),
        in_specs=[smem()] + [vmem()] * (3 + len(blocks)),
        out_specs=[vmem()] * (2 * groups),
        compiler_params=pltpu.CompilerParams(vmem_limit_bytes=38 * 1024 * 1024),
        cost_estimate=pl.CostEstimate(
            flops=12 * groups * rows * D * ef,
            bytes_accessed=8 * groups * rows * D + 6 * D * ef,
            transcendentals=0,
        ),
        name="experts",
    )(expert.reshape(1), *weights, *blocks)
    return [(results[2 * g], results[2 * g + 1]) for g in range(groups)]


def body(
    hidden_in, query, keyval, out_proj, norm_gain, expert_ids, gate_weights, w_gate, w_up, w_down
):
    n_ctx = lax.axis_size("ctx")
    n_exp = lax.axis_size("exp")
    position = lax.axis_index("ctx")
    rows = hidden_in.shape[1]
    proj_rows = out_proj.shape[0]
    columns = lax.all_gather(
        own_columns(position, out_proj, n_ctx),
        "exp",
        axis=0,
        tiled=True,
        axis_index_groups=core_rings(n_exp),
    )

    def times_columns(block):
        return jnp.dot(block, columns, preferred_element_type=jnp.float32)

    core = lax.axis_index("exp") % 2
    blocks = [keyval[0]] + [rotate(keyval[0], "ctx", back) for back in range(1, n_ctx)]
    attended = attend(position, core, query[0], blocks, n_exp, proj_rows)
    own_heads, other_heads = attended[0], attended[1]
    sibling_heads = swap_cores(other_heads)
    projected = []
    for back in range(n_ctx):
        heads = [rotate(own_heads, "ctx", back), rotate(sibling_heads, "ctx", back)]
        from_sibling = swap_cores(times_columns(heads[1]).astype(jnp.bfloat16))
        part = times_columns(heads[0]) + from_sibling.astype(jnp.float32)
        if back:
            part = rotate(part.astype(jnp.bfloat16), "ctx", -back)
        projected.append(part)

    local_experts = w_gate.shape[0]
    experts_all = n_exp * local_experts
    extra = -(-TERMS * experts_all // LANES) * LANES
    residual, tokens = pl.pallas_call(
        functools.partial(norm_kernel, experts_all),
        out_shape=(
            jax.ShapeDtypeStruct((rows, D), jnp.float32),
            jax.ShapeDtypeStruct((rows, D + extra), jnp.bfloat16),
        ),
        in_specs=[smem()] + [vmem()] * (4 + n_ctx),
        out_specs=(vmem(), vmem()),
        compiler_params=pltpu.CompilerParams(vmem_limit_bytes=16 * 1024 * 1024),
        name="norm",
    )(
        position.reshape(1),
        hidden_in[0],
        *projected,
        norm_gain.reshape(1, D),
        expert_ids[0],
        gate_weights[0],
    )

    n_chip = n_exp // 2
    far = n_chip // 2
    half_rows = rows // 2
    sums = {}

    def experts_on(chips):
        offsets = [offset for offset, _, _ in chips]
        total = None
        for local in range(local_experts):
            expert = lax.axis_index("exp") * local_experts + local
            weights = (w_gate[local], w_up[local], w_down[local])
            pairs = run_expert(
                experts_all, expert, [(own, other) for _, own, other in chips], weights
            )
            total = pairs if total is None else jax.tree.map(jnp.add, total, pairs)
        return dict(zip(offsets, total))

    def swap_results(results):
        return {offset: [own, swap_cores(other)] for offset, (own, other) in results.items()}

    def send_on(forward, backward, step):
        if step < far:
            return round_ring(forward, 1), round_ring(backward, -1)
        return round_ring(forward[:half_rows], 1), round_ring(backward[half_rows:], -1)

    def total_of(terms, half):
        at = slice(half * half_rows, (half + 1) * half_rows)
        terms = [term if term.shape[0] == half_rows else term[at] for term in terms]
        return functools.reduce(jnp.add, [term.astype(jnp.float32) for term in terms])

    barrier = lax.optimization_barrier
    forward, backward = send_on(tokens, tokens, 1)
    results = experts_on([(0, [tokens], [swap_cores(tokens)])])
    forward, backward, results = barrier((forward, backward, results))
    for step in range(1, far):
        ours = forward, backward
        swapped = swap_cores(forward), swap_cores(backward)
        forward, backward = send_on(forward, backward, step + 1)
        if step + 1 < far:
            swapped, results = barrier((swapped, results))
        sums |= swap_results(results)
        results = experts_on(
            [(n_chip - step, [ours[0]], [swapped[0]]), (step, [ours[1]], [swapped[1]])]
        )
        forward, backward, results, sums = barrier((forward, backward, results, sums))
    swapped = [swap_cores(forward), swap_cores(backward)]
    swapped, results = barrier((swapped, results))
    sums |= swap_results(results)
    results = experts_on([(far, [forward, backward], swapped)])
    results, sums = barrier((results, sums))
    sums |= swap_results(results)

    def total_at(direction, half, hop, carried):
        offset = hop if direction > 0 else n_chip - hop
        return total_of(sums[offset] + carried, half).astype(jnp.bfloat16)

    def running_sum(direction, half, hops):
        carried = []
        for hop in range(hops, 0, -1):
            carried = [round_ring(total_at(direction, half, hop, carried), direction)]
        return carried

    arrived = [
        running_sum(1, 0, far) + running_sum(-1, 0, far - 1),
        running_sum(1, 1, far - 1) + running_sum(-1, 1, far),
    ]
    return pl.pallas_call(
        final_kernel,
        out_shape=jax.ShapeDtypeStruct((1, rows, D), jnp.bfloat16),
        in_specs=[vmem()] * 7,
        out_specs=vmem(),
        compiler_params=pltpu.CompilerParams(vmem_limit_bytes=16 * 1024 * 1024),
        name="final",
    )(residual, *sums[0], *arrived[0], *arrived[1])


def solution(mesh):
    in_specs = (
        P("exp", "ctx", None),
        P("exp", "ctx", None),
        P("exp", "ctx", None),
        P("exp", None),
        P(),
        P("exp", "ctx", None),
        P("exp", "ctx", None),
        P("exp", None, None),
        P("exp", None, None),
        P("exp", None, None),
    )
    out_specs = P("exp", "ctx", None)
    return jax.shard_map(body, mesh=mesh, in_specs=in_specs, out_specs=out_specs, check_vma=False)
```

```python
import functools

import jax
import jax.numpy as jnp
from jax import lax
from jax.experimental import pallas as pl
from jax.experimental.pallas import tpu as pltpu
from jax.sharding import PartitionSpec as P

D = 2048
QH = 32
KVH = 2
HD = 128
TOP = 8
LANES = 128
TERMS = 3


def chip_ring(n):
    chips = n // 2
    return list(range(0, chips, 2)) + list(range(1, chips, 2))[::-1]


def device_ring(n):
    return [2 * chip + core for chip in chip_ring(n) for core in range(2)]


def core_rings(n):
    return [[2 * chip + core for chip in chip_ring(n)] for core in range(2)]


def swap_cores(block):
    n = lax.axis_size("exp")
    return lax.ppermute(block, "exp", [(i, i ^ 1) for i in range(n)])


def round_ring(block, direction):
    n = lax.axis_size("exp")
    route = []
    for ring in core_rings(n):
        route += [(ring[i], ring[(i + direction) % len(ring)]) for i in range(len(ring))]
    return lax.ppermute(block, "exp", route)


def rotate(block, axis, distance):
    if distance == 0:
        return block
    n = lax.axis_size(axis)
    return lax.ppermute(block, axis, [(i, (i + distance) % n) for i in range(n)])


def attention_kernel(places, pos_ref, query_ref, *refs):
    *kv_refs, out_ref = refs
    n_ctx = len(kv_refs)
    position = pos_ref[0]
    rows = query_ref.shape[0]
    row = lax.broadcasted_iota(jnp.int32, (rows, rows), 0)
    col = lax.broadcasted_iota(jnp.int32, (rows, rows), 1)
    visible = [row >= col]
    for back in range(1, n_ctx):
        visible.append(jnp.full((rows, rows), position, jnp.int32) >= back)
    visible = jnp.concatenate(visible, axis=1)
    for kv_head in range(KVH):
        k_at = kv_head * HD
        v_at = (KVH + kv_head) * HD
        keys = jnp.concatenate([ref[:, k_at : k_at + HD] for ref in kv_refs], axis=0)
        values = jnp.concatenate([ref[:, v_at : v_at + HD] for ref in kv_refs], axis=0)
        for group in range(QH // KVH):
            head = kv_head * (QH // KVH) + group
            scores = lax.dot_general(
                query_ref[:, head * HD : (head + 1) * HD],
                keys,
                (((1,), (1,)), ((), ())),
                preferred_element_type=jnp.float32,
            ) * HD ** (-0.5)
            scores = jnp.where(visible, scores, -1e30)
            weights = jnp.exp(scores - jnp.max(scores, axis=1, keepdims=True))
            row_sum = jnp.sum(weights, axis=1, keepdims=True)
            mixed = jnp.dot(
                weights.astype(jnp.bfloat16), values, preferred_element_type=jnp.float32
            )
            core, at = places[head]
            slot = lax.rem(core + pos_ref[1], 2)
            out_ref[slot, :, at : at + HD] = (mixed / row_sum).astype(jnp.bfloat16)


def norm_kernel(experts_all, pos_ref, hidden_ref, *refs):
    *projected_refs, gain_ref, ids_ref, gates_ref, residual_ref, tokens_ref = refs
    n_ctx = len(projected_refs)
    wide = D // n_ctx
    square_sum = None
    for back, ref in enumerate(projected_refs):
        at = pl.ds(pl.multiple_of(lax.rem(pos_ref[0] + back, n_ctx) * wide, wide), wide)
        part = hidden_ref[:, at].astype(jnp.float32) + ref[...].astype(jnp.float32)
        residual_ref[:, at] = part
        squares = jnp.sum(part * part, axis=1, keepdims=True)
        square_sum = squares if square_sum is None else square_sum + squares
    scale_inv = lax.rsqrt(square_sum * (1.0 / D) + 1e-06)
    normed = residual_ref[...] * scale_inv * gain_ref[...].astype(jnp.float32)
    tokens_ref[:, :D] = normed.astype(jnp.bfloat16)
    shape = (tokens_ref.shape[0], tokens_ref.shape[1] - D)
    column = lax.broadcasted_iota(jnp.int32, shape, 1)
    expert = lax.rem(column, experts_all)
    gates = jnp.zeros(shape, jnp.float32)
    for k in range(TOP):
        gates = gates + jnp.where(ids_ref[:, k : k + 1] == expert, gates_ref[:, k : k + 1], 0.0)
    terms = jnp.zeros(shape, jnp.float32)
    for term in range(TERMS):
        rounded = gates.astype(jnp.bfloat16).astype(jnp.float32)
        terms = jnp.where(column // experts_all == term, rounded, terms)
        gates = gates - rounded
    tokens_ref[:, D:] = terms.astype(jnp.bfloat16)


def final_kernel(residual_ref, own_ref, sibling_ref, *refs):
    *arrived_refs, out_ref = refs
    rows = arrived_refs[0].shape[0]
    for half in range(2):
        at = pl.ds(half * rows, rows)
        total = residual_ref[at, :]
        for ref in (own_ref.at[at], sibling_ref.at[at], *arrived_refs[2 * half : 2 * half + 2]):
            total = total + ref[...].astype(jnp.float32)
        out_ref[0, at, :] = total.astype(jnp.bfloat16)


def expert_kernel(experts_all, groups, parts, expert_ref, *refs):
    gate_ref, up_ref, down_ref, *refs = refs
    block_refs, out_refs = refs[: 2 * groups * parts], refs[2 * groups * parts :]
    blocks = jnp.concatenate([ref[...] for ref in block_refs], axis=0)
    terms = blocks[:, D:].astype(jnp.float32)
    column = lax.broadcasted_iota(jnp.int32, terms.shape, 1)
    mine = (lax.rem(column, experts_all) == expert_ref[0]) & (column < TERMS * experts_all)
    gates = jnp.sum(jnp.where(mine, terms, 0.0), axis=1, keepdims=True)
    tokens = blocks[:, :D]
    gate_pre = jnp.dot(tokens, gate_ref[...], preferred_element_type=jnp.float32)
    up_pre = jnp.dot(tokens, up_ref[...], preferred_element_type=jnp.float32)
    activated = (gate_pre / (1.0 + jnp.exp(-gate_pre)) * up_pre).astype(jnp.bfloat16)
    expert_out = jnp.dot(activated, down_ref[...], preferred_element_type=jnp.float32)
    weighted = jnp.where(gates > 0.0, expert_out * gates, 0.0).astype(jnp.bfloat16)
    rows = out_refs[0].shape[0]
    for i, ref in enumerate(out_refs):
        ref[...] = weighted[i * rows : (i + 1) * rows]


def vmem():
    return pl.BlockSpec(memory_space=pltpu.VMEM)


def smem():
    return pl.BlockSpec(memory_space=pltpu.SMEM)


def attend(position, core, queries, blocks, n_exp, proj_rows):
    rows = queries.shape[0]
    rings = core_rings(n_exp)
    places = {}
    for head in range(QH):
        device, inside = divmod(head * HD, proj_rows)
        places[head] = (device % 2, rings[device % 2].index(device) * proj_rows + inside)
    return pl.pallas_call(
        functools.partial(attention_kernel, places),
        out_shape=jax.ShapeDtypeStruct((2, rows, QH * HD // 2), jnp.bfloat16),
        in_specs=[smem()] + [vmem()] * (1 + len(blocks)),
        out_specs=vmem(),
        compiler_params=pltpu.CompilerParams(vmem_limit_bytes=16 * 1024 * 1024),
        name="attention",
    )(jnp.stack([position, core]), queries, *blocks)


def run_expert(experts_all, expert, chips, weights):
    groups, parts = len(chips), len(chips[0][0])
    blocks = [block for own, other in chips for block in own + other]
    rows = sum(block.shape[0] for block in blocks) // (2 * groups)
    ef = weights[0].shape[1]
    results = pl.pallas_call(
        functools.partial(expert_kernel, experts_all, groups, parts),
        out_shape=[jax.ShapeDtypeStruct((rows, D), jnp.bfloat16)] * (2 * groups),
        in_specs=[smem()] + [vmem()] * (3 + len(blocks)),
        out_specs=[vmem()] * (2 * groups),
        compiler_params=pltpu.CompilerParams(vmem_limit_bytes=38 * 1024 * 1024),
        cost_estimate=pl.CostEstimate(
            flops=12 * groups * rows * D * ef,
            bytes_accessed=8 * groups * rows * D + 6 * D * ef,
            transcendentals=0,
        ),
        name="experts",
    )(expert.reshape(1), *weights, *blocks)
    return [(results[2 * g], results[2 * g + 1]) for g in range(groups)]


def body(
    hidden_in, query, keyval, out_proj, norm_gain, expert_ids, gate_weights, w_gate, w_up, w_down
):
    n_ctx = lax.axis_size("ctx")
    n_exp = lax.axis_size("exp")
    position = lax.axis_index("ctx")
    rows = hidden_in.shape[1]
    proj_rows = out_proj.shape[0]
    wide = D // n_ctx
    columns = lax.all_gather(
        lax.dynamic_slice_in_dim(out_proj, position * wide, wide, axis=1),
        "exp",
        axis=0,
        tiled=True,
        axis_index_groups=core_rings(n_exp),
    )

    def times_columns(block):
        return jnp.dot(block, columns, preferred_element_type=jnp.float32)

    core = lax.axis_index("exp") % 2
    blocks = [keyval[0]] + [rotate(keyval[0], "ctx", back) for back in range(1, n_ctx)]
    attended = attend(position, core, query[0], blocks, n_exp, proj_rows)
    own_heads, other_heads = attended[0], attended[1]
    sibling_heads = swap_cores(other_heads)
    projected = []
    for back in range(n_ctx):
        heads = [rotate(own_heads, "ctx", back), rotate(sibling_heads, "ctx", back)]
        from_sibling = swap_cores(times_columns(heads[1]).astype(jnp.bfloat16))
        part = times_columns(heads[0]) + from_sibling.astype(jnp.float32)
        if back:
            part = rotate(part.astype(jnp.bfloat16), "ctx", -back)
        projected.append(part)

    local_experts = w_gate.shape[0]
    experts_all = n_exp * local_experts
    extra = -(-TERMS * experts_all // LANES) * LANES
    residual, tokens = pl.pallas_call(
        functools.partial(norm_kernel, experts_all),
        out_shape=(
            jax.ShapeDtypeStruct((rows, D), jnp.float32),
            jax.ShapeDtypeStruct((rows, D + extra), jnp.bfloat16),
        ),
        in_specs=[smem()] + [vmem()] * (4 + n_ctx),
        out_specs=(vmem(), vmem()),
        compiler_params=pltpu.CompilerParams(vmem_limit_bytes=16 * 1024 * 1024),
        name="norm",
    )(
        position.reshape(1),
        hidden_in[0],
        *projected,
        norm_gain.reshape(1, D),
        expert_ids[0],
        gate_weights[0],
    )

    n_chip = n_exp // 2
    far = n_chip // 2
    half_rows = rows // 2
    sums = {}

    def experts_on(chips):
        offsets = [offset for offset, _, _ in chips]
        total = None
        for local in range(local_experts):
            expert = lax.axis_index("exp") * local_experts + local
            weights = (w_gate[local], w_up[local], w_down[local])
            pairs = run_expert(
                experts_all, expert, [(own, other) for _, own, other in chips], weights
            )
            total = pairs if total is None else jax.tree.map(jnp.add, total, pairs)
        return dict(zip(offsets, total))

    def swap_results(results):
        return {offset: [own, swap_cores(other)] for offset, (own, other) in results.items()}

    def send_on(forward, backward, step):
        if step < far:
            return round_ring(forward, 1), round_ring(backward, -1)
        return round_ring(forward[:half_rows], 1), round_ring(backward[half_rows:], -1)

    def total_of(terms, half):
        at = slice(half * half_rows, (half + 1) * half_rows)
        terms = [term if term.shape[0] == half_rows else term[at] for term in terms]
        return functools.reduce(jnp.add, [term.astype(jnp.float32) for term in terms])

    barrier = lax.optimization_barrier
    forward, backward = send_on(tokens, tokens, 1)
    results = experts_on([(0, [tokens], [swap_cores(tokens)])])
    forward, backward, results = barrier((forward, backward, results))
    for step in range(1, far):
        ours = forward, backward
        swapped = swap_cores(forward), swap_cores(backward)
        forward, backward = send_on(forward, backward, step + 1)
        if step + 1 < far:
            swapped, results = barrier((swapped, results))
        sums |= swap_results(results)
        results = experts_on(
            [(n_chip - step, [ours[0]], [swapped[0]]), (step, [ours[1]], [swapped[1]])]
        )
        forward, backward, results, sums = barrier((forward, backward, results, sums))
    swapped = [swap_cores(forward), swap_cores(backward)]
    swapped, results = barrier((swapped, results))
    sums |= swap_results(results)
    results = experts_on([(far, [forward, backward], swapped)])
    results, sums = barrier((results, sums))
    sums |= swap_results(results)

    def running_sum(direction, half, hops, parts):
        carried = []
        for hop in range(hops, 0, -1):
            offset = hop if direction > 0 else n_chip - hop
            total = total_of(parts[offset] + carried, half).astype(jnp.bfloat16)
            carried = [round_ring(total, direction)]
        return carried

    apart = barrier(sums)
    arrived = [
        running_sum(1, 0, far, sums) + running_sum(-1, 0, far - 1, apart),
        running_sum(1, 1, far - 1, apart) + running_sum(-1, 1, far, sums),
    ]
    return pl.pallas_call(
        final_kernel,
        out_shape=jax.ShapeDtypeStruct((1, rows, D), jnp.bfloat16),
        in_specs=[vmem()] * 7,
        out_specs=vmem(),
        compiler_params=pltpu.CompilerParams(vmem_limit_bytes=16 * 1024 * 1024),
        name="final",
    )(residual, *sums[0], *arrived[0], *arrived[1])


def solution(mesh):
    in_specs = (
        P("exp", "ctx", None),
        P("exp", "ctx", None),
        P("exp", "ctx", None),
        P("exp", None),
        P(),
        P("exp", "ctx", None),
        P("exp", "ctx", None),
        P("exp", None, None),
        P("exp", None, None),
        P("exp", None, None),
    )
    out_specs = P("exp", "ctx", None)
    return jax.shard_map(body, mesh=mesh, in_specs=in_specs, out_specs=out_specs, check_vma=False)
```

```python
import functools

import jax
import jax.numpy as jnp
from jax import lax
from jax.experimental import pallas as pl
from jax.experimental.pallas import tpu as pltpu
from jax.sharding import PartitionSpec as P

D = 2048
QH = 32
KVH = 2
HD = 128
TOP = 8
LANES = 128
TERMS = 3


def chip_ring(n):
    chips = n // 2
    return list(range(0, chips, 2)) + list(range(1, chips, 2))[::-1]


def device_ring(n):
    return [2 * chip + core for chip in chip_ring(n) for core in range(2)]


def core_rings(n):
    return [[2 * chip + core for chip in chip_ring(n)] for core in range(2)]


def swap_cores(block):
    n = lax.axis_size("exp")
    return lax.ppermute(block, "exp", [(i, i ^ 1) for i in range(n)])


def round_ring(block, direction):
    n = lax.axis_size("exp")
    route = []
    for ring in core_rings(n):
        route += [(ring[i], ring[(i + direction) % len(ring)]) for i in range(len(ring))]
    return lax.ppermute(block, "exp", route)


def rotate(block, axis, distance):
    if distance == 0:
        return block
    n = lax.axis_size(axis)
    return lax.ppermute(block, axis, [(i, (i + distance) % n) for i in range(n)])


def attention_kernel(places, pos_ref, query_ref, *refs):
    *kv_refs, out_ref = refs
    n_ctx = len(kv_refs)
    position = pos_ref[0]
    rows = query_ref.shape[0]
    row = lax.broadcasted_iota(jnp.int32, (rows, rows), 0)
    col = lax.broadcasted_iota(jnp.int32, (rows, rows), 1)
    visible = [row >= col]
    for back in range(1, n_ctx):
        visible.append(jnp.full((rows, rows), position, jnp.int32) >= back)
    visible = jnp.concatenate(visible, axis=1)
    for kv_head in range(KVH):
        k_at = kv_head * HD
        v_at = (KVH + kv_head) * HD
        keys = jnp.concatenate([ref[:, k_at : k_at + HD] for ref in kv_refs], axis=0)
        values = jnp.concatenate([ref[:, v_at : v_at + HD] for ref in kv_refs], axis=0)
        for group in range(QH // KVH):
            head = kv_head * (QH // KVH) + group
            scores = lax.dot_general(
                query_ref[:, head * HD : (head + 1) * HD],
                keys,
                (((1,), (1,)), ((), ())),
                preferred_element_type=jnp.float32,
            ) * HD ** (-0.5)
            scores = jnp.where(visible, scores, -1e30)
            weights = jnp.exp(scores - jnp.max(scores, axis=1, keepdims=True))
            row_sum = jnp.sum(weights, axis=1, keepdims=True)
            mixed = jnp.dot(
                weights.astype(jnp.bfloat16), values, preferred_element_type=jnp.float32
            )
            core, at = places[head]
            slot = lax.rem(core + pos_ref[1], 2)
            out_ref[slot, :, at : at + HD] = (mixed / row_sum).astype(jnp.bfloat16)


def sent_kernel(kept_ref, given_ref, weight_hbm, keep_ref, give_ref, weight_ref, sems):
    pieces = sems.shape[0]
    deep = weight_ref.shape[0] // pieces
    copies = []
    for i in range(pieces):
        at = pl.ds(i * deep, deep)
        copies.append(
            pltpu.make_async_copy(weight_hbm.at[at], weight_ref.at[at], sems.at[i])
        )
        copies[-1].start()
    total = None
    for i in range(pieces):
        copies[i].wait()
        at = pl.ds(i * deep, deep)
        left = jnp.concatenate([kept_ref[:, at], given_ref[:, at]], axis=0)
        part = jnp.dot(left, weight_ref[at, :], preferred_element_type=jnp.float32)
        total = part if total is None else total + part
    rows = kept_ref.shape[0]
    keep_ref[...] = total[:rows]
    give_ref[...] = total[rows:].astype(jnp.bfloat16)


def norm_kernel(experts_all, pos_ref, hidden_ref, *refs):
    *projected_refs, gain_ref, ids_ref, gates_ref, residual_ref, tokens_ref = refs
    n_ctx = len(projected_refs)
    wide = D // n_ctx
    square_sum = None
    for back, ref in enumerate(projected_refs):
        at = pl.ds(pl.multiple_of(lax.rem(pos_ref[0] + back, n_ctx) * wide, wide), wide)
        part = hidden_ref[:, at].astype(jnp.float32) + ref[...].astype(jnp.float32)
        residual_ref[:, at] = part
        squares = jnp.sum(part * part, axis=1, keepdims=True)
        square_sum = squares if square_sum is None else square_sum + squares
    scale_inv = lax.rsqrt(square_sum * (1.0 / D) + 1e-06)
    normed = residual_ref[...] * scale_inv * gain_ref[...].astype(jnp.float32)
    tokens_ref[:, :D] = normed.astype(jnp.bfloat16)
    shape = (tokens_ref.shape[0], tokens_ref.shape[1] - D)
    column = lax.broadcasted_iota(jnp.int32, shape, 1)
    expert = lax.rem(column, experts_all)
    gates = jnp.zeros(shape, jnp.float32)
    for k in range(TOP):
        gates = gates + jnp.where(ids_ref[:, k : k + 1] == expert, gates_ref[:, k : k + 1], 0.0)
    terms = jnp.zeros(shape, jnp.float32)
    for term in range(TERMS):
        rounded = gates.astype(jnp.bfloat16).astype(jnp.float32)
        terms = jnp.where(column // experts_all == term, rounded, terms)
        gates = gates - rounded
    tokens_ref[:, D:] = terms.astype(jnp.bfloat16)


def final_kernel(residual_ref, own_ref, sibling_ref, *refs):
    *arrived_refs, out_ref = refs
    rows = arrived_refs[0].shape[0]
    for half in range(2):
        at = pl.ds(half * rows, rows)
        total = residual_ref[at, :]
        for ref in (own_ref.at[at], sibling_ref.at[at], *arrived_refs[2 * half : 2 * half + 2]):
            total = total + ref[...].astype(jnp.float32)
        out_ref[0, at, :] = total.astype(jnp.bfloat16)


def expert_kernel(experts_all, groups, parts, expert_ref, *refs):
    gate_ref, up_ref, down_ref, *refs = refs
    block_refs, out_refs = refs[: 2 * groups * parts], refs[2 * groups * parts :]
    blocks = jnp.concatenate([ref[...] for ref in block_refs], axis=0)
    terms = blocks[:, D:].astype(jnp.float32)
    column = lax.broadcasted_iota(jnp.int32, terms.shape, 1)
    mine = (lax.rem(column, experts_all) == expert_ref[0]) & (column < TERMS * experts_all)
    gates = jnp.sum(jnp.where(mine, terms, 0.0), axis=1, keepdims=True)
    tokens = blocks[:, :D]
    gate_pre = jnp.dot(tokens, gate_ref[...], preferred_element_type=jnp.float32)
    up_pre = jnp.dot(tokens, up_ref[...], preferred_element_type=jnp.float32)
    activated = (gate_pre / (1.0 + jnp.exp(-gate_pre)) * up_pre).astype(jnp.bfloat16)
    expert_out = jnp.dot(activated, down_ref[...], preferred_element_type=jnp.float32)
    weighted = jnp.where(gates > 0.0, expert_out * gates, 0.0).astype(jnp.bfloat16)
    rows = out_refs[0].shape[0]
    for i, ref in enumerate(out_refs):
        ref[...] = weighted[i * rows : (i + 1) * rows]


def vmem():
    return pl.BlockSpec(memory_space=pltpu.VMEM)


def smem():
    return pl.BlockSpec(memory_space=pltpu.SMEM)


def attend(position, core, queries, blocks, n_exp, proj_rows):
    rows = queries.shape[0]
    rings = core_rings(n_exp)
    places = {}
    for head in range(QH):
        device, inside = divmod(head * HD, proj_rows)
        places[head] = (device % 2, rings[device % 2].index(device) * proj_rows + inside)
    return pl.pallas_call(
        functools.partial(attention_kernel, places),
        out_shape=jax.ShapeDtypeStruct((2, rows, QH * HD // 2), jnp.bfloat16),
        in_specs=[smem()] + [vmem()] * (1 + len(blocks)),
        out_specs=vmem(),
        compiler_params=pltpu.CompilerParams(vmem_limit_bytes=16 * 1024 * 1024),
        name="attention",
    )(jnp.stack([position, core]), queries, *blocks)


def sent_products(kept, given, columns):
    shape = (kept.shape[0], columns.shape[1])
    return pl.pallas_call(
        sent_kernel,
        out_shape=(
            jax.ShapeDtypeStruct(shape, jnp.float32),
            jax.ShapeDtypeStruct(shape, jnp.bfloat16),
        ),
        in_specs=[vmem(), vmem(), pl.BlockSpec(memory_space=pl.ANY)],
        out_specs=(vmem(), vmem()),
        scratch_shapes=[
            pltpu.VMEM(columns.shape, columns.dtype),
            pltpu.SemaphoreType.DMA((4,)),
        ],
        compiler_params=pltpu.CompilerParams(vmem_limit_bytes=56 * 1024 * 1024),
        name="sent",
    )(kept, given, columns)


def run_expert(experts_all, expert, chips, weights):
    groups, parts = len(chips), len(chips[0][0])
    blocks = [block for own, other in chips for block in own + other]
    rows = sum(block.shape[0] for block in blocks) // (2 * groups)
    ef = weights[0].shape[1]
    results = pl.pallas_call(
        functools.partial(expert_kernel, experts_all, groups, parts),
        out_shape=[jax.ShapeDtypeStruct((rows, D), jnp.bfloat16)] * (2 * groups),
        in_specs=[smem()] + [vmem()] * (3 + len(blocks)),
        out_specs=[vmem()] * (2 * groups),
        compiler_params=pltpu.CompilerParams(vmem_limit_bytes=38 * 1024 * 1024),
        cost_estimate=pl.CostEstimate(
            flops=12 * groups * rows * D * ef,
            bytes_accessed=8 * groups * rows * D + 6 * D * ef,
            transcendentals=0,
        ),
        name="experts",
    )(expert.reshape(1), *weights, *blocks)
    return [(results[2 * g], results[2 * g + 1]) for g in range(groups)]


def body(
    hidden_in, query, keyval, out_proj, norm_gain, expert_ids, gate_weights, w_gate, w_up, w_down
):
    n_ctx = lax.axis_size("ctx")
    n_exp = lax.axis_size("exp")
    position = lax.axis_index("ctx")
    rows = hidden_in.shape[1]
    proj_rows = out_proj.shape[0]
    wide = D // n_ctx
    columns = lax.all_gather(
        lax.dynamic_slice_in_dim(out_proj, position * wide, wide, axis=1),
        "exp",
        axis=0,
        tiled=True,
        axis_index_groups=core_rings(n_exp),
    )

    def times_columns(block):
        return jnp.dot(block, columns, preferred_element_type=jnp.float32)

    core = lax.axis_index("exp") % 2
    blocks = [keyval[0]] + [rotate(keyval[0], "ctx", back) for back in range(1, n_ctx)]
    attended = attend(position, core, query[0], blocks, n_exp, proj_rows)
    own_heads, other_heads = attended[0], attended[1]
    sibling_heads = swap_cores(other_heads)
    projected = []
    for back in range(1, n_ctx):
        heads = [rotate(own_heads, "ctx", back), rotate(sibling_heads, "ctx", back)]
        keep, give = sent_products(heads[0], heads[1], columns)
        part = (keep + swap_cores(give).astype(jnp.float32)).astype(jnp.bfloat16)
        own_heads, sibling_heads, part = lax.optimization_barrier((own_heads, sibling_heads, part))
        projected.append(rotate(part, "ctx", -back))
    from_sibling = swap_cores(times_columns(sibling_heads).astype(jnp.bfloat16))
    projected = [times_columns(own_heads) + from_sibling.astype(jnp.float32)] + projected

    local_experts = w_gate.shape[0]
    experts_all = n_exp * local_experts
    extra = -(-TERMS * experts_all // LANES) * LANES
    residual, tokens = pl.pallas_call(
        functools.partial(norm_kernel, experts_all),
        out_shape=(
            jax.ShapeDtypeStruct((rows, D), jnp.float32),
            jax.ShapeDtypeStruct((rows, D + extra), jnp.bfloat16),
        ),
        in_specs=[smem()] + [vmem()] * (4 + n_ctx),
        out_specs=(vmem(), vmem()),
        compiler_params=pltpu.CompilerParams(vmem_limit_bytes=16 * 1024 * 1024),
        name="norm",
    )(
        position.reshape(1),
        hidden_in[0],
        *projected,
        norm_gain.reshape(1, D),
        expert_ids[0],
        gate_weights[0],
    )

    n_chip = n_exp // 2
    far = n_chip // 2
    half_rows = rows // 2
    sums = {}

    def experts_on(chips):
        offsets = [offset for offset, _, _ in chips]
        total = None
        for local in range(local_experts):
            expert = lax.axis_index("exp") * local_experts + local
            weights = (w_gate[local], w_up[local], w_down[local])
            pairs = run_expert(
                experts_all, expert, [(own, other) for _, own, other in chips], weights
            )
            total = pairs if total is None else jax.tree.map(jnp.add, total, pairs)
        return dict(zip(offsets, total))

    def swap_results(results):
        return {offset: [own, swap_cores(other)] for offset, (own, other) in results.items()}

    def send_on(forward, backward, step):
        if step < far:
            return round_ring(forward, 1), round_ring(backward, -1)
        return round_ring(forward[:half_rows], 1), round_ring(backward[half_rows:], -1)

    def total_of(terms, half):
        at = slice(half * half_rows, (half + 1) * half_rows)
        terms = [term if term.shape[0] == half_rows else term[at] for term in terms]
        return functools.reduce(jnp.add, [term.astype(jnp.float32) for term in terms])

    barrier = lax.optimization_barrier
    forward, backward = send_on(tokens, tokens, 1)
    results = experts_on([(0, [tokens], [swap_cores(tokens)])])
    forward, backward, results = barrier((forward, backward, results))
    for step in range(1, far):
        ours = forward, backward
        swapped = swap_cores(forward), swap_cores(backward)
        forward, backward = send_on(forward, backward, step + 1)
        if step + 1 < far:
            swapped, results = barrier((swapped, results))
        sums |= swap_results(results)
        results = experts_on(
            [(n_chip - step, [ours[0]], [swapped[0]]), (step, [ours[1]], [swapped[1]])]
        )
        forward, backward, results, sums = barrier((forward, backward, results, sums))
    swapped = [swap_cores(forward), swap_cores(backward)]
    swapped, results = barrier((swapped, results))
    sums |= swap_results(results)
    results = experts_on([(far, [forward, backward], swapped)])
    results, sums = barrier((results, sums))
    sums |= swap_results(results)

    def running_sum(direction, half, hops, parts):
        carried = []
        for hop in range(hops, 0, -1):
            offset = hop if direction > 0 else n_chip - hop
            total = total_of(parts[offset] + carried, half).astype(jnp.bfloat16)
            carried = [round_ring(total, direction)]
        return carried

    apart = barrier(sums)
    arrived = [
        running_sum(1, 0, far, sums) + running_sum(-1, 0, far - 1, apart),
        running_sum(1, 1, far - 1, apart) + running_sum(-1, 1, far, sums),
    ]
    return pl.pallas_call(
        final_kernel,
        out_shape=jax.ShapeDtypeStruct((1, rows, D), jnp.bfloat16),
        in_specs=[vmem()] * 7,
        out_specs=vmem(),
        compiler_params=pltpu.CompilerParams(vmem_limit_bytes=16 * 1024 * 1024),
        name="final",
    )(residual, *sums[0], *arrived[0], *arrived[1])


def solution(mesh):
    in_specs = (
        P("exp", "ctx", None),
        P("exp", "ctx", None),
        P("exp", "ctx", None),
        P("exp", None),
        P(),
        P("exp", "ctx", None),
        P("exp", "ctx", None),
        P("exp", None, None),
        P("exp", None, None),
        P("exp", None, None),
    )
    out_specs = P("exp", "ctx", None)
    return jax.shard_map(body, mesh=mesh, in_specs=in_specs, out_specs=out_specs, check_vma=False)
```
